32 devices in a mesh: dp: 16 (over z, y, x), rep: 2 (over core).
Axes of the slice: x: 2, y: 2, z: 4, core: 2. Of those that a mesh axis runs over, the one named last changes fastest.
Arguments:
- source: int32 [16384], P(('dp', 'rep')), may hold values from 0 to 8191
- target: int32 [16384], P(('dp', 'rep')), may hold values from 0 to 8191
- neighbours: int32 [16384, 2, 10], P(('dp', 'rep')), may hold values from 0 to 8191
- neighbour_ticks: int32 [16384, 2, 10], P(('dp', 'rep')), may hold values from 0 to 16383
- event_ticks: int32 [16384], P(('dp', 'rep')), may hold values from 0 to 16383, each once
- event_types: int32 [16384], P(('dp', 'rep')), may hold values 0 or 1
- labels: int32 [16384], P(('dp', 'rep')), may hold values 0 or 1
- edge_feats: bfloat16 [16384, 172], P(('dp', 'rep')), may hold values from -6 to 6
- weights: float32 [16384], P(('dp', 'rep')), may hold values from 0.25 to 10, as said below
- memory: float32 [8192, 172], replicated, may hold values from -6 to 6
- node_ticks: int32 [8192], replicated, may hold values from 0 to 16383
- gru_in: float32 [688, 516], replicated, may hold values from -0.21875 to 0.21875
- gru_hid: float32 [172, 516], replicated, may hold values from -0.4375 to 0.4375
- keys_values: float32 [344, 344], replicated, may hold values from -0.3125 to 0.3125
- tall_stack: float32 [3, 344, 172], replicated, may hold values from -0.3125 to 0.3125
- squares: float32 [2, 172, 172], replicated, may hold values from -0.625 to 0.625
- vectors: float32 [15, 172], replicated, may hold values from -2 to 2
- first_gru_in: float32 [688, 516], replicated, may hold values from -8.34465e-07 to 8.34465e-07
- first_gru_hid: float32 [172, 516], replicated, may hold values from -4.7683716e-07 to 4.7683716e-07
- first_keys_values: float32 [344, 344], replicated, may hold values from -3.8146973e-06 to 3.8146973e-06
- first_tall: float32 [3, 344, 172], replicated, may hold values from -3.8146973e-06 to 3.8146973e-06
- first_squares: float32 [2, 172, 172], replicated, may hold values from -3.8146973e-06 to 3.8146973e-06
- first_vectors: float32 [15, 172], replicated, may hold values from -1.9073486e-05 to 1.9073486e-05
- second_gru_in: float32 [688, 516], replicated, may hold values from 1.56491e-15 to 6.25964e-15
- second_gru_hid: float32 [172, 516], replicated, may hold values from 6.2596397e-16 to 2.5038559e-15
- second_keys_values: float32 [344, 344], replicated, may hold values from 3.12982e-14 to 1.251928e-13
- second_tall: float32 [3, 344, 172], replicated, may hold values from 3.12982e-14 to 1.251928e-13
- second_squares: float32 [2, 172, 172], replicated, may hold values from 3.12982e-14 to 1.251928e-13
- second_vectors: float32 [15, 172], replicated, may hold values from 7.82455e-13 to 3.12982e-12
Outputs:
- grad_norm: float32 [], replicated
- loss_sum: float32 [], replicated
- weight_sum: float32 [], replicated
- new_memory: float32 [8192, 172], replicated
- new_gru_in: float32 [688, 516], replicated
- new_gru_hid: float32 [172, 516], replicated
- new_keys_values: float32 [344, 344], replicated
- new_tall: float32 [3, 344, 172], replicated
- new_squares: float32 [2, 172, 172], replicated
- new_vectors: float32 [15, 172], replicated
- out_first_gru_in: float32 [688, 516], replicated
- out_first_gru_hid: float32 [172, 516], replicated
- out_first_keys_values: float32 [344, 344], replicated
- out_first_tall: float32 [3, 344, 172], replicated
- out_first_squares: float32 [2, 172, 172], replicated
- out_first_vectors: float32 [15, 172], replicated
- out_second_gru_in: float32 [688, 516], replicated
- out_second_gru_hid: float32 [172, 516], replicated
- out_second_keys_values: float32 [344, 344], replicated
- out_second_tall: float32 [3, 344, 172], replicated
- out_second_squares: float32 [2, 172, 172], replicated
- out_second_vectors: float32 [15, 172], replicated
The draws below stay inside these ranges and needn't reach their ends.
Inputs may be any that keep to these rules, and one draw needn't show every extreme that they name: `event_ticks`: each tick 0 to 16383 appears once. `weights`: positive.
All inputs are finite; a program needn't handle non-finite values. No bound on the sum of `event_types` or of `labels` on one device may be relied on, other than what follows from the above.
Results may differ from the reference program's by a relative error of at most 0.0048.
Values sent between devices are 32-bit elements; how exact they have to be, the bound alone decides.
No kernel may reach another device: no remote copies, remote signals or barrier semaphores. Data moves between devices by JAX's collectives and lax.ppermute only.
A program may use at most 192 MiB of HBM per device.

```python
import math
import jax
import jax.numpy as jnp
import numpy as np
from jax import lax

MEM = 172
HEADS = 2
NBR = 10
STEP = 10
NODES = 8192
EVENTS = 16384


def draw_weights(key, part):
    key = jax.random.fold_in(key, 11)
    place = jnp.arange(EVENTS, dtype=jnp.float32) / EVENTS
    base = jnp.exp(jax.random.uniform(key, (EVENTS,), jnp.float32, -0.7, 0.7))
    return base * (1.0 + 2.0 * place)


def with_ends(drawn, key, least, high):
    extent = drawn.shape
    spot = [jax.random.randint(jax.random.fold_in(key, axis), (), 0, extent[axis]) for axis in range(len(extent))]
    drawn = drawn.at[tuple(spot)].set(least)
    longest = extent.index(max(extent))
    spot[longest] = (spot[longest] + 1) % extent[longest]
    return drawn.at[tuple(spot)].set(high)


def levels(own_key, dims, shards, low, top_value):
    factor_of, own = 1.0, jax.random.fold_in(own_key, 6)
    for dim, parts in shards:
        heights = jnp.exp(jax.random.uniform(jax.random.fold_in(own, dim), (parts,), jnp.float32, low / len(shards), top_value / len(shards)))
        factor_of = factor_of * jnp.repeat(heights, dims[dim] // parts).reshape([-1 if axis == dim else 1 for axis in range(len(dims))])
    return factor_of


def cumulative_ranks(amount, slope):
    loads = [(1 << 20) // math.isqrt(grade ** slope) + 1 for grade in range(1, amount + 1)]
    scale = 1 + sum(loads) // (1 << 30)
    return np.cumsum(np.array([max(1, weight // scale) for weight in loads]))


def ranked_ids(own_key, extent, amount, skew):
    table = cumulative_ranks(amount, skew)
    ticket = jax.random.randint(jax.random.fold_in(own_key, 1), extent, 0, int(table[amount - 1]))
    grade = jnp.searchsorted(jnp.asarray(table, jnp.int32), ticket, side="right")
    return jax.random.permutation(jax.random.fold_in(own_key, 2), amount)[grade].astype(jnp.int32)


def scatter_about(own_key, shape, scale, bound, shards=(), kind=jnp.bfloat16):
    loudness = levels(own_key, shape, shards, -0.22, 0.18) if shards else 1.0
    values = jax.random.normal(own_key, shape, jnp.float32) * scale * loudness
    return jnp.minimum(jnp.maximum(values, -bound), bound).astype(kind)


def setup_inputs(seed: int = 0) -> dict:
    keys = jax.random.split(jax.random.key(seed), 30)
    source = with_ends(ranked_ids(keys[0], (EVENTS,), NODES, 2), jax.random.fold_in(keys[0], 3), 0, NODES - 1).astype(jnp.int32)
    target = with_ends(ranked_ids(keys[1], (EVENTS,), NODES, 1), jax.random.fold_in(keys[1], 3), 0, NODES - 1).astype(jnp.int32)
    neighbours = with_ends(ranked_ids(keys[2], (EVENTS, 2, NBR), NODES, 2), jax.random.fold_in(keys[2], 3), 0, NODES - 1).astype(jnp.int32)
    neighbour_ticks = with_ends(jax.random.randint(keys[3], (EVENTS, 2, NBR), 0, EVENTS), jax.random.fold_in(keys[3], 1), 0, EVENTS - 1).astype(jnp.int32)
    event_ticks = jax.random.permutation(keys[4], EVENTS).astype(jnp.int32)
    event_types = with_ends((jax.random.randint(keys[5], (EVENTS,), 0, 4) < 3).astype(jnp.int32), jax.random.fold_in(keys[5], 1), 0, 1)
    labels = with_ends((jax.random.randint(keys[6], (EVENTS,), 0, 2) < 1).astype(jnp.int32), jax.random.fold_in(keys[6], 1), 0, 1)
    edge_feats = scatter_about(keys[7], (EVENTS, MEM), 1.0, 6.0, ((0, 32),))
    weights = draw_weights(jax.random.fold_in(keys[29], 71), 0)
    memory = scatter_about(keys[9], (NODES, MEM), 1.0, 6.0, (), jnp.float32)
    node_ticks = with_ends(jax.random.randint(keys[10], (NODES,), 0, EVENTS), jax.random.fold_in(keys[10], 1), 0, EVENTS - 1).astype(jnp.int32)
    gru_in = scatter_about(keys[11], (4 * MEM, 3 * MEM), (4 * MEM) ** -0.5, 0.21875, (), jnp.float32)
    gru_hid = scatter_about(keys[12], (MEM, 3 * MEM), MEM ** -0.5, 0.4375, (), jnp.float32)
    keys_values = scatter_about(keys[13], (2 * MEM, 2 * MEM), (2 * MEM) ** -0.5, 0.3125, (), jnp.float32)
    tall_stack = scatter_about(keys[14], (3, 2 * MEM, MEM), (2 * MEM) ** -0.5, 0.3125, (), jnp.float32)
    squares = scatter_about(keys[15], (2, MEM, MEM), (MEM // 2) ** -0.5, 0.625, (), jnp.float32)
    vectors = scatter_about(keys[16], (15, MEM), 0.3, 2.0, (), jnp.float32)
    first_gru_in = scatter_about(keys[17], (4 * MEM, 3 * MEM), (1.2e-4 / (27 * MEM * MEM) ** 0.5), 8.344650268554688e-07, (), jnp.float32)
    first_gru_hid = scatter_about(keys[18], (MEM, 3 * MEM), (7.8e-5 / (27 * MEM * MEM) ** 0.5), 4.76837158203125e-07, (), jnp.float32)
    first_keys_values = scatter_about(keys[19], (2 * MEM, 2 * MEM), (5.5e-4 / (27 * MEM * MEM) ** 0.5), 3.814697265625e-06, (), jnp.float32)
    first_tall = scatter_about(keys[20], (3, 2 * MEM, MEM), (5.5e-4 / (27 * MEM * MEM) ** 0.5), 3.814697265625e-06, (), jnp.float32)
    first_squares = scatter_about(keys[21], (2, MEM, MEM), (5.5e-4 / (27 * MEM * MEM) ** 0.5), 3.814697265625e-06, (), jnp.float32)
    first_vectors = scatter_about(keys[22], (15, MEM), (2.75e-3 / (27 * MEM * MEM) ** 0.5), 1.9073486328125e-05, (), jnp.float32)
    second_gru_in = jnp.clip(jnp.exp(jax.random.uniform(keys[23], (4 * MEM, 3 * MEM), jnp.float32, math.log(1.5649099930739097e-15), math.log(6.259639972295639e-15))), 1.5649099930739097e-15, 6.259639972295639e-15)
    second_gru_hid = jnp.clip(jnp.exp(jax.random.uniform(keys[24], (MEM, 3 * MEM), jnp.float32, math.log(6.259639654658284e-16), math.log(2.5038558618633135e-15))), 6.259639654658284e-16, 2.5038558618633135e-15)
    second_keys_values = jnp.clip(jnp.exp(jax.random.uniform(keys[25], (2 * MEM, 2 * MEM), jnp.float32, math.log(3.129819943796172e-14), math.log(1.2519279775184688e-13))), 3.129819943796172e-14, 1.2519279775184688e-13)
    second_tall = jnp.clip(jnp.exp(jax.random.uniform(keys[26], (3, 2 * MEM, MEM), jnp.float32, math.log(3.129819943796172e-14), math.log(1.2519279775184688e-13))), 3.129819943796172e-14, 1.2519279775184688e-13)
    second_squares = jnp.clip(jnp.exp(jax.random.uniform(keys[27], (2, MEM, MEM), jnp.float32, math.log(3.129819943796172e-14), math.log(1.2519279775184688e-13))), 3.129819943796172e-14, 1.2519279775184688e-13)
    second_vectors = jnp.clip(jnp.exp(jax.random.uniform(keys[28], (15, MEM), jnp.float32, math.log(7.824549927253066e-13), math.log(3.1298199709012264e-12))), 7.824549927253066e-13, 3.1298199709012264e-12)
    return {"source": source, "target": target, "neighbours": neighbours, "neighbour_ticks": neighbour_ticks, "event_ticks": event_ticks, "event_types": event_types, "labels": labels, "edge_feats": edge_feats, "weights": weights, "memory": memory, "node_ticks": node_ticks, "gru_in": gru_in, "gru_hid": gru_hid, "keys_values": keys_values, "tall_stack": tall_stack, "squares": squares, "vectors": vectors, "first_gru_in": first_gru_in, "first_gru_hid": first_gru_hid, "first_keys_values": first_keys_values, "first_tall": first_tall, "first_squares": first_squares, "first_vectors": first_vectors, "second_gru_in": second_gru_in, "second_gru_hid": second_gru_hid, "second_keys_values": second_keys_values, "second_tall": second_tall, "second_squares": second_squares, "second_vectors": second_vectors}


@jax.custom_vjp
def low(v):
    return lax.optimization_barrier(v.astype(jnp.bfloat16)).astype(jnp.float32)

@jax.custom_vjp
def low_back(v):
    return v

def low_keep(v):
    return (low(v), None)

def low_pass(kept, grad):
    return (grad,)

def back_keep(v):
    return (v, None)

def back_low(kept, grad):
    return (low(grad),)
low.defvjp(low_keep, low_pass)
low_back.defvjp(back_keep, back_low)
HIGHEST = lax.Precision.HIGHEST
LEARN_RATE = 0.03
VECTOR_RATE = 0.3
BETA_ONE = 0.9
BETA_TWO = 0.999
ADAM_EPS = 1e-08
DECAY = 0.01
CLIP_AT = 0.005
TIME_RATE = 64.0
NORM_EPS = 1e-06

def product(left_op, right_op):
    return jnp.dot(left_op, right_op, precision=HIGHEST, preferred_element_type=jnp.float32)

def time_code(time_gap, frequency, phase_row):
    return jnp.cos(time_gap[..., None] * frequency + phase_row)

def softplus(logit_in):
    return jnp.maximum(logit_in, 0.0) + jnp.log1p(jnp.exp(-jnp.abs(logit_in)))

def gru_cell(gates_in, gates_hid, own_rows, vector_rows):
    feat_width = own_rows.shape[-1]
    total_in = gates_in + vector_rows[2:5].reshape(-1)
    total_hid = gates_hid + vector_rows[5:8].reshape(-1)
    update = jax.nn.sigmoid(total_in[:, :feat_width] + total_hid[:, :feat_width])
    reset_gate = jax.nn.sigmoid(total_in[:, feat_width:2 * feat_width] + total_hid[:, feat_width:2 * feat_width])
    candidate = jnp.tanh(total_in[:, 2 * feat_width:] + reset_gate * total_hid[:, 2 * feat_width:])
    return (1.0 - update) * candidate + update * own_rows

def attend(query_rows, key_rows, value_rows):
    row_count, near_count, feat_width = key_rows.shape
    head_size = feat_width // HEADS
    heads_q = query_rows.reshape(row_count, HEADS, head_size)
    heads_k = key_rows.reshape(row_count, near_count, HEADS, head_size)
    heads_v = value_rows.reshape(row_count, near_count, HEADS, head_size)
    scores = jnp.einsum('rhd,rjhd->rhj', heads_q, heads_k, precision=HIGHEST) * head_size ** (-0.5)
    scores = scores - lax.optimization_barrier(jnp.max(scores, axis=-1, keepdims=True))
    exponent = jnp.exp(scores)
    attn_weights = exponent / lax.optimization_barrier(jnp.sum(exponent, axis=-1, keepdims=True))
    attended = jnp.einsum('rhj,rjhd->rhd', attn_weights, heads_v, precision=HIGHEST)
    return attended.reshape(row_count, feat_width)

def head_terms(pre_rows, out_row, label_wide, weights):
    logit = lax.optimization_barrier(jnp.sum(jax.nn.gelu(pre_rows) * out_row, axis=-1))
    return weights * (softplus(logit) - label_wide * logit)

def adam_all(params, firsts, seconds, grads):
    squares_sum = jnp.zeros((), jnp.float32)
    for grad_item in grads:
        squares_sum = squares_sum + jnp.sum(grad_item * grad_item)
    grad_norm = jnp.sqrt(squares_sum)
    factor = jnp.minimum(1.0, CLIP_AT / (grad_norm + NORM_EPS))
    new_params, new_firsts, new_seconds = ([], [], [])
    for position in range(len(params)):
        clipped = grads[position] * factor
        moment_one = BETA_ONE * firsts[position] + (1.0 - BETA_ONE) * clipped
        moment_two = BETA_TWO * seconds[position] + (1.0 - BETA_TWO) * clipped * clipped
        step_dir = moment_one / (1.0 - BETA_ONE ** STEP) / (jnp.sqrt(moment_two / (1.0 - BETA_TWO ** STEP)) + ADAM_EPS)
        decay_rate = DECAY if position < len(params) - 1 else 0.0
        step_rate = LEARN_RATE if position < len(params) - 1 else VECTOR_RATE
        new_params.append(params[position] - step_rate * (step_dir + decay_rate * params[position]))
        new_firsts.append(moment_one)
        new_seconds.append(moment_two)
    return (grad_norm, new_params, new_firsts, new_seconds)

def forward_block(params, memory_low, node_ticks, event_block):
    gru_in, gru_hid, keys_values, tall_stack, squares, vectors = params
    source, target, neighbours, neighbour_ticks, event_ticks, event_types, labels, edge_feats, weights = event_block
    events_here = event_ticks.shape[0]
    feat_width = memory_low.shape[1]
    time_scale = TIME_RATE / EVENTS
    end_nodes = jnp.concatenate([source, target])
    own_rows = memory_low[end_nodes]
    partner = jnp.concatenate([own_rows[events_here:], own_rows[:events_here]])
    near_rows = memory_low[jnp.transpose(neighbours, (1, 0, 2)).reshape(-1)]
    both_ticks = jnp.concatenate([event_ticks, event_ticks])
    gap_own = (both_ticks - node_ticks[end_nodes]).astype(jnp.float32) * time_scale
    gap_near = (both_ticks[:, None] - jnp.transpose(neighbour_ticks, (1, 0, 2)).reshape(2 * events_here, -1)).astype(jnp.float32) * time_scale
    edge_rows = edge_feats.astype(jnp.float32) * event_types.astype(jnp.float32)[:, None]
    edge_rows = jnp.concatenate([edge_rows, edge_rows])
    message = jnp.concatenate([own_rows, partner, low(time_code(gap_own, vectors[0], vectors[1])), edge_rows], axis=1)
    gates_in = low_back(product(message, low(gru_in)))
    gates_hid = low_back(product(own_rows, low(gru_hid)))
    renewed = gru_cell(gates_in, gates_hid, own_rows, vectors)
    renewed_low = low(renewed)
    phase_low = jnp.broadcast_to(low(jnp.cos(vectors[1])), renewed.shape)
    query_in = jnp.concatenate([renewed_low, phase_low], axis=1)
    queries = low_back(product(query_in, low(tall_stack[0]))) + vectors[8]
    code_near = low(time_code(gap_near, vectors[0], vectors[1]))
    near_in = jnp.concatenate([near_rows, code_near.reshape(near_rows.shape)], axis=1)
    pair_rows = low_back(product(near_in, low(keys_values))).reshape(2 * events_here, -1, 2 * feat_width)
    attended = attend(queries, pair_rows[..., :feat_width], pair_rows[..., feat_width:] + vectors[9])
    projected = low_back(product(low(attended), low(squares[0]))) + vectors[10]
    mlp_in = jnp.concatenate([low(projected), renewed_low], axis=1)
    inner_pre = low_back(product(mlp_in, low(tall_stack[1]))) + vectors[11]
    embedding = low_back(product(low(jax.nn.gelu(inner_pre)), low(squares[1]))) + vectors[12]
    embedding_low = low(embedding)
    dec_in = jnp.concatenate([embedding_low[:events_here], embedding_low[events_here:]], axis=1)
    dec_pre = low_back(product(dec_in, low(tall_stack[2]))) + vectors[13]
    loss_terms = head_terms(dec_pre, vectors[14], labels.astype(jnp.float32), weights)
    return (jnp.sum(loss_terms), renewed)

def reference(source, target, neighbours, neighbour_ticks, event_ticks, event_types, labels, edge_feats, weights, memory, node_ticks, gru_in, gru_hid, keys_values, tall_stack, squares, vectors, first_gru_in, first_gru_hid, first_keys_values, first_tall, first_squares, first_vectors, second_gru_in, second_gru_hid, second_keys_values, second_tall, second_squares, second_vectors):
    params = (gru_in, gru_hid, keys_values, tall_stack, squares, vectors)
    firsts = (first_gru_in, first_gru_hid, first_keys_values, first_tall, first_squares, first_vectors)
    seconds = (second_gru_in, second_gru_hid, second_keys_values, second_tall, second_squares, second_vectors)
    memory_low = memory.astype(jnp.bfloat16).astype(jnp.float32)
    block_rows = min(4096, EVENTS)

    def split(whole):
        return whole.reshape((EVENTS // block_rows, block_rows) + whole.shape[1:])
    blocks = tuple((split(item) for item in (source, target, neighbours, neighbour_ticks, event_ticks, event_types, labels, edge_feats, weights)))
    weight_sum = jnp.sum(weights)
    checked = jax.checkpoint(forward_block)

    def total_loss(param_set):

        def scan_step(carry, event_block):
            block_loss, renewed = checked(param_set, memory_low, node_ticks, event_block)
            return (carry + block_loss, renewed)
        loss_sum, renewed = lax.scan(scan_step, jnp.zeros((), jnp.float32), blocks)
        return (loss_sum / weight_sum, (loss_sum, renewed))
    loss_mean, back_fn, (loss_sum, renewed) = jax.vjp(total_loss, params, has_aux=True)
    grads = back_fn(jnp.ones((), jnp.float32))[0]
    grad_norm, new_params, new_firsts, new_seconds = adam_all(params, firsts, seconds, grads)
    end_nodes = jnp.concatenate([blocks[0], blocks[1]], axis=1).reshape(-1)
    update_order = jnp.concatenate([2 * blocks[4], 2 * blocks[4] + 1], axis=1).reshape(-1).astype(jnp.int32)
    fresh_rows = renewed.reshape(-1, memory.shape[1])
    latest_order = jnp.full((NODES,), -1, jnp.int32).at[end_nodes].max(update_order)
    winner = update_order == latest_order[end_nodes]
    merged = jnp.zeros_like(memory).at[end_nodes].add(jnp.where(winner[:, None], fresh_rows, 0.0))
    new_memory = jnp.where(latest_order[:, None] >= 0, merged, memory)
    return (grad_norm, loss_sum, weight_sum, new_memory, new_params[0], new_params[1], new_params[2], new_params[3], new_params[4], new_params[5], new_firsts[0], new_firsts[1], new_firsts[2], new_firsts[3], new_firsts[4], new_firsts[5], new_seconds[0], new_seconds[1], new_seconds[2], new_seconds[3], new_seconds[4], new_seconds[5])
```

```python
import math

import jax
import jax.numpy as jnp
from jax import lax
from jax.experimental import pallas as pl
from jax.experimental.pallas import tpu as pltpu
from jax.sharding import PartitionSpec as P

F32 = jnp.float32
BF = jnp.bfloat16
I32 = jnp.int32
NBR = 10
MEM = 172
PAD = 176
HALF = 86
HPAD = 88
STEP = 10
LEARN_RATE = 0.03
VECTOR_RATE = 0.3
BETA_ONE = 0.9
BETA_TWO = 0.999
ADAM_EPS = 1e-08
DECAY = 0.01
CLIP_AT = 0.005
TIME_RATE = 64.0
NORM_EPS = 1e-06
VMEM_CAP = 58 * 2**20


def params(limit=VMEM_CAP):
    return pltpu.CompilerParams(vmem_limit_bytes=limit)


def nn(a, b):
    return lax.dot_general(a, b, (((1,), (0,)), ((), ())), preferred_element_type=F32)


def nt(a, b):
    return lax.dot_general(a, b, (((1,), (1,)), ((), ())), preferred_element_type=F32)


def zeros(rows, cols):
    return jnp.zeros((rows, cols), F32)


def rows_to(x, total):
    return jnp.concatenate([x, zeros(total - x.shape[0], x.shape[1])], axis=0)


def cols_to(x, total):
    return jnp.concatenate([x, zeros(x.shape[0], total - x.shape[1])], axis=1)


def split_rows(x):
    gap = zeros(HPAD - HALF, x.shape[1])
    return jnp.concatenate([x[:HALF], gap, x[HALF:], gap], axis=0)


def prep_kernel(gin, ghid, kv, tall, sq, vec,
                wg, wgc, wh, kvm, kvct, kvc, t0t, t0, t1t, t1, t2t, t2, s0t, s0, s1t, s1, vb):
    full = gin[...]
    for gate in range(3):
        rows = full[gate * MEM : (gate + 1) * MEM]
        parts = [cols_to(rows[:, q * MEM : (q + 1) * MEM], PAD) for q in range(4)]
        wide = rows_to(jnp.concatenate(parts, axis=1), PAD)
        wg[pl.ds(gate * PAD, PAD), :] = wide.astype(BF)
        code = cols_to(rows_to(rows[:, 2 * MEM : 3 * MEM], PAD), 256)
        wgc[:, gate * PAD : (gate + 1) * PAD] = jnp.transpose(code)[:PAD].astype(BF)
    hid = ghid[...]
    for gate in range(3):
        part = cols_to(rows_to(hid[:, gate * MEM : (gate + 1) * MEM], PAD), 256)
        wh[pl.ds(gate * PAD, PAD), :] = jnp.transpose(part)[:PAD].astype(BF)
    pairs = kv[...]
    mem_t = jnp.transpose(cols_to(rows_to(pairs[:MEM], 256), 384))
    code_t = jnp.transpose(cols_to(rows_to(pairs[MEM:], 256), 384))
    kvm[...] = jnp.concatenate([split_rows(mem_t[:MEM]), split_rows(mem_t[MEM : 2 * MEM])], axis=0).astype(BF)
    code_rows = jnp.concatenate([split_rows(code_t[:MEM]), split_rows(code_t[MEM : 2 * MEM])], axis=0)
    kvct[...] = code_rows[:, :PAD].astype(BF)
    kvc[...] = jnp.transpose(rows_to(code_rows, 384))[:PAD, : 2 * PAD].astype(BF)
    query = tall[0]
    query_t = split_rows(query[:, :MEM])
    t0t[...] = cols_to(query_t, PAD).astype(BF)
    t0[...] = jnp.transpose(rows_to(cols_to(query_t, 256), 256))[:PAD, :PAD].astype(BF)
    for src, fwd, back in ((tall[1], t1t, t1), (tall[2], t2t, t2)):
        wide = jnp.concatenate([cols_to(src[:, :MEM], PAD), cols_to(src[:, MEM:], PAD)], axis=1)
        fwd[...] = rows_to(wide, PAD).astype(BF)
        back[...] = jnp.transpose(rows_to(cols_to(wide, 384), 256))[: 2 * PAD, :PAD].astype(BF)
    first = cols_to(split_rows(sq[0]), PAD)
    s0[...] = first.astype(BF)
    s0t[...] = jnp.transpose(rows_to(cols_to(first, 256), 256))[:PAD, :PAD].astype(BF)
    second = rows_to(cols_to(sq[1], PAD), PAD)
    s1[...] = second.astype(BF)
    s1t[...] = jnp.transpose(rows_to(cols_to(second, 256), 256))[:PAD, :PAD].astype(BF)
    cols = jnp.transpose(cols_to(rows_to(vec[...], 128), 256))
    phase_low = jnp.cos(cols[:PAD, 1:2]).astype(BF)
    wide_phase = jnp.broadcast_to(phase_low.astype(F32), (PAD, 128)).astype(BF)
    row_id = lax.broadcasted_iota(I32, (PAD, 128), 0)
    wide_phase = jnp.where(row_id < MEM, wide_phase.astype(F32), 0.0).astype(BF)
    steady = nn(cols_to(split_rows(query[:, MEM:]), PAD).astype(BF), wide_phase)
    for i in range(15):
        column = cols[:, i : i + 1]
        if i in (8, 9):
            column = split_rows(column[:MEM])
        wide = jnp.broadcast_to(column[:PAD], (PAD, 128))
        vb[i] = wide + steady if i == 8 else wide


def prep(gin, ghid, kv, tall, sq, vec):
    bf = lambda *s: jax.ShapeDtypeStruct(s, BF)
    outs = [bf(528, 704), bf(176, 528), bf(528, 176), bf(352, 256), bf(352, 176), bf(176, 352),
            bf(176, 176), bf(176, 176), bf(176, 352), bf(352, 176), bf(176, 352), bf(352, 176),
            bf(176, 176), bf(176, 176), bf(176, 176), bf(176, 176), jax.ShapeDtypeStruct((15, PAD, 128), F32)]
    return pl.pallas_call(
        prep_kernel, out_shape=outs, compiler_params=params(), name="prep",
    )(gin.T, ghid, kv, jnp.transpose(tall, (0, 2, 1)), sq, vec)


def table_kernel(steps, ids, mem, ticks, table, own, wide):
    step = pl.program_id(0)
    cols = mem.shape[1]

    @pl.when(step == 0)
    def _():
        wide[...] = jnp.zeros_like(wide)

    @pl.when(step < steps)
    def _():
        wide[0:MEM, :] = mem[...].astype(BF).astype(F32)
        wide[PAD : PAD + 1, :] = ticks[...].astype(F32)
        base = pl.multiple_of(step * cols, cols)
        for c in range(cols // 128):
            for h in range(2):
                table[pl.ds(base + 128 * c, 128), 128 * h : 128 * h + 128] = jnp.transpose(
                    wide[128 * h : 128 * h + 128, 128 * c : 128 * c + 128])

    @pl.when(step == steps)
    def _():
        def group(g, carry):
            for v in range(4):
                at = pl.multiple_of(g * 32 + v * 8, 8)
                rows = [table[pl.ds(ids[at + u], 1), :] for u in range(8)]
                own[pl.ds(at, 8), :] = jnp.concatenate(rows, axis=0)
            return carry

        lax.fori_loop(0, own.shape[0] // 32, group, 0)


def build_table(ids, mem_t, ticks):
    nodes = mem_t.shape[1]
    ends = ids.shape[0]
    cols = 1024
    steps = nodes // cols
    return pl.pallas_call(
        lambda *r: table_kernel(steps, *r),
        out_shape=[jax.ShapeDtypeStruct((nodes, 256), F32), jax.ShapeDtypeStruct((ends, 256), F32)],
        grid=(steps + 1,),
        in_specs=[pl.BlockSpec(memory_space=pltpu.SMEM),
                  pl.BlockSpec((MEM, cols), lambda i: (0, jnp.minimum(i, steps - 1))),
                  pl.BlockSpec((1, cols), lambda i: (0, jnp.minimum(i, steps - 1)))],
        out_specs=[pl.BlockSpec((nodes, 256), lambda i: (0, 0)), pl.BlockSpec((ends, 256), lambda i: (0, 0))],
        scratch_shapes=[pltpu.VMEM((256, cols), F32)],
        compiler_params=params(), name="table",
    )(ids, mem_t, ticks.reshape(1, nodes))


def near_kernel(chunk, ids, table, near):
    step = pl.program_id(0)
    base = step * chunk

    def group(g, carry):
        for v in range(2):
            at = pl.multiple_of(g * 32 + v * 16, 16)
            rows = [table[pl.ds(ids[base + at + u], 1), :] for u in range(16)]
            near[pl.ds(at, 16), :] = jnp.concatenate(rows, axis=0).astype(BF)
        return carry

    lax.fori_loop(0, chunk // 32, group, 0)


def gather_near(ids, table):
    chunk = 1024
    total = ids.shape[0]
    return pl.pallas_call(
        lambda *r: near_kernel(chunk, *r),
        out_shape=jax.ShapeDtypeStruct((total, 256), BF),
        grid=(total // chunk,),
        in_specs=[pl.BlockSpec(memory_space=pltpu.SMEM), pl.BlockSpec(table.shape, lambda i: (0, 0))],
        out_specs=pl.BlockSpec((chunk, 256), lambda i: (i, 0)),
        compiler_params=params(), name="near",
    )(ids, table)


PI_HI = 1.5703125
PI_MID = 4.8351287841796875e-04
PI_LO = 3.1385571319e-07
TURN = 12582912.0


def cos_sin(x):
    shifted = x * (2.0 / math.pi) + TURN
    n = shifted - TURN
    r = ((x - n * PI_HI) - n * PI_MID) - n * PI_LO
    z = r * r
    sin_r = r + r * (z * (-1.6666654611e-01 + z * (8.3321608736e-03 + z * -1.9515295891e-04)))
    cos_r = (1.0 - 0.5 * z) + (z * z) * (4.166664568298827e-02 + z * (-1.388731625493765e-03 + z * 2.443315711809948e-05))
    q = n.astype(I32)
    odd = (q & 1) == 1
    c = jnp.where(odd, sin_r, cos_r)
    s = jnp.where(odd, cos_r, sin_r)
    c = jnp.where(((q + 1) & 2) == 2, -c, c)
    s = jnp.where((q & 2) == 2, -s, s)
    return c, s


def sigmoid(x):
    return 0.5 * jnp.tanh(0.5 * x) + 0.5


def twice(x):
    return jnp.concatenate([x, x], axis=1)


def wide_rows(x, rows):
    return jnp.broadcast_to(x, (rows, x.shape[1]))


def gru_kernel(scale, own, ticks, edge, types, wg, wh, vb, msg, keep, ren, rows, gap_out):
    own_t = jnp.concatenate(
        [jnp.transpose(own[0:128, :]), jnp.transpose(own[128:256, :])], axis=1)
    gap = (twice(ticks[...].astype(F32)) - own_t[PAD : PAD + 1]) * scale
    row_id = lax.broadcasted_iota(I32, (PAD, 256), 0)
    own_x = jnp.where(row_id < MEM, own_t[:PAD], 0.0)
    msg[0:PAD, :] = own_x.astype(BF)
    msg[PAD : 2 * PAD, :] = jnp.concatenate([own_x[:, 128:], own_x[:, :128]], axis=1).astype(BF)
    edges = rows_to(edge[...].astype(F32) * types[...].astype(F32), PAD)
    msg[3 * PAD : 4 * PAD, :] = twice(edges).astype(BF)
    gap_out[...] = wide_rows(gap, 8)
    gap16 = wide_rows(gap, 16)
    for st in range(PAD // 16):
        at = 16 * st
        x = twice(vb[0, at : at + 16, :]) * gap16 + twice(vb[1, at : at + 16, :])
        c, s = cos_sin(x)
        msg[2 * PAD + at : 2 * PAD + at + 16, :] = c.astype(BF)
        keep[4, at : at + 16, :] = -s
    gates = nn(wg[...], msg[...])
    hidden = nn(wh[...], msg[0:PAD, :])
    for st in range(PAD // 8):
        at = 8 * st
        o = own_x[at : at + 8]
        pre = [gates[g * PAD + at : g * PAD + at + 8] + twice(vb[2 + g, at : at + 8, :]) for g in range(3)]
        hid = [hidden[g * PAD + at : g * PAD + at + 8] + twice(vb[5 + g, at : at + 8, :]) for g in range(3)]
        u = sigmoid(pre[0] + hid[0])
        r = sigmoid(pre[1] + hid[1])
        n = jnp.tanh(pre[2] + r * hid[2])
        keep[0, at : at + 8, :] = u
        keep[1, at : at + 8, :] = r
        keep[2, at : at + 8, :] = n
        keep[3, at : at + 8, :] = hid[2]
        ren[at : at + 8, :] = (1.0 - u) * n + u * o
    full = jnp.concatenate([ren[...], zeros(256 - PAD, 256)], axis=0)
    rows[0:128, :] = jnp.transpose(full[:, :128])
    rows[128:256, :] = jnp.transpose(full[:, 128:])


def gru(scale, own, ticks, edge_t, types, wg, wh, vb):
    ends = own.shape[0]
    blocks = ends // 256
    whole = lambda a: pl.BlockSpec(a.shape, lambda i: (0,) * len(a.shape))
    return pl.pallas_call(
        lambda *r: gru_kernel(scale, *r),
        out_shape=[jax.ShapeDtypeStruct((4 * PAD, ends), BF), jax.ShapeDtypeStruct((5, PAD, ends), F32),
                   jax.ShapeDtypeStruct((PAD, ends), F32), jax.ShapeDtypeStruct((ends, 256), F32),
                   jax.ShapeDtypeStruct((8, ends), F32)],
        grid=(blocks,),
        in_specs=[pl.BlockSpec((256, 256), lambda i: (i, 0)), pl.BlockSpec((1, 128), lambda i: (0, i)),
                  pl.BlockSpec((MEM, 128), lambda i: (0, i)), pl.BlockSpec((1, 128), lambda i: (0, i)),
                  whole(wg), whole(wh), whole(vb)],
        out_specs=[pl.BlockSpec((4 * PAD, 256), lambda i: (0, i)), pl.BlockSpec((5, PAD, 256), lambda i: (0, 0, i)),
                   pl.BlockSpec((PAD, 256), lambda i: (0, i)), pl.BlockSpec((256, 256), lambda i: (i, 0)),
                   pl.BlockSpec((8, 256), lambda i: (0, i))],
        compiler_params=params(), name="gru",
    )(own, ticks, edge_t, types, wg, wh, vb)


GELU_C = math.sqrt(2.0 / math.pi)


def gelu_parts(x):
    sq = x * x
    t = jnp.tanh(GELU_C * (x + 0.044715 * (sq * x)))
    half = 0.5 * (1.0 + t)
    slope = half + (0.5 * x) * (1.0 - t * t) * (GELU_C + (GELU_C * 3.0 * 0.044715) * sq)
    return x * half, slope


def fold(x):
    return x[:, :128] + x[:, 128:]


def main_kernel(scale, near, gaps_t, ticks, msg, keep, ren, gap_own, labels, weights, total,
                wgc, kvm, kvct, kvc, t0t, t0, t1t, t1, t2t, t2, s0t, s0, s1t, s1, vb,
                ga, gb, loss,
                pair, code, dcode, soft, back, grads, g_in, g_kv, g_one, g_dec, g_qo, g_th, vacc):
    step = pl.program_id(0)
    inv_size = HALF ** -0.5

    @pl.when(step == 0)
    def _():
        for ref in (g_in, g_kv, g_one, g_dec, g_qo, g_th, vacc, loss):
            ref[...] = jnp.zeros_like(ref)

    tick2 = twice(ticks[...].astype(F32))
    renewed = ren[...]
    ren_low = renewed.astype(BF)
    queries = nn(t0t[...], ren_low) + twice(vb[8])
    for j in range(NBR):
        gap16 = wide_rows((tick2 - gaps_t[j : j + 1, :].astype(F32)) * scale, 16)
        for st in range(PAD // 16):
            at = 16 * st
            x = twice(vb[0, at : at + 16, :]) * gap16 + twice(vb[1, at : at + 16, :])
            c, s = cos_sin(x)
            code[j, at : at + 16, :] = c.astype(BF)
            dcode[j, at : at + 16, :] = -s
        pair[j] = nt(kvm[...], near[j]) + nn(kvct[...], code[j])
        for h in range(2):
            acc = zeros(8, 256)
            for st in range(HPAD // 8):
                at = HPAD * h + 8 * st
                acc = acc + pair[j, at : at + 8, :] * queries[at : at + 8]
            soft[2 * j + h] = wide_rows(jnp.sum(acc, axis=0, keepdims=True) * inv_size, 8)
    for h in range(2):
        top = soft[h]
        for j in range(1, NBR):
            top = jnp.maximum(top, soft[2 * j + h])
        norm = zeros(8, 256)
        for j in range(NBR):
            e = jnp.exp(soft[2 * j + h] - top)
            soft[2 * j + h] = e
            norm = norm + e
        inv = 1.0 / norm
        for j in range(NBR):
            soft[2 * j + h] = soft[2 * j + h] * inv
    att = []
    for st in range(PAD // 8):
        at = 8 * st
        h = 0 if at < HPAD else 1
        acc = twice(vb[9, at : at + 8, :])
        for j in range(NBR):
            acc = acc + soft[2 * j + h] * pair[j, PAD + at : PAD + at + 8, :]
        att.append(acc)
    att_low = jnp.concatenate(att, axis=0).astype(BF)
    projected = nn(s0t[...], att_low) + twice(vb[10])
    mlp_in = jnp.concatenate([projected.astype(BF), ren_low], axis=0)
    inner = nn(t1t[...], mlp_in) + twice(vb[11])
    act, act_slope = gelu_parts(inner)
    act_low = act.astype(BF)
    emb_low = (nn(s1t[...], act_low) + twice(vb[12])).astype(BF)
    dec_in = jnp.concatenate([emb_low[:, :128], emb_low[:, 128:]], axis=0)
    dec_pre = nn(t2t[...], dec_in) + vb[13]
    dec_act, dec_slope = gelu_parts(dec_pre)
    logit = jnp.sum(dec_act * vb[14], axis=0, keepdims=True)
    label = labels[...].astype(F32)
    tail = jnp.exp(-jnp.abs(logit))
    plus = jnp.maximum(logit, 0.0) + jnp.log1p(tail)
    loss[...] += weights[...] * (plus - label * logit)
    d_logit = weights[...] / total[...] * (sigmoid(logit) - label)
    d_out = d_logit * dec_act
    d_dec = (d_logit * vb[14]) * dec_slope
    d_dec_low = d_dec.astype(BF)
    g_dec[...] += nt(d_dec_low, dec_in)
    d_dec_in = nn(t2[...], d_dec_low)
    d_emb = jnp.concatenate([d_dec_in[:PAD], d_dec_in[PAD:]], axis=1)
    d_emb_low = d_emb.astype(BF)
    g_th[:, 0:256] += jnp.concatenate([nt(act_low, d_emb_low), zeros(PAD, 256 - PAD)], axis=1)
    d_inner = nn(s1[...], d_emb_low) * act_slope
    d_inner_low = d_inner.astype(BF)
    g_one[...] += nt(d_inner_low, mlp_in)
    d_mlp = nn(t1[...], d_inner_low)
    d_proj = d_mlp[:PAD]
    d_proj_low = d_proj.astype(BF)
    g_qo[:, 256:512] += jnp.concatenate([nt(att_low, d_proj_low), zeros(PAD, 256 - PAD)], axis=1)
    d_att = nn(s0[...], d_proj_low)
    for h in range(2):
        mean = zeros(8, 256)
        for j in range(NBR):
            acc = zeros(8, 256)
            for st in range(HPAD // 8):
                at = HPAD * h + 8 * st
                acc = acc + pair[j, PAD + at : PAD + at + 8, :] * d_att[at : at + 8]
            wide = wide_rows(jnp.sum(acc, axis=0, keepdims=True), 8)
            back[2 * j + h] = wide
            mean = mean + wide * soft[2 * j + h]
        for j in range(NBR):
            back[2 * j + h] = (soft[2 * j + h] * inv_size) * (back[2 * j + h] - mean)
    d_q = []
    for st in range(PAD // 8):
        at = 8 * st
        h = 0 if at < HPAD else 1
        acc = zeros(8, 256)
        for j in range(NBR):
            acc = acc + back[2 * j + h] * pair[j, at : at + 8, :]
        d_q.append(acc)
    d_query = jnp.concatenate(d_q, axis=0)
    for j in range(NBR):
        for st in range(2 * PAD // 16):
            parts = []
            for half in range(2):
                at = 16 * st + 8 * half
                if at < PAD:
                    parts.append(back[2 * j + (at >= HPAD)] * queries[at : at + 8])
                else:
                    parts.append(soft[2 * j + (at - PAD >= HPAD)] * d_att[at - PAD : at - PAD + 8])
            grads[16 * st : 16 * st + 16, 256 * j : 256 * j + 256] = jnp.concatenate(parts, axis=0).astype(BF)
    d_codes = nn(kvc[...], grads[...])
    for st in range(PAD // 8):
        at = 8 * st
        f_acc = zeros(8, 256)
        p_acc = zeros(8, 256)
        for j in range(NBR):
            gap8 = wide_rows((tick2 - gaps_t[j : j + 1, :].astype(F32)) * scale, 8)
            d_arg = d_codes[at : at + 8, 256 * j : 256 * j + 256] * dcode[j, at : at + 8, :]
            f_acc = f_acc + d_arg * gap8
            p_acc = p_acc + d_arg
        vacc[0, at : at + 8, :] += fold(f_acc)
        vacc[1, at : at + 8, :] += fold(p_acc)
    mem_part = nn(grads[:, 0:256], near[0])
    code_part = nt(grads[:, 0:256], code[0])
    for j in range(1, NBR):
        mem_part = mem_part + nn(grads[:, 256 * j : 256 * j + 256], near[j])
        code_part = code_part + nt(grads[:, 256 * j : 256 * j + 256], code[j])
    g_kv[:, 0:256] += mem_part
    g_kv[:, 256:512] += jnp.concatenate([code_part, zeros(2 * PAD, 256 - PAD)], axis=1)
    d_q_low = d_query.astype(BF)
    g_qo[:, 0:256] += jnp.concatenate([nt(d_q_low, ren_low), zeros(PAD, 256 - PAD)], axis=1)
    d_ren = d_mlp[PAD:] + nn(t0[...], d_q_low)
    own_x = msg[0:PAD, :].astype(F32)
    u, r, n, hn = keep[0], keep[1], keep[2], keep[3]
    d_u = d_ren * (own_x - n) * (u * (1.0 - u))
    d_n = d_ren * (1.0 - u) * (1.0 - n * n)
    d_r = d_n * hn * (r * (1.0 - r))
    d_h = d_n * r
    gates = jnp.concatenate([d_u, d_r, d_n], axis=0).astype(BF)
    g_in[...] += nt(gates, msg[...])
    g_th[:, 256:512] += jnp.concatenate([nt(msg[0:PAD, :], d_h.astype(BF)), zeros(PAD, 256 - PAD)], axis=1)
    d_arg = nn(wgc[...], gates) * keep[4]
    vacc[0] += fold(d_arg * gap_own[0:1, :])
    vacc[1] += fold(d_arg)
    for i, item in ((2, d_u), (3, d_r), (4, d_n), (7, d_h), (8, d_query), (9, d_att), (10, d_proj), (11, d_inner),
                    (12, d_emb), (15, d_q_low.astype(F32))):
        vacc[i] += fold(item)
    vacc[13] += d_dec
    vacc[14] += d_out

    @pl.when(step == pl.num_programs(0) - 1)
    def _():
        wide = cols_to(g_in[...], 768)
        for c in range(6):
            gb[528 * c : 528 * c + 528, :] = wide[:, 128 * c : 128 * c + 128]
        lane = lax.broadcasted_iota(I32, (PAD, 128), 1)
        vecs = zeros(PAD, 128)
        for i in range(16):
            column = jnp.sum(vacc[i], axis=1, keepdims=True)
            vecs = jnp.where(lane == i, column, vecs)
        flat = jnp.transpose(jnp.concatenate([vecs, zeros(256 - PAD, 128)], axis=0))
        gb[3168:3184, :] = flat[0:16, 0:128]
        gb[3184:3200, :] = flat[0:16, 128:256]
        at = 0
        for left, right, rows in ((g_kv[:, 0:PAD], g_kv[:, 256 : 256 + PAD], 352),
                                  (g_one[:, 0:PAD], g_one[:, PAD : 2 * PAD], 176),
                                  (g_dec[:, 0:PAD], g_dec[:, PAD : 2 * PAD], 176),
                                  (g_qo[:, 0:PAD], g_qo[:, 256 : 256 + PAD], 176),
                                  (g_th[:, 0:PAD], g_th[:, 256 : 256 + PAD], 176)):
            wide = jnp.concatenate([left, right, zeros(rows, 32)], axis=1)
            for c in range(3):
                ga[at : at + rows, :] = wide[:, 128 * c : 128 * c + 128]
                at += rows
        ga[3168:3200, :] = zeros(32, 128)


def main(scale, near, near_ticks, ticks, msg, keep, ren, gap_own, labels, weights, total, w):
    ends = ren.shape[1]
    blocks = ends // 256
    whole = lambda a: pl.BlockSpec(a.shape, lambda i: (0,) * len(a.shape))
    lanes = lambda: pl.BlockSpec((1, 128), lambda i: (0, i))
    return pl.pallas_call(
        lambda *r: main_kernel(scale, *r),
        out_shape=[jax.ShapeDtypeStruct((3200, 128), F32), jax.ShapeDtypeStruct((3200, 128), F32),
                   jax.ShapeDtypeStruct((1, 128), F32)],
        grid=(blocks,),
        in_specs=[pl.BlockSpec((NBR, 256, 256), lambda i: (0, i, 0)), pl.BlockSpec((NBR, 256), lambda i: (0, i)), lanes(),
                  pl.BlockSpec((4 * PAD, 256), lambda i: (0, i)), pl.BlockSpec((5, PAD, 256), lambda i: (0, 0, i)),
                  pl.BlockSpec((PAD, 256), lambda i: (0, i)), pl.BlockSpec((8, 256), lambda i: (0, i)), lanes(), lanes(),
                  pl.BlockSpec((1, 128), lambda i: (0, 0))] + [whole(a) for a in w],
        out_specs=[pl.BlockSpec((3200, 128), lambda i: (0, 0)), pl.BlockSpec((3200, 128), lambda i: (0, 0)),
                   pl.BlockSpec((1, 128), lambda i: (0, 0))],
        scratch_shapes=[pltpu.VMEM((NBR, 352, 256), F32), pltpu.VMEM((NBR, PAD, 256), BF), pltpu.VMEM((NBR, PAD, 256), F32),
                        pltpu.VMEM((20, 8, 256), F32), pltpu.VMEM((20, 8, 256), F32), pltpu.VMEM((352, 2560), BF),
                        pltpu.VMEM((528, 704), F32), pltpu.VMEM((352, 512), F32), pltpu.VMEM((PAD, 352), F32),
                        pltpu.VMEM((PAD, 352), F32), pltpu.VMEM((PAD, 512), F32), pltpu.VMEM((PAD, 512), F32),
                        pltpu.VMEM((16, PAD, 128), F32)],
        compiler_params=params(), name="main",
    )(near.reshape(NBR, ends, 256), near_ticks, ticks, msg, keep, ren, gap_own, labels, weights, total, *w)


def panels(flat, at, rows, count):
    return jnp.concatenate([flat[at + c * rows : at + (c + 1) * rows] for c in range(count)], axis=1)


def unsplit(x, axis):
    take = lambda a, b: lax.slice_in_dim(x, a, b, axis=axis)
    return jnp.concatenate([take(0, HALF), take(HPAD, HPAD + HALF)], axis=axis)


def unpack(ga, gb, vec):
    wide = panels(gb, 0, 528, 6)[:, :704].reshape(3, PAD, 4, PAD)[:, :MEM, :, :MEM].reshape(3 * MEM, 4 * MEM)
    vecs = jnp.concatenate([gb[3168:3184], gb[3184:3200]], axis=1)[:, :PAD]
    kv = panels(ga, 0, 352, 3)
    kv_out = jnp.concatenate([unsplit(kv[:PAD], 0), unsplit(kv[PAD:], 0)], axis=0)
    kv_out = jnp.concatenate([kv_out[:, :MEM], kv_out[:, PAD : PAD + MEM]], axis=1).T
    pick = lambda x: jnp.concatenate([x[:MEM, :MEM], x[:MEM, PAD : PAD + MEM]], axis=1)
    one = pick(panels(ga, 1056, PAD, 3))
    dec = pick(panels(ga, 1584, PAD, 3))
    qo = panels(ga, 2112, PAD, 3)
    th = panels(ga, 2640, PAD, 3)
    query_t = unsplit(qo[:, :MEM], 0)
    out = unsplit(qo[:, PAD : PAD + MEM], 0)[:, :MEM]
    two = th[:MEM, :MEM]
    hid_n = th[:MEM, PAD : PAD + MEM]
    phase = vec[1]
    phase_low = jnp.cos(phase).astype(BF).astype(F32)
    sum_dq = unsplit(vecs[15], 0)
    query = jnp.concatenate([query_t.T, phase_low[:, None] * sum_dq[None, :]], axis=0)
    grad_in = wide.T
    hid = jnp.concatenate([grad_in[:MEM, : 2 * MEM], hid_n], axis=1)
    tall = jnp.stack([query, one.T, dec.T])
    rows = [vecs[0, :MEM], vecs[1, :MEM], vecs[2, :MEM], vecs[3, :MEM], vecs[4, :MEM], vecs[2, :MEM], vecs[3, :MEM],
            vecs[7, :MEM], unsplit(vecs[8], 0), unsplit(vecs[9], 0)] + [vecs[i, :MEM] for i in range(10, 15)]
    return grad_in, hid, kv_out, tall, jnp.stack([out, two]), jnp.stack(rows), sum_dq


def adam_all(params_in, firsts, seconds, grads):
    squares_sum = jnp.zeros((), F32)
    for item in grads:
        squares_sum = squares_sum + jnp.sum(item * item)
    grad_norm = jnp.sqrt(squares_sum)
    factor = jnp.minimum(1.0, CLIP_AT / (grad_norm + NORM_EPS))
    new_params, new_firsts, new_seconds = [], [], []
    for at in range(len(params_in)):
        clipped = grads[at] * factor
        one = BETA_ONE * firsts[at] + (1.0 - BETA_ONE) * clipped
        two = BETA_TWO * seconds[at] + (1.0 - BETA_TWO) * clipped * clipped
        move = one / (1.0 - BETA_ONE**STEP) / (jnp.sqrt(two / (1.0 - BETA_TWO**STEP)) + ADAM_EPS)
        last = at == len(params_in) - 1
        decay, rate = (0.0, VECTOR_RATE) if last else (DECAY, LEARN_RATE)
        new_params.append(params_in[at] - rate * (move + decay * params_in[at]))
        new_firsts.append(one)
        new_seconds.append(two)
    return grad_norm, new_params, new_firsts, new_seconds


AXES = ("dp", "rep")


def body(source, target, neighbours, neighbour_ticks, event_ticks, event_types, labels, edge_feats, weights, memory,
         node_ticks, gru_in, gru_hid, keys_values, tall_stack, squares, vectors, *moments):
    events = event_ticks.shape[0]
    nodes = memory.shape[0]
    devices = lax.axis_size("dp") * lax.axis_size("rep")
    scale = TIME_RATE / (events * devices)
    tiles = events // 128
    order = lambda x: jnp.transpose(x, (2, 1, 0)).reshape(NBR, 2, tiles, 128).transpose(0, 2, 1, 3).reshape(NBR, 2 * events)
    end_nodes = jnp.stack([source.reshape(tiles, 128), target.reshape(tiles, 128)], axis=1).reshape(-1)
    near_ids = order(neighbours).reshape(-1)
    near_ticks = order(neighbour_ticks)
    row = lambda x: x.reshape(1, events)
    mem_t = memory.T
    w = prep(gru_in, gru_hid, keys_values, tall_stack, squares, vectors)
    wg, wgc, wh = w[0], w[1], w[2]
    vb = w[-1]
    table, own = build_table(end_nodes, mem_t, node_ticks)
    msg, keep, ren, ren_rows, gap_own = gru(scale, own, row(event_ticks), edge_feats.T, row(event_types), wg, wh, vb)
    near = gather_near(near_ids, table)
    weight_sum = lax.psum(jnp.sum(weights), AXES)
    ga, gb, loss = main(scale, near, near_ticks, row(event_ticks), msg, keep, ren, gap_own, row(labels), row(weights),
                        jnp.full((1, 128), weight_sum, F32), [wgc] + list(w[3:]))
    ga, gb, loss_sum = lax.psum((ga, gb, jnp.sum(loss)), AXES)
    grad_in, hid, kv, tall, square, vec, sum_dq = unpack(ga, gb, vectors)
    phase_in = jnp.sum(tall_stack[0][MEM:].astype(BF).astype(F32) * sum_dq[None, :], axis=1)
    vec = vec.at[1].add(-jnp.sin(vectors[1]) * phase_in)
    grad_norm, new_p, new_f, new_s = adam_all(
        (gru_in, gru_hid, keys_values, tall_stack, squares, vectors), moments[:6], moments[6:],
        (grad_in, hid, kv, tall, square, vec))
    ticks2 = jnp.stack([2 * event_ticks.reshape(tiles, 128), 2 * event_ticks.reshape(tiles, 128) + 1], axis=1).reshape(-1)
    local = jnp.full((nodes,), -1, I32).at[end_nodes].max(ticks2)
    latest = lax.pmax(local, AXES)
    winner = ticks2 == latest[end_nodes]
    rows = jnp.zeros((nodes, MEM), F32).at[end_nodes].add(jnp.where(winner[:, None], ren_rows[:, :MEM], 0.0))
    merged = lax.psum(rows, AXES)
    new_memory = jnp.where(latest[:, None] >= 0, merged, memory)
    return (grad_norm, loss_sum, weight_sum, new_memory, *new_p, *new_f, *new_s)


def solution(mesh):
    split = P(AXES)
    placed = (split, split, P(AXES, None, None), P(AXES, None, None), split, split, split, P(AXES, None), split)
    return jax.shard_map(body, mesh=mesh, in_specs=placed + (P(),) * 20, out_specs=(P(),) * 22, check_vma=False)
```

```python
import math

import jax
import jax.numpy as jnp
from jax import lax
from jax.experimental import pallas as pl
from jax.experimental.pallas import tpu as pltpu
from jax.sharding import PartitionSpec as P

F32 = jnp.float32
BF = jnp.bfloat16
I32 = jnp.int32
NBR = 10
MEM = 172
PAD = 176
HALF = 86
HPAD = 88
STEP = 10
LEARN_RATE = 0.03
VECTOR_RATE = 0.3
BETA_ONE = 0.9
BETA_TWO = 0.999
ADAM_EPS = 1e-08
DECAY = 0.01
CLIP_AT = 0.005
TIME_RATE = 64.0
NORM_EPS = 1e-06
VMEM_CAP = 58 * 2**20


def params(limit=VMEM_CAP):
    return pltpu.CompilerParams(vmem_limit_bytes=limit)


def nn(a, b):
    return lax.dot_general(a, b, (((1,), (0,)), ((), ())), preferred_element_type=F32)


def nt(a, b):
    return lax.dot_general(a, b, (((1,), (1,)), ((), ())), preferred_element_type=F32)


def zeros(rows, cols):
    return jnp.zeros((rows, cols), F32)


def rows_to(x, total):
    return jnp.concatenate([x, zeros(total - x.shape[0], x.shape[1])], axis=0)


def cols_to(x, total):
    return jnp.concatenate([x, zeros(x.shape[0], total - x.shape[1])], axis=1)


def split_rows(x):
    gap = zeros(HPAD - HALF, x.shape[1])
    return jnp.concatenate([x[:HALF], gap, x[HALF:], gap], axis=0)


def prep_kernel(gin, ghid, kv, tall, sq, vec,
                wg, wgc, wh, kvm, kvct, kvc, t0t, t0, t1t, t1, t2t, t2, s0t, s0, s1t, s1, vb):
    full = gin[...]
    for gate in range(3):
        rows = full[gate * MEM : (gate + 1) * MEM]
        parts = [cols_to(rows[:, q * MEM : (q + 1) * MEM], PAD) for q in range(4)]
        wide = rows_to(jnp.concatenate(parts, axis=1), PAD)
        wg[pl.ds(gate * PAD, PAD), :] = wide.astype(BF)
        code = cols_to(rows_to(rows[:, 2 * MEM : 3 * MEM], PAD), 256)
        wgc[:, gate * PAD : (gate + 1) * PAD] = jnp.transpose(code)[:PAD].astype(BF)
    hid = ghid[...]
    for gate in range(3):
        part = cols_to(rows_to(hid[:, gate * MEM : (gate + 1) * MEM], PAD), 256)
        wh[pl.ds(gate * PAD, PAD), :] = jnp.transpose(part)[:PAD].astype(BF)
    pairs = kv[...]
    mem_t = jnp.transpose(cols_to(rows_to(pairs[:MEM], 256), 384))
    code_t = jnp.transpose(cols_to(rows_to(pairs[MEM:], 256), 384))
    kvm[...] = jnp.concatenate([split_rows(mem_t[:MEM]), split_rows(mem_t[MEM : 2 * MEM])], axis=0).astype(BF)
    code_rows = jnp.concatenate([split_rows(code_t[:MEM]), split_rows(code_t[MEM : 2 * MEM])], axis=0)
    kvct[...] = code_rows[:, :PAD].astype(BF)
    kvc[...] = jnp.transpose(rows_to(code_rows, 384))[:PAD, : 2 * PAD].astype(BF)
    query = tall[0]
    query_t = split_rows(query[:, :MEM])
    t0t[...] = cols_to(query_t, PAD).astype(BF)
    t0[...] = jnp.transpose(rows_to(cols_to(query_t, 256), 256))[:PAD, :PAD].astype(BF)
    for src, fwd, back in ((tall[1], t1t, t1), (tall[2], t2t, t2)):
        wide = jnp.concatenate([cols_to(src[:, :MEM], PAD), cols_to(src[:, MEM:], PAD)], axis=1)
        fwd[...] = rows_to(wide, PAD).astype(BF)
        back[...] = jnp.transpose(rows_to(cols_to(wide, 384), 256))[: 2 * PAD, :PAD].astype(BF)
    first = cols_to(split_rows(sq[0]), PAD)
    s0[...] = first.astype(BF)
    s0t[...] = jnp.transpose(rows_to(cols_to(first, 256), 256))[:PAD, :PAD].astype(BF)
    second = rows_to(cols_to(sq[1], PAD), PAD)
    s1[...] = second.astype(BF)
    s1t[...] = jnp.transpose(rows_to(cols_to(second, 256), 256))[:PAD, :PAD].astype(BF)
    cols = jnp.transpose(cols_to(rows_to(vec[...], 128), 256))
    phase_low = jnp.cos(cols[:PAD, 1:2]).astype(BF)
    wide_phase = jnp.broadcast_to(phase_low.astype(F32), (PAD, 128)).astype(BF)
    row_id = lax.broadcasted_iota(I32, (PAD, 128), 0)
    wide_phase = jnp.where(row_id < MEM, wide_phase.astype(F32), 0.0).astype(BF)
    steady = nn(cols_to(split_rows(query[:, MEM:]), PAD).astype(BF), wide_phase)
    for i in range(15):
        column = cols[:, i : i + 1]
        if i in (8, 9):
            column = split_rows(column[:MEM])
        wide = jnp.broadcast_to(column[:PAD], (PAD, 128))
        vb[i] = wide + steady if i == 8 else wide


def prep(gin, ghid, kv, tall, sq, vec):
    bf = lambda *s: jax.ShapeDtypeStruct(s, BF)
    outs = [bf(528, 704), bf(176, 528), bf(528, 176), bf(352, 256), bf(352, 176), bf(176, 352),
            bf(176, 176), bf(176, 176), bf(176, 352), bf(352, 176), bf(176, 352), bf(352, 176),
            bf(176, 176), bf(176, 176), bf(176, 176), bf(176, 176), jax.ShapeDtypeStruct((15, PAD, 128), F32)]
    return pl.pallas_call(
        prep_kernel, out_shape=outs, compiler_params=params(), name="prep",
    )(gin.T, ghid, kv, jnp.transpose(tall, (0, 2, 1)), sq, vec)


def table_kernel(steps, ids, mem, ticks, table, own, wide):
    step = pl.program_id(0)
    cols = mem.shape[1]

    @pl.when(step == 0)
    def _():
        wide[...] = jnp.zeros_like(wide)

    @pl.when(step < steps)
    def _():
        wide[0:MEM, :] = mem[...].astype(BF).astype(F32)
        wide[PAD : PAD + 1, :] = ticks[...].astype(F32)
        base = pl.multiple_of(step * cols, cols)
        wide[PAD + 1 : PAD + 2, :] = (lax.broadcasted_iota(I32, (1, cols), 1) + base).astype(F32)
        for c in range(cols // 128):
            for h in range(2):
                table[pl.ds(base + 128 * c, 128), 128 * h : 128 * h + 128] = jnp.transpose(
                    wide[128 * h : 128 * h + 128, 128 * c : 128 * c + 128])

    @pl.when(step == steps)
    def _():
        def group(g, carry):
            for v in range(4):
                at = pl.multiple_of(g * 32 + v * 8, 8)
                rows = [table[pl.ds(ids[at + u], 1), :] for u in range(8)]
                own[pl.ds(at, 8), :] = jnp.concatenate(rows, axis=0)
            return carry

        lax.fori_loop(0, own.shape[0] // 32, group, 0)


def build_table(ids, mem_t, ticks):
    nodes = mem_t.shape[1]
    ends = ids.shape[0]
    cols = 1024
    steps = nodes // cols
    return pl.pallas_call(
        lambda *r: table_kernel(steps, *r),
        out_shape=[jax.ShapeDtypeStruct((nodes, 256), F32), jax.ShapeDtypeStruct((ends, 256), F32)],
        grid=(steps + 1,),
        in_specs=[pl.BlockSpec(memory_space=pltpu.SMEM),
                  pl.BlockSpec((MEM, cols), lambda i: (0, jnp.minimum(i, steps - 1))),
                  pl.BlockSpec((1, cols), lambda i: (0, jnp.minimum(i, steps - 1)))],
        out_specs=[pl.BlockSpec((nodes, 256), lambda i: (0, 0)), pl.BlockSpec((ends, 256), lambda i: (0, 0))],
        scratch_shapes=[pltpu.VMEM((256, cols), F32)],
        compiler_params=params(), name="table",
    )(ids, mem_t, ticks.reshape(1, nodes))


def near_kernel(chunk, ids, table, near):
    step = pl.program_id(0)
    base = step * chunk

    def group(g, carry):
        for v in range(2):
            at = pl.multiple_of(g * 32 + v * 16, 16)
            rows = [table[pl.ds(ids[base + at + u], 1), :] for u in range(16)]
            near[pl.ds(at, 16), :] = jnp.concatenate(rows, axis=0).astype(BF)
        return carry

    lax.fori_loop(0, chunk // 32, group, 0)


def gather_near(ids, table):
    chunk = 1024
    total = ids.shape[0]
    return pl.pallas_call(
        lambda *r: near_kernel(chunk, *r),
        out_shape=jax.ShapeDtypeStruct((total, 256), BF),
        grid=(total // chunk,),
        in_specs=[pl.BlockSpec(memory_space=pltpu.SMEM), pl.BlockSpec(table.shape, lambda i: (0, 0))],
        out_specs=pl.BlockSpec((chunk, 256), lambda i: (i, 0)),
        compiler_params=params(), name="near",
    )(ids, table)


PI_HI = 1.5703125
PI_MID = 4.8351287841796875e-04
PI_LO = 3.1385571319e-07
TURN = 12582912.0


def cos_sin(x):
    shifted = x * (2.0 / math.pi) + TURN
    n = shifted - TURN
    r = ((x - n * PI_HI) - n * PI_MID) - n * PI_LO
    z = r * r
    sin_r = r + r * (z * (-1.6666654611e-01 + z * (8.3321608736e-03 + z * -1.9515295891e-04)))
    cos_r = (1.0 - 0.5 * z) + (z * z) * (4.166664568298827e-02 + z * (-1.388731625493765e-03 + z * 2.443315711809948e-05))
    q = n.astype(I32)
    odd = (q & 1) == 1
    c = jnp.where(odd, sin_r, cos_r)
    s = jnp.where(odd, cos_r, sin_r)
    c = jnp.where(((q + 1) & 2) == 2, -c, c)
    s = jnp.where((q & 2) == 2, -s, s)
    return c, s


def sigmoid(x):
    return 0.5 * jnp.tanh(0.5 * x) + 0.5


def twice(x):
    return jnp.concatenate([x, x], axis=1)


def wide_rows(x, rows):
    return jnp.broadcast_to(x, (rows, x.shape[1]))


def gru_kernel(scale, own, ticks, edge, types, wg, wh, vb, msg, keep, ren, rows, gap_out):
    own_t = jnp.concatenate(
        [jnp.transpose(own[0:128, :]), jnp.transpose(own[128:256, :])], axis=1)
    gap = (twice(ticks[...].astype(F32)) - own_t[PAD : PAD + 1]) * scale
    row_id = lax.broadcasted_iota(I32, (PAD, 256), 0)
    own_x = jnp.where(row_id < MEM, own_t[:PAD], 0.0)
    msg[0:PAD, :] = own_x.astype(BF)
    msg[PAD : 2 * PAD, :] = jnp.concatenate([own_x[:, 128:], own_x[:, :128]], axis=1).astype(BF)
    edges = rows_to(edge[...].astype(F32) * types[...].astype(F32), PAD)
    msg[3 * PAD : 4 * PAD, :] = twice(edges).astype(BF)
    gap_out[...] = wide_rows(gap, 8)
    gap16 = wide_rows(gap, 16)
    for st in range(PAD // 16):
        at = 16 * st
        x = twice(vb[0, at : at + 16, :]) * gap16 + twice(vb[1, at : at + 16, :])
        c, s = cos_sin(x)
        msg[2 * PAD + at : 2 * PAD + at + 16, :] = c.astype(BF)
        keep[4, at : at + 16, :] = -s
    gates = nn(wg[...], msg[...])
    hidden = nn(wh[...], msg[0:PAD, :])
    for st in range(PAD // 8):
        at = 8 * st
        o = own_x[at : at + 8]
        pre = [gates[g * PAD + at : g * PAD + at + 8] + twice(vb[2 + g, at : at + 8, :]) for g in range(3)]
        hid = [hidden[g * PAD + at : g * PAD + at + 8] + twice(vb[5 + g, at : at + 8, :]) for g in range(3)]
        u = sigmoid(pre[0] + hid[0])
        r = sigmoid(pre[1] + hid[1])
        n = jnp.tanh(pre[2] + r * hid[2])
        keep[0, at : at + 8, :] = u
        keep[1, at : at + 8, :] = r
        keep[2, at : at + 8, :] = n
        keep[3, at : at + 8, :] = hid[2]
        ren[at : at + 8, :] = (1.0 - u) * n + u * o
    full = jnp.concatenate([ren[0:MEM, :], own_t[PAD + 1 : PAD + 2], zeros(255 - MEM, 256)], axis=0)
    rows[0:128, :] = jnp.transpose(full[:, :128])
    rows[128:256, :] = jnp.transpose(full[:, 128:])


def gru(scale, own, ticks, edge_t, types, wg, wh, vb):
    ends = own.shape[0]
    blocks = ends // 256
    whole = lambda a: pl.BlockSpec(a.shape, lambda i: (0,) * len(a.shape))
    return pl.pallas_call(
        lambda *r: gru_kernel(scale, *r),
        out_shape=[jax.ShapeDtypeStruct((4 * PAD, ends), BF), jax.ShapeDtypeStruct((5, PAD, ends), F32),
                   jax.ShapeDtypeStruct((PAD, ends), F32), jax.ShapeDtypeStruct((ends, 256), F32),
                   jax.ShapeDtypeStruct((8, ends), F32)],
        grid=(blocks,),
        in_specs=[pl.BlockSpec((256, 256), lambda i: (i, 0)), pl.BlockSpec((1, 128), lambda i: (0, i)),
                  pl.BlockSpec((MEM, 128), lambda i: (0, i)), pl.BlockSpec((1, 128), lambda i: (0, i)),
                  whole(wg), whole(wh), whole(vb)],
        out_specs=[pl.BlockSpec((4 * PAD, 256), lambda i: (0, i)), pl.BlockSpec((5, PAD, 256), lambda i: (0, 0, i)),
                   pl.BlockSpec((PAD, 256), lambda i: (0, i)), pl.BlockSpec((256, 256), lambda i: (i, 0)),
                   pl.BlockSpec((8, 256), lambda i: (0, i))],
        compiler_params=params(), name="gru",
    )(own, ticks, edge_t, types, wg, wh, vb)


GELU_C = math.sqrt(2.0 / math.pi)


def gelu_parts(x):
    sq = x * x
    t = jnp.tanh(GELU_C * (x + 0.044715 * (sq * x)))
    half = 0.5 * (1.0 + t)
    slope = half + (0.5 * x) * (1.0 - t * t) * (GELU_C + (GELU_C * 3.0 * 0.044715) * sq)
    return x * half, slope


def fold(x):
    return x[:, :128] + x[:, 128:]


def main_kernel(scale, core, near, gaps_t, ticks, msg, keep, ren, gap_own, labels, weights, total,
                wgc, kvm, kvct, kvc, t0t, t0, t1t, t1, t2t, t2, s0t, s0, s1t, s1, vb,
                mine, theirs,
                loss, pair, code, dcode, soft, back, grads, g_in, g_kv, g_one, g_dec, g_qo, g_th, vacc):
    step = pl.program_id(0)
    inv_size = HALF ** -0.5

    @pl.when(step == 0)
    def _():
        for ref in (g_in, g_kv, g_one, g_dec, g_qo, g_th, vacc, loss):
            ref[...] = jnp.zeros_like(ref)

    tick2 = twice(ticks[...].astype(F32))
    renewed = ren[...]
    ren_low = renewed.astype(BF)
    queries = nn(t0t[...], ren_low) + twice(vb[8])
    for j in range(NBR):
        gap16 = wide_rows((tick2 - gaps_t[j : j + 1, :].astype(F32)) * scale, 16)
        for st in range(PAD // 16):
            at = 16 * st
            x = twice(vb[0, at : at + 16, :]) * gap16 + twice(vb[1, at : at + 16, :])
            c, s = cos_sin(x)
            code[j, at : at + 16, :] = c.astype(BF)
            dcode[j, at : at + 16, :] = -s
        pair[j] = nt(kvm[...], near[j]) + nn(kvct[...], code[j])
        for h in range(2):
            acc = zeros(8, 256)
            for st in range(HPAD // 8):
                at = HPAD * h + 8 * st
                acc = acc + pair[j, at : at + 8, :] * queries[at : at + 8]
            soft[2 * j + h] = wide_rows(jnp.sum(acc, axis=0, keepdims=True) * inv_size, 8)
    for h in range(2):
        top = soft[h]
        for j in range(1, NBR):
            top = jnp.maximum(top, soft[2 * j + h])
        norm = zeros(8, 256)
        for j in range(NBR):
            e = jnp.exp(soft[2 * j + h] - top)
            soft[2 * j + h] = e
            norm = norm + e
        inv = 1.0 / norm
        for j in range(NBR):
            soft[2 * j + h] = soft[2 * j + h] * inv
    att = []
    for st in range(PAD // 8):
        at = 8 * st
        h = 0 if at < HPAD else 1
        acc = twice(vb[9, at : at + 8, :])
        for j in range(NBR):
            acc = acc + soft[2 * j + h] * pair[j, PAD + at : PAD + at + 8, :]
        att.append(acc)
    att_low = jnp.concatenate(att, axis=0).astype(BF)
    projected = nn(s0t[...], att_low) + twice(vb[10])
    mlp_in = jnp.concatenate([projected.astype(BF), ren_low], axis=0)
    inner = nn(t1t[...], mlp_in) + twice(vb[11])
    act, act_slope = gelu_parts(inner)
    act_low = act.astype(BF)
    emb_low = (nn(s1t[...], act_low) + twice(vb[12])).astype(BF)
    dec_in = jnp.concatenate([emb_low[:, :128], emb_low[:, 128:]], axis=0)
    dec_pre = nn(t2t[...], dec_in) + vb[13]
    dec_act, dec_slope = gelu_parts(dec_pre)
    logit = jnp.sum(dec_act * vb[14], axis=0, keepdims=True)
    label = labels[...].astype(F32)
    tail = jnp.exp(-jnp.abs(logit))
    plus = jnp.maximum(logit, 0.0) + jnp.log1p(tail)
    loss[...] += weights[...] * (plus - label * logit)
    d_logit = weights[...] / total[...] * (sigmoid(logit) - label)
    d_out = d_logit * dec_act
    d_dec = (d_logit * vb[14]) * dec_slope
    d_dec_low = d_dec.astype(BF)
    g_dec[...] += nt(d_dec_low, dec_in)
    d_dec_in = nn(t2[...], d_dec_low)
    d_emb = jnp.concatenate([d_dec_in[:PAD], d_dec_in[PAD:]], axis=1)
    d_emb_low = d_emb.astype(BF)
    g_th[:, 0:256] += jnp.concatenate([nt(act_low, d_emb_low), zeros(PAD, 256 - PAD)], axis=1)
    d_inner = nn(s1[...], d_emb_low) * act_slope
    d_inner_low = d_inner.astype(BF)
    g_one[...] += nt(d_inner_low, mlp_in)
    d_mlp = nn(t1[...], d_inner_low)
    d_proj = d_mlp[:PAD]
    d_proj_low = d_proj.astype(BF)
    g_qo[:, 256:512] += jnp.concatenate([nt(att_low, d_proj_low), zeros(PAD, 256 - PAD)], axis=1)
    d_att = nn(s0[...], d_proj_low)
    for h in range(2):
        mean = zeros(8, 256)
        for j in range(NBR):
            acc = zeros(8, 256)
            for st in range(HPAD // 8):
                at = HPAD * h + 8 * st
                acc = acc + pair[j, PAD + at : PAD + at + 8, :] * d_att[at : at + 8]
            wide = wide_rows(jnp.sum(acc, axis=0, keepdims=True), 8)
            back[2 * j + h] = wide
            mean = mean + wide * soft[2 * j + h]
        for j in range(NBR):
            back[2 * j + h] = (soft[2 * j + h] * inv_size) * (back[2 * j + h] - mean)
    d_q = []
    for st in range(PAD // 8):
        at = 8 * st
        h = 0 if at < HPAD else 1
        acc = zeros(8, 256)
        for j in range(NBR):
            acc = acc + back[2 * j + h] * pair[j, at : at + 8, :]
        d_q.append(acc)
    d_query = jnp.concatenate(d_q, axis=0)
    for j in range(NBR):
        for st in range(2 * PAD // 16):
            parts = []
            for half in range(2):
                at = 16 * st + 8 * half
                if at < PAD:
                    parts.append(back[2 * j + (at >= HPAD)] * queries[at : at + 8])
                else:
                    parts.append(soft[2 * j + (at - PAD >= HPAD)] * d_att[at - PAD : at - PAD + 8])
            grads[16 * st : 16 * st + 16, 256 * j : 256 * j + 256] = jnp.concatenate(parts, axis=0).astype(BF)
    d_codes = nn(kvc[...], grads[...])
    for st in range(PAD // 8):
        at = 8 * st
        f_acc = zeros(8, 256)
        p_acc = zeros(8, 256)
        for j in range(NBR):
            gap8 = wide_rows((tick2 - gaps_t[j : j + 1, :].astype(F32)) * scale, 8)
            d_arg = d_codes[at : at + 8, 256 * j : 256 * j + 256] * dcode[j, at : at + 8, :]
            f_acc = f_acc + d_arg * gap8
            p_acc = p_acc + d_arg
        vacc[0, at : at + 8, :] += fold(f_acc)
        vacc[1, at : at + 8, :] += fold(p_acc)
    mem_part = nn(grads[:, 0:256], near[0])
    code_part = nt(grads[:, 0:256], code[0])
    for j in range(1, NBR):
        mem_part = mem_part + nn(grads[:, 256 * j : 256 * j + 256], near[j])
        code_part = code_part + nt(grads[:, 256 * j : 256 * j + 256], code[j])
    g_kv[:, 0:256] += mem_part
    g_kv[:, 256:512] += jnp.concatenate([code_part, zeros(2 * PAD, 256 - PAD)], axis=1)
    d_q_low = d_query.astype(BF)
    g_qo[:, 0:256] += jnp.concatenate([nt(d_q_low, ren_low), zeros(PAD, 256 - PAD)], axis=1)
    d_ren = d_mlp[PAD:] + nn(t0[...], d_q_low)
    own_x = msg[0:PAD, :].astype(F32)
    u, r, n, hn = keep[0], keep[1], keep[2], keep[3]
    d_u = d_ren * (own_x - n) * (u * (1.0 - u))
    d_n = d_ren * (1.0 - u) * (1.0 - n * n)
    d_r = d_n * hn * (r * (1.0 - r))
    d_h = d_n * r
    gates = jnp.concatenate([d_u, d_r, d_n], axis=0).astype(BF)
    g_in[...] += nt(gates, msg[...])
    g_th[:, 256:512] += jnp.concatenate([nt(msg[0:PAD, :], d_h.astype(BF)), zeros(PAD, 256 - PAD)], axis=1)
    d_arg = nn(wgc[...], gates) * keep[4]
    vacc[0] += fold(d_arg * gap_own[0:1, :])
    vacc[1] += fold(d_arg)
    for i, item in ((2, d_u), (3, d_r), (4, d_n), (7, d_h), (8, d_query), (9, d_att), (10, d_proj), (11, d_inner),
                    (12, d_emb), (15, d_q_low.astype(F32))):
        vacc[i] += fold(item)
    vacc[13] += d_dec
    vacc[14] += d_out

    def finish(ga, gb):
        wide = cols_to(g_in[...], 768)
        for c in range(6):
            gb[528 * c : 528 * c + 528, :] = wide[:, 128 * c : 128 * c + 128]
        lane = lax.broadcasted_iota(I32, (PAD, 128), 1)
        vecs = zeros(PAD, 128)
        for i in range(16):
            column = jnp.sum(vacc[i], axis=1, keepdims=True)
            vecs = jnp.where(lane == i, column, vecs)
        flat = jnp.transpose(jnp.concatenate([vecs, zeros(256 - PAD, 128)], axis=0))
        gb[3168:3184, :] = flat[0:16, 0:128]
        gb[3184:3200, :] = flat[0:16, 128:256]
        at = 0
        for left, right, rows in ((g_kv[:, 0:PAD], g_kv[:, 256 : 256 + PAD], 352),
                                  (g_one[:, 0:PAD], g_one[:, PAD : 2 * PAD], 176),
                                  (g_dec[:, 0:PAD], g_dec[:, PAD : 2 * PAD], 176),
                                  (g_qo[:, 0:PAD], g_qo[:, 256 : 256 + PAD], 176),
                                  (g_th[:, 0:PAD], g_th[:, 256 : 256 + PAD], 176)):
            wide = jnp.concatenate([left, right, zeros(rows, 32)], axis=1)
            for c in range(3):
                ga[at : at + rows, :] = wide[:, 128 * c : 128 * c + 128]
                at += rows
        ga[3168:3200, :] = rows_to(loss[...], 32)

    @pl.when((step == pl.num_programs(0) - 1) & (core[0] == 0))
    def _():
        finish(mine, theirs)

    @pl.when((step == pl.num_programs(0) - 1) & (core[0] != 0))
    def _():
        finish(theirs, mine)


def main(scale, near, near_ticks, ticks, msg, keep, ren, gap_own, labels, weights, total, core, w):
    ends = ren.shape[1]
    blocks = ends // 256
    whole = lambda a: pl.BlockSpec(a.shape, lambda i: (0,) * len(a.shape))
    lanes = lambda: pl.BlockSpec((1, 128), lambda i: (0, i))
    return pl.pallas_call(
        lambda *r: main_kernel(scale, *r),
        out_shape=[jax.ShapeDtypeStruct((3200, 128), F32), jax.ShapeDtypeStruct((3200, 128), F32)],
        grid=(blocks,),
        in_specs=[pl.BlockSpec(memory_space=pltpu.SMEM), pl.BlockSpec((NBR, 256, 256), lambda i: (0, i, 0)), pl.BlockSpec((NBR, 256), lambda i: (0, i)), lanes(),
                  pl.BlockSpec((4 * PAD, 256), lambda i: (0, i)), pl.BlockSpec((5, PAD, 256), lambda i: (0, 0, i)),
                  pl.BlockSpec((PAD, 256), lambda i: (0, i)), pl.BlockSpec((8, 256), lambda i: (0, i)), lanes(), lanes(),
                  pl.BlockSpec((1, 128), lambda i: (0, 0))] + [whole(a) for a in w],
        out_specs=[pl.BlockSpec((3200, 128), lambda i: (0, 0)), pl.BlockSpec((3200, 128), lambda i: (0, 0))],
        scratch_shapes=[pltpu.VMEM((1, 128), F32), pltpu.VMEM((NBR, 352, 256), F32), pltpu.VMEM((NBR, PAD, 256), BF), pltpu.VMEM((NBR, PAD, 256), F32),
                        pltpu.VMEM((20, 8, 256), F32), pltpu.VMEM((20, 8, 256), F32), pltpu.VMEM((352, 2560), BF),
                        pltpu.VMEM((528, 704), F32), pltpu.VMEM((352, 512), F32), pltpu.VMEM((PAD, 352), F32),
                        pltpu.VMEM((PAD, 352), F32), pltpu.VMEM((PAD, 512), F32), pltpu.VMEM((PAD, 512), F32),
                        pltpu.VMEM((16, PAD, 128), F32)],
        compiler_params=params(), name="main",
    )(core, near.reshape(NBR, ends, 256), near_ticks, ticks, msg, keep, ren, gap_own, labels, weights, total, *w)


def room(nodes, devices):
    return -(-(nodes * 9) // (devices * 8 * 16)) * 16


def pack_kernel(cap, rounds, nodes, ticks, latest, rows, out, first, second):
    second[...] = jnp.full_like(second, -1.0)

    def chunk(b, count):
        base = b * 128
        ticks_at = lax.div(b, 2) * 128
        role = lax.rem(b, 2)

        def eight(g, count):
            for v in range(8):
                e = g * 8 + v
                i = base + e
                won = latest[nodes[i]] == 2 * ticks[ticks_at + e] + role
                row = rows[pl.ds(i, 1), :]
                first[pl.ds(count, 1), :] = row[:, 0:128]
                second[pl.ds(count, 1), :] = row[:, 128:256]
                count = count + won.astype(I32)
            return count

        return lax.fori_loop(0, 16, eight, count)

    count = lax.fori_loop(0, nodes.shape[0] // 128, chunk, jnp.int32(0))
    second[pl.ds(count, 1), :] = jnp.full((1, 128), -1.0, F32)
    tail = cap // 2
    for r in range(rounds):
        at = r * cap
        out[r, 0:cap, :] = first[at : at + cap, :]
        out[r, cap : cap + tail, :] = jnp.concatenate(
            [second[at : at + tail, 0:64], second[at + tail : at + cap, 0:64]], axis=1)


def pack(cap, nodes, ticks, latest, rows):
    ends = nodes.shape[0]
    rounds = ends // cap + 1
    smem = pl.BlockSpec(memory_space=pltpu.SMEM)
    spare = rounds * cap + 8
    return pl.pallas_call(
        lambda *r: pack_kernel(cap, rounds, *r),
        out_shape=jax.ShapeDtypeStruct((rounds, cap + cap // 2, 128), F32),
        in_specs=[smem, smem, smem, pl.BlockSpec(memory_space=pltpu.VMEM)],
        out_specs=pl.BlockSpec(memory_space=pltpu.VMEM),
        scratch_shapes=[pltpu.VMEM((spare, 128), F32), pltpu.VMEM((spare, 128), F32)],
        compiler_params=params(), name="pack",
    )(nodes, ticks, latest, rows)


def merge_kernel(cap, blocks, ids, counts, rows, mem, out, table, second):
    step = pl.program_id(0)
    tail = cap // 2

    @pl.when(step == 0)
    def _():
        table[...] = jnp.full_like(table, -1.0)

    @pl.when(step < blocks)
    def _():
        half = rows[0, cap : cap + tail, :]
        second[0:tail, :] = half
        second[tail:cap, :] = jnp.concatenate([half[:, 64:], half[:, :64]], axis=1)
        base = step * cap

        def eight(g, carry):
            for v in range(8):
                i = g * 8 + v
                table[pl.ds(ids[base + i], 1), :] = jnp.concatenate(
                    [rows[0, pl.ds(i, 1), :], second[pl.ds(i, 1), :]], axis=1)
            return carry

        lax.fori_loop(0, lax.div(counts[step] + 7, 8), eight, 0)

    @pl.when(step >= blocks)
    def _():
        cols = mem.shape[1]
        base = pl.multiple_of((step - blocks) * cols, cols)
        for c in range(cols // 128):
            at = base + 128 * c
            top = jnp.transpose(table[pl.ds(at, 128), 0:128])
            low = jnp.transpose(table[pl.ds(at, 128), 128:256])
            fresh = low[MEM - 128 : MEM - 127] >= 0.0
            out[0:128, 128 * c : 128 * c + 128] = jnp.where(fresh, top, mem[0:128, 128 * c : 128 * c + 128])
            out[128:MEM, 128 * c : 128 * c + 128] = jnp.where(
                fresh, low[: MEM - 128], mem[128:MEM, 128 * c : 128 * c + 128])


def merge(cap, gathered, mem_t):
    blocks, height, _ = gathered.shape
    nodes = mem_t.shape[1]
    cols = 1024
    ids = jnp.concatenate([gathered[:, cap:, MEM - 128], gathered[:, cap:, MEM - 64]], axis=1)
    counts = jnp.sum((ids >= 0.0).astype(I32), axis=1)
    ids = jnp.where(ids >= 0.0, ids, float(nodes)).astype(I32).reshape(-1)
    smem = pl.BlockSpec(memory_space=pltpu.SMEM)
    part = lambda i: (0, jnp.maximum(i - blocks, 0))
    new = pl.pallas_call(
        lambda *r: merge_kernel(cap, blocks, *r),
        out_shape=jax.ShapeDtypeStruct((MEM, nodes), F32),
        grid=(blocks + nodes // cols,),
        in_specs=[smem, smem, pl.BlockSpec((1, height, 128), lambda i: (jnp.minimum(i, blocks - 1), 0, 0)),
                  pl.BlockSpec((MEM, cols), part)],
        out_specs=pl.BlockSpec((MEM, cols), part),
        scratch_shapes=[pltpu.VMEM((nodes + 8, 256), F32), pltpu.VMEM((cap, 128), F32)],
        compiler_params=params(), name="merge",
    )(ids, counts, gathered, mem_t)
    return new, jnp.any(counts == cap)


def move(param, one, two, grad, factor, rate, decay):
    clipped = grad * factor
    one = BETA_ONE * one + (1.0 - BETA_ONE) * clipped
    two = BETA_TWO * two + (1.0 - BETA_TWO) * clipped * clipped
    step = (one * (1.0 / (1.0 - BETA_ONE**STEP))) / (jnp.sqrt(two * (1.0 / (1.0 - BETA_TWO**STEP))) + ADAM_EPS)
    return param - rate * (step + decay * param), one, two


def unsplit(x, axis):
    take = lambda a, b: lax.slice_in_dim(x, a, b, axis=axis)
    return jnp.concatenate([take(0, HALF), take(HPAD, HPAD + HALF)], axis=axis)


def adam_kernel(count, where, *refs):
    mine, other = refs[:count], refs[count : 2 * count]
    refs = refs[2 * count :]
    state, news, (norm_out, loss_out) = refs[:18], refs[18:36], refs[36:38]
    a, b, g_gin, g_hid, g_kv, g_tall, g_sq, g_vec = refs[38:]
    core, place = where[0], where[1]
    height = mine[0].shape[0]
    for k in range(count):
        at = pl.multiple_of((place ^ k) * height, 8)

        @pl.when(core == 0)
        def _():
            a[pl.ds(at, height), :] = mine[k][...]
            b[pl.ds(at, height), :] = other[k][...]

        @pl.when(core != 0)
        def _():
            b[pl.ds(at, height), :] = mine[k][...]
            a[pl.ds(at, height), :] = other[k][...]

    def panels(ref, at, rows, n):
        return jnp.concatenate([ref[at + c * rows : at + (c + 1) * rows, :] for c in range(n)], axis=1)

    vec = state[5]
    tall = state[3]
    wide = panels(b, 0, 528, 6)
    gates = []
    for g in range(3):
        rows = wide[PAD * g : PAD * g + MEM]
        gates.append(jnp.concatenate([rows[:, PAD * q : PAD * q + MEM] for q in range(4)], axis=1))
    g_gin[...] = jnp.concatenate(gates, axis=0)
    vecs = jnp.concatenate([b[3168:3184, :], b[3184:3200, :]], axis=1)
    kv = panels(a, 0, 352, 3)
    kv = jnp.concatenate([unsplit(kv[:PAD], 0), unsplit(kv[PAD:], 0)], axis=0)
    kv = jnp.concatenate([kv[:, :MEM], kv[:, PAD : PAD + MEM]], axis=1)
    g_kv[...] = jnp.transpose(rows_to(cols_to(kv, 384), 384))[: 2 * MEM, : 2 * MEM]
    for i, at in ((1, 1056), (2, 1584)):
        x = panels(a, at, PAD, 3)[:MEM]
        g_tall[i] = jnp.concatenate([x[:, :MEM], x[:, PAD : PAD + MEM]], axis=1)
    both = unsplit(panels(a, 2112, PAD, 3), 0)
    sum_dq = unsplit(jnp.transpose(rows_to(vecs, 128))[:PAD, 15:16], 0)
    phase = vec[1:2, :]
    phase_low = jnp.cos(phase).astype(BF).astype(F32)
    g_tall[0] = jnp.concatenate([both[:, :MEM], sum_dq * phase_low], axis=1)
    g_sq[0] = both[:, PAD : PAD + MEM]
    last = panels(a, 2640, PAD, 3)[:MEM]
    g_sq[1] = last[:, :MEM]
    shared = jnp.transpose(rows_to(cols_to(g_gin[0 : 2 * MEM, 0:MEM], 256), 384))[:MEM, : 2 * MEM]
    g_hid[...] = jnp.concatenate([shared, last[:, PAD : PAD + MEM]], axis=1)
    query_low = tall[0][:, MEM:].astype(BF).astype(F32)
    phase_in = jnp.sum(query_low * sum_dq, axis=0, keepdims=True)
    row = lambda i: vecs[i : i + 1, :MEM]
    g_vec[...] = jnp.concatenate(
        [row(0), row(1) - jnp.sin(phase) * phase_in, row(2), row(3), row(4), row(2), row(3), row(7),
         unsplit(vecs[8:9], 1), unsplit(vecs[9:10], 1)] + [row(i) for i in range(10, 15)], axis=0)
    total = jnp.zeros((1, 1), F32)
    for ref in (g_gin, g_hid, g_kv, g_vec):
        total += jnp.sum(ref[...] * ref[...], keepdims=True)
    for ref in (g_tall, g_sq):
        for i in range(ref.shape[0]):
            total += jnp.sum(ref[i] * ref[i], keepdims=True)
    norm = jnp.sqrt(total)
    factor = jnp.minimum(1.0, CLIP_AT / (norm + NORM_EPS))
    norm_out[...] = norm
    loss_out[...] = jnp.sum(a[3168:3169, :], keepdims=True)
    for i, grad in enumerate((g_gin, g_hid, g_kv, g_tall, g_sq, g_vec)):
        rate, decay = (VECTOR_RATE, 0.0) if i == 5 else (LEARN_RATE, DECAY)
        param, one, two = state[i], state[6 + i], state[12 + i]
        new = news[i], news[6 + i], news[12 + i]
        if len(param.shape) == 3:
            for j in range(param.shape[0]):
                made = move(param[j], one[j], two[j], grad[j], factor, rate, decay)
                for ref, value in zip(new, made):
                    ref[j] = value
        else:
            rows = param.shape[0]
            for at in range(0, rows, 16):
                s = slice(at, min(at + 16, rows))
                made = move(param[s], one[s], two[s], grad[s], factor, rate, decay)
                for ref, value in zip(new, made):
                    ref[s] = value


def adam(where, mine, other, state):
    swap = lambda x: jnp.transpose(x, (0, 2, 1))
    def ready(group):
        gin, hid, kv, tall, sq, vec = group
        return [gin.T, hid, kv, swap(tall), sq, vec]
    state = ready(state[0:6]) + ready(state[6:12]) + ready(state[12:18])
    count = len(mine)
    shapes = [x.shape for x in state[:6]]
    vm = pl.BlockSpec(memory_space=pltpu.VMEM)
    outs = [jax.ShapeDtypeStruct(x.shape, F32) for x in state] + [jax.ShapeDtypeStruct((1, 1), F32)] * 2
    out = pl.pallas_call(
        lambda *r: adam_kernel(count, *r),
        out_shape=outs,
        in_specs=[pl.BlockSpec(memory_space=pltpu.SMEM)] + [vm] * (2 * count + 18),
        out_specs=[vm] * 20,
        scratch_shapes=[pltpu.VMEM((3200, 128), F32), pltpu.VMEM((3200, 128), F32)] + [pltpu.VMEM(s, F32) for s in shapes],
        compiler_params=params(), name="adam",
    )(where, *mine, *other, *state)
    back = lambda group: [group[0].T, group[1], group[2], swap(group[3]), group[4], group[5]]
    return out[18].reshape(()), out[19].reshape(()), back(out[0:6]) + back(out[6:12]) + back(out[12:18])


AXES = ("dp", "rep")


def levels(size):
    found, stride = [], 1
    while size > 1:
        n = size if size <= 8 else 4
        found.append((stride, n))
        stride, size = stride * n, size // n
    return found


def peers(stride, k):
    dp, rep = lax.axis_size("dp"), lax.axis_size("rep")
    return [(d * rep + r, (d ^ (k * stride)) * rep + r) for d in range(dp) for r in range(rep)]


def twin():
    dp, rep = lax.axis_size("dp"), lax.axis_size("rep")
    return [(d * rep + r, d * rep + (rep - 1 - r)) for d in range(dp) for r in range(rep)]


def send(x, pairs):
    return lax.ppermute(x, AXES, pairs)


def tree(items, join):
    while len(items) > 1:
        items = [join(items[i], items[i + 1]) for i in range(0, len(items), 2)]
    return items[0]


def place(d, stride, n):
    return lax.rem(lax.div(d, stride), n)


def reduce_level(x, d, stride, n):
    c = place(d, stride, n)
    rows = x.shape[0] // n
    piece = lambda k: lax.dynamic_slice_in_dim(x, (c ^ k) * rows, rows, 0)
    got = [send(piece(k), peers(stride, k)) for k in range(1, n)]
    return tree([piece(0)] + got, jnp.add)


def gather_level(x, d, stride, n):
    return [x] + [send(x, peers(stride, k)) for k in range(1, n)]


def in_order(pieces, d, stride, n):
    c = place(d, stride, n)
    lines = []
    for i in range(n):
        line = pieces[i]
        for k in range(n):
            if k != i:
                line = jnp.where((c ^ k) == i, pieces[k], line)
        lines.append(line)
    return jnp.concatenate(lines, axis=0)


def spread_latest(x, d):
    nodes = lax.broadcasted_iota(I32, x.shape, 0) < x.shape[0] - 1
    join = lambda p, q: jnp.where(nodes, jnp.maximum(p, q), p + q)
    x = join(x, send(x, twin()))
    for stride, n in levels(lax.axis_size("dp")):
        x = tree(gather_level(x, d, stride, n), join)
    return x


def sum_grads(mine, theirs, d):
    steps = levels(lax.axis_size("dp"))
    x = mine + send(theirs, twin())
    for stride, n in steps:
        x = reduce_level(x, d, stride, n)
    for stride, n in reversed(steps[1:]):
        x = in_order(gather_level(x, d, stride, n), d, stride, n)
    mine = gather_level(x, d, *steps[0])
    return mine, [send(x, twin()) for x in mine]


def body(source, target, neighbours, neighbour_ticks, event_ticks, event_types, labels, edge_feats, weights, memory,
         node_ticks, gru_in, gru_hid, keys_values, tall_stack, squares, vectors, *moments):
    events = event_ticks.shape[0]
    nodes = memory.shape[0]
    devices = lax.axis_size("dp") * lax.axis_size("rep")
    d, core = lax.axis_index("dp"), lax.axis_index("rep")
    scale = TIME_RATE / (events * devices)
    tiles = events // 128
    order = lambda x: jnp.transpose(x, (2, 1, 0)).reshape(NBR, 2, tiles, 128).transpose(0, 2, 1, 3).reshape(NBR, 2 * events)
    pair = lambda x, y: jnp.stack([x.reshape(tiles, 128), y.reshape(tiles, 128)], axis=1).reshape(-1)
    end_nodes = pair(source, target)
    near_ids = order(neighbours).reshape(-1)
    near_ticks = order(neighbour_ticks)
    row = lambda x: x.reshape(1, events)
    mem_t = memory.T
    local = jnp.full((nodes,), -1, I32).at[end_nodes].max(pair(2 * event_ticks, 2 * event_ticks + 1))
    spread = jnp.concatenate([local.astype(F32).reshape(-1, 128), jnp.full((1, 128), jnp.sum(weights), F32)], axis=0)
    spread = spread_latest(spread, d)
    latest = spread[:-1].reshape(-1).astype(I32)
    weight_sum = spread[-1, 0]
    w = prep(gru_in, gru_hid, keys_values, tall_stack, squares, vectors)
    wg, wgc, wh = w[0], w[1], w[2]
    vb = w[-1]
    table, own = build_table(end_nodes, mem_t, node_ticks)
    msg, keep, ren, ren_rows, gap_own = gru(scale, own, row(event_ticks), edge_feats.T, row(event_types), wg, wh, vb)
    cap = room(nodes, devices)
    packed = pack(cap, end_nodes, event_ticks, latest, ren_rows)
    gathered = lax.all_gather(packed[0], AXES)
    near = gather_near(near_ids, table)
    mine, theirs = main(scale, near, near_ticks, row(event_ticks), msg, keep, ren, gap_own, row(labels), row(weights),
                        jnp.full((1, 128), weight_sum, F32), core.reshape(1), [wgc] + list(w[3:]))
    mine, other = sum_grads(mine, theirs, d)
    where = jnp.stack([core, place(d, *levels(lax.axis_size("dp"))[0])])
    grad_norm, loss_sum, news = adam(
        where, mine, other, (gru_in, gru_hid, keys_values, tall_stack, squares, vectors) + moments)
    new_mem, more = merge(cap, gathered, mem_t)

    def again(carry):
        r, _, mem_now = carry
        mem_now, more = merge(cap, lax.all_gather(lax.dynamic_index_in_dim(packed, r, 0, False), AXES), mem_now)
        return r + 1, more & (r + 1 < packed.shape[0]), mem_now

    if packed.shape[0] > 1:
        new_mem = lax.while_loop(lambda c: c[1], again, (jnp.int32(1), more, new_mem))[2]
    return (grad_norm, loss_sum, weight_sum, new_mem.T, *news)


def solution(mesh):
    split = P(AXES)
    placed = (split, split, P(AXES, None, None), P(AXES, None, None), split, split, split, P(AXES, None), split)
    return jax.shard_map(body, mesh=mesh, in_specs=placed + (P(),) * 20, out_specs=(P(),) * 22, check_vma=False)
```

```python
import math

import jax
import jax.numpy as jnp
from jax import lax
from jax.experimental import pallas as pl
from jax.experimental.pallas import tpu as pltpu
from jax.sharding import PartitionSpec as P

F32 = jnp.float32
BF = jnp.bfloat16
I32 = jnp.int32
NBR = 10
MEM = 172
PAD = 176
HALF = 86
HPAD = 88
STEP = 10
LEARN_RATE = 0.03
VECTOR_RATE = 0.3
BETA_ONE = 0.9
BETA_TWO = 0.999
ADAM_EPS = 1e-08
DECAY = 0.01
CLIP_AT = 0.005
TIME_RATE = 64.0
NORM_EPS = 1e-06
VMEM_CAP = 58 * 2**20


def params(limit=VMEM_CAP):
    return pltpu.CompilerParams(vmem_limit_bytes=limit)


def cost(us):
    return pl.CostEstimate(flops=int(us * 1e9), bytes_accessed=int(us * 3e6), transcendentals=0)


def nn(a, b):
    return lax.dot_general(a, b, (((1,), (0,)), ((), ())), preferred_element_type=F32)


def nt(a, b):
    return lax.dot_general(a, b, (((1,), (1,)), ((), ())), preferred_element_type=F32)


def zeros(rows, cols):
    return jnp.zeros((rows, cols), F32)


def rows_to(x, total):
    return jnp.concatenate([x, zeros(total - x.shape[0], x.shape[1])], axis=0)


def cols_to(x, total):
    return jnp.concatenate([x, zeros(x.shape[0], total - x.shape[1])], axis=1)


def split_rows(x):
    gap = zeros(HPAD - HALF, x.shape[1])
    return jnp.concatenate([x[:HALF], gap, x[HALF:], gap], axis=0)


def eye(n):
    return (lax.broadcasted_iota(I32, (n, n), 0) == lax.broadcasted_iota(I32, (n, n), 1)).astype(BF)


def turned(x):
    return nt(eye(x.shape[1]), x.astype(BF))


def prep_kernel(gin, ghid, kv, tall, sq, vec,
                wg, wgc, wh, kvm, kvct, kvc, t0t, t0, t1t, t1, t2t, t2, s0t, s0, s1t, s1, vb):
    full = gin[...]
    for gate in range(3):
        rows = full[gate * MEM : (gate + 1) * MEM]
        parts = [cols_to(rows[:, q * MEM : (q + 1) * MEM], PAD) for q in range(4)]
        wide = rows_to(jnp.concatenate(parts, axis=1), PAD)
        wg[pl.ds(gate * PAD, PAD), :] = wide.astype(BF)
        code = cols_to(rows_to(rows[:, 2 * MEM : 3 * MEM], PAD), 256)
        wgc[:, gate * PAD : (gate + 1) * PAD] = turned(code)[:PAD].astype(BF)
    hid = ghid[...]
    for gate in range(3):
        part = cols_to(rows_to(hid[:, gate * MEM : (gate + 1) * MEM], PAD), 256)
        wh[pl.ds(gate * PAD, PAD), :] = turned(part)[:PAD].astype(BF)
    pairs = kv[...]
    both = turned(cols_to(pairs, 384))
    halves = jnp.concatenate([split_rows(both[:MEM]), split_rows(both[MEM : 2 * MEM])], axis=0)
    kvm[...] = cols_to(halves[:, :MEM], 256).astype(BF)
    code_rows = cols_to(halves[:, MEM:], 256)
    kvct[...] = code_rows[:, :PAD].astype(BF)
    kvc[...] = turned(code_rows)[:PAD].astype(BF)
    query = tall[0]
    query_t = cols_to(split_rows(query[:, :MEM]), 256)
    t0t[...] = query_t[:, :PAD].astype(BF)
    t0[...] = turned(query_t)[:PAD].astype(BF)
    for src, fwd, back in ((tall[1], t1t, t1), (tall[2], t2t, t2)):
        wide = rows_to(jnp.concatenate([cols_to(src[:, :MEM], PAD), cols_to(src[:, MEM:], PAD)], axis=1), PAD)
        fwd[...] = wide.astype(BF)
        back[...] = turned(cols_to(wide, 384))[: 2 * PAD].astype(BF)
    first = cols_to(split_rows(sq[:, 0, :]), 256)
    s0[...] = first[:, :PAD].astype(BF)
    s0t[...] = turned(first)[:PAD].astype(BF)
    second = cols_to(rows_to(sq[:, 1, :], PAD), 256)
    s1[...] = second[:, :PAD].astype(BF)
    s1t[...] = turned(second)[:PAD].astype(BF)
    cols = jnp.transpose(cols_to(rows_to(vec[...], 128), 256))
    phase_low = jnp.cos(cols[:PAD, 1:2]).astype(BF).astype(F32)
    row_id = lax.broadcasted_iota(I32, (PAD, 128), 0)
    wide_phase = jnp.where(row_id < MEM, jnp.broadcast_to(phase_low, (PAD, 128)), 0.0).astype(BF)
    steady = nn(cols_to(split_rows(query[:, MEM:]), PAD).astype(BF), wide_phase)
    for i in range(15):
        column = cols[:, i : i + 1]
        if i in (8, 9):
            column = split_rows(column[:MEM])
        wide = jnp.broadcast_to(column[:PAD], (PAD, 128))
        vb[i] = wide + steady if i == 8 else (wide * (0.5 / math.pi) if i < 2 else wide)


def prep(gin, ghid, kv, tall, sq, vec):
    bf = lambda *s: jax.ShapeDtypeStruct(s, BF)
    outs = [bf(528, 704), bf(176, 528), bf(528, 176), bf(352, 256), bf(352, 176), bf(176, 352),
            bf(176, 176), bf(176, 176), bf(176, 352), bf(352, 176), bf(176, 352), bf(352, 176),
            bf(176, 176), bf(176, 176), bf(176, 176), bf(176, 176), jax.ShapeDtypeStruct((15, PAD, 128), F32)]
    return pl.pallas_call(
        prep_kernel, out_shape=outs, compiler_params=params(), name="prep", cost_estimate=cost(6),
    )(gin.T, ghid, kv, jnp.transpose(tall, (0, 2, 1)), jnp.transpose(sq, (1, 0, 2)), vec)


def first_kernel(source, target, ticks, weights, out):
    tiles = source.shape[0]
    heights = out.shape[0] - 1
    nodes, orders = [], []
    for b in range(tiles):
        nodes += [source[b : b + 1, :], target[b : b + 1, :]]
        orders += [2 * ticks[b : b + 1, :], 2 * ticks[b : b + 1, :] + 1]
    count = 2 * tiles
    stack = jnp.concatenate([x.astype(F32) for x in nodes + orders], axis=0)
    cols = jnp.transpose(rows_to(stack, 128))
    lane = lax.broadcasted_iota(I32, (128, 128), 1)
    line = lax.broadcasted_iota(I32, (heights, 128), 0)
    total = zeros(heights, 384)
    for c in range(count):
        node = jnp.broadcast_to(cols[:, c : c + 1], (128, 128)).astype(I32)
        order = jnp.broadcast_to(cols[:, count + c : count + c + 1], (128, 128)).astype(I32)
        beaten = zeros(128, 128)
        for e in range(count):
            beaten = jnp.where((node == nodes[e]) & (orders[e] > order), 1.0, beaten)
        beaten = jnp.max(beaten, axis=1, keepdims=True)
        value = jnp.where(beaten > 0.0, 0, order + 1)
        here = (node & 127) == lane
        pick = lambda v: jnp.where(here, v, 0).astype(F32).astype(BF)
        right = jnp.concatenate([pick(value & 127), pick((value >> 7) & 127), pick(value >> 14)], axis=1)
        left = (jnp.broadcast_to(nodes[c] >> 7, (heights, 128)) == line).astype(BF)
        total = total + nn(left, right)
    out[0:heights, :] = total[:, :128] + 128.0 * total[:, 128:256] + 16384.0 * total[:, 256:] - 1.0
    out[heights : heights + 1, :] = jnp.broadcast_to(jnp.sum(weights[...], keepdims=True), (1, 128))


def first_latest(nodes, source, target, ticks, weights):
    return pl.pallas_call(
        first_kernel, out_shape=jax.ShapeDtypeStruct((nodes // 128 + 1, 128), F32),
        compiler_params=params(), name="latest", cost_estimate=cost(2),
    )(source, target, ticks, weights)


def fetch_kernel(steps, chunk, source, target, near_ids, mem, ticks, own, near, wide, left, right):
    step = pl.program_id(0)
    cols = mem.shape[1]

    @pl.when(step == 0)
    def _():
        wide[...] = jnp.zeros_like(wide)

    @pl.when(step < steps)
    def _():
        base = pl.multiple_of(step * cols, cols)
        wide[0:MEM, :] = mem[...].astype(BF).astype(F32)
        tick = ticks[...]
        for at, part in ((PAD, tick & 127), (PAD + 1, (tick >> 7) & 127), (PAD + 2, tick >> 14)):
            wide[at : at + 1, :] = part.astype(F32)
        unit = eye(256)
        for c in range(cols // 256):
            rows = nt(unit, wide[:, 256 * c : 256 * c + 256].astype(BF))
            left[pl.ds(base + 256 * c, 256), :] = rows[:, :128]
            right[pl.ds(base + 256 * c, 256), :] = rows[:, 128:]

    def move(out, at, ids):
        for h, table in enumerate((left, right)):
            rows = jnp.concatenate([table[pl.ds(i, 1), :] for i in ids], axis=0)
            out[pl.ds(at, 16), 128 * h : 128 * h + 128] = rows.astype(BF)

    @pl.when(step == steps)
    def _():
        def group(b, carry):
            for role, ids in enumerate((source, target)):
                def some(g, carry):
                    for v in range(2):
                        e = g * 32 + v * 16
                        at = pl.multiple_of(b * 256 + role * 128 + e, 16)
                        move(own, at, [ids[b * 128 + e + u] for u in range(16)])
                    return carry

                lax.fori_loop(0, 4, some, 0)
            return carry

        lax.fori_loop(0, own.shape[0] // 256, group, 0)

    @pl.when(step > steps)
    def _():
        base = (step - steps - 1) * chunk

        def group(g, carry):
            for v in range(4):
                at = pl.multiple_of(g * 64 + v * 16, 16)
                move(near, at, [near_ids[base + at + u] for u in range(16)])
            return carry

        lax.fori_loop(0, chunk // 64, group, 0)


def fetch(source, target, near_ids, mem_t, ticks):
    nodes = mem_t.shape[1]
    ends, nears = 2 * source.shape[0], near_ids.shape[0]
    cols, chunk = 4096, 5120
    steps = nodes // cols
    smem = pl.BlockSpec(memory_space=pltpu.SMEM)
    part = lambda i: (0, jnp.minimum(i, steps - 1))
    return pl.pallas_call(
        lambda *r: fetch_kernel(steps, chunk, *r),
        out_shape=[jax.ShapeDtypeStruct((ends, 256), BF), jax.ShapeDtypeStruct((nears, 256), BF)],
        grid=(steps + 1 + nears // chunk,),
        in_specs=[smem, smem, smem, pl.BlockSpec((MEM, cols), part), pl.BlockSpec((1, cols), part)],
        out_specs=[pl.BlockSpec((ends, 256), lambda i: (0, 0)),
                   pl.BlockSpec((chunk, 256), lambda i: (jnp.maximum(i - steps - 1, 0), 0))],
        scratch_shapes=[pltpu.VMEM((256, cols), F32), pltpu.VMEM((nodes, 128), F32), pltpu.VMEM((nodes, 128), F32)],
        compiler_params=params(), name="fetch", cost_estimate=cost(18),
    )(source, target, near_ids, mem_t, ticks.reshape(1, nodes))


ROUND = 12582912.0
SIN = (6.283185005187988, -41.34165573120117, 81.60100555419922, -76.5497817993164, 39.536705017089844)
COS = (0.9999999403953552, -19.739171981811523, 64.9345932006836, -85.2403335571289, 56.24237823486328)


def cos_sin(turns):
    e = turns - ((turns + ROUND) - ROUND)
    w = 0.25 - jnp.abs(e)
    z = w * w
    c = w * (SIN[0] + z * (SIN[1] + z * (SIN[2] + z * (SIN[3] + z * SIN[4]))))
    s = COS[0] + z * (COS[1] + z * (COS[2] + z * (COS[3] + z * COS[4])))
    return c, jnp.where(e > 0.0, -s, s)


def sigmoid(x):
    return 0.5 * jnp.tanh(0.5 * x) + 0.5


BLOCK = 512
TILES = BLOCK // 256


def across(x):
    return jnp.concatenate([x] * (2 * TILES), axis=1)


def chunks(x, width=128):
    return [x[:, at : at + width] for at in range(0, x.shape[1], width)]


def both(x):
    return jnp.concatenate([c for c in chunks(x) for _ in range(2)], axis=1)


def mix(x, y):
    return jnp.concatenate([c for pair in zip(chunks(x), chunks(y)) for c in pair], axis=1)


def sources_of(x):
    return jnp.concatenate(chunks(x)[0::2], axis=1)


def targets_of(x):
    return jnp.concatenate(chunks(x)[1::2], axis=1)


def wide_rows(x, rows):
    return jnp.broadcast_to(x, (rows, x.shape[1]))


def gru_kernel(scale, cap, rounds, sources, targets, ticks_at, latest, own, source, target, ticks, edge, types, wg, wh, vb,
               msg, keep, ren, gap_out, packed, left, right, first, second):
    step = pl.program_id(0)
    own_t = nt(eye(256), own[...])
    seen = own_t[PAD : PAD + 1] + 128.0 * own_t[PAD + 1 : PAD + 2] + 16384.0 * own_t[PAD + 2 : PAD + 3]
    gap = (both(ticks[...].astype(F32)) - seen) * scale
    row_id = lax.broadcasted_iota(I32, (PAD, BLOCK), 0)
    own_x = jnp.where(row_id < MEM, own_t[:PAD], 0.0)
    msg[0:PAD, :] = own_x.astype(BF)
    msg[PAD : 2 * PAD, :] = mix(targets_of(own_x), sources_of(own_x)).astype(BF)
    edges = rows_to(edge[...].astype(F32) * types[...].astype(F32), PAD)
    msg[3 * PAD : 4 * PAD, :] = both(edges).astype(BF)
    gap_out[...] = wide_rows(gap, 8)
    gap16 = wide_rows(gap, 16)
    for st in range(PAD // 16):
        at = 16 * st
        for m in range(TILES):
            q = slice(256 * m, 256 * m + 256)
            rate, phase = vb[0, at : at + 16, :], vb[1, at : at + 16, :]
            x = jnp.concatenate([rate, rate], axis=1) * gap16[:, q] + jnp.concatenate([phase, phase], axis=1)
            c, s = cos_sin(x)
            msg[2 * PAD + at : 2 * PAD + at + 16, q] = c.astype(BF)
            keep[4, at : at + 16, q] = s
    gates = nn(wg[...], msg[...])
    hidden = nn(wh[...], msg[0:PAD, :])
    for st in range(PAD // 8):
        at = 8 * st
        o = own_x[at : at + 8]
        pre = [gates[g * PAD + at : g * PAD + at + 8] + across(vb[2 + g, at : at + 8, :]) for g in range(3)]
        hid = [hidden[g * PAD + at : g * PAD + at + 8] + across(vb[5 + g, at : at + 8, :]) for g in range(3)]
        u = sigmoid(pre[0] + hid[0])
        r = sigmoid(pre[1] + hid[1])
        n = jnp.tanh(pre[2] + r * hid[2])
        keep[0, at : at + 8, :] = u
        keep[1, at : at + 8, :] = r
        keep[2, at : at + 8, :] = n
        keep[3, at : at + 8, :] = hid[2]
        ren[at : at + 8, :] = (1.0 - u) * n + u * o
    numbers = mix(source[...], target[...]).astype(F32)
    low = jnp.concatenate([ren[128:MEM, :], numbers, zeros(255 - MEM, BLOCK)], axis=0)
    for role in range(2 * TILES):
        at = pl.multiple_of(step * BLOCK + 128 * role, 128)
        left[pl.ds(at, 128), :] = jnp.transpose(ren[0:128, 128 * role : 128 * role + 128])
        right[pl.ds(at, 128), :] = jnp.transpose(low[:, 128 * role : 128 * role + 128])

    @pl.when(step == pl.num_programs(0) - 1)
    def _():
        pack_rows(cap, rounds, sources, targets, ticks_at, latest, left, right, packed, first, second)


def pack_rows(cap, rounds, sources, targets, ticks, latest, left, right, out, first, second):
    second[...] = jnp.full_like(second, -1.0)

    def chunk(b, count):
        for role, ids in enumerate((sources, targets)):
            def some(g, count):
                for v in range(32):
                    e = b * 128 + g * 32 + v
                    i = b * 256 + role * 128 + g * 32 + v
                    won = latest[ids[e]] == 2 * ticks[e] + role
                    first[pl.ds(count, 1), :] = left[pl.ds(i, 1), :]
                    second[pl.ds(count, 1), :] = right[pl.ds(i, 1), :]
                    count = count + won.astype(I32)
                return count

            count = lax.fori_loop(0, 4, some, count)
        return count

    count = lax.fori_loop(0, sources.shape[0] // 128, chunk, jnp.int32(0))
    second[pl.ds(count, 1), :] = jnp.full((1, 128), -1.0, F32)
    tail = cap // 2
    lane = lax.broadcasted_iota(I32, (1, 128), 1)
    for r in range(rounds):
        at = r * cap
        out[r, 0:cap, :] = first[at : at + cap, :]
        out[r, cap : cap + tail, :] = jnp.concatenate(
            [second[at : at + tail, 0:64], second[at + tail : at + cap, 0:64]], axis=1)
        lines = []
        for q in range(-(-cap // 128)):
            numbers = jnp.transpose(second[at + 128 * q : at + 128 * q + 128, :])[MEM - 128 : MEM - 127]
            lines.append(jnp.where(lane + 128 * q < cap, numbers, -1.0))
        out[r, cap + tail :, :] = jnp.concatenate(lines + [zeros(1, 128)] * (8 - len(lines)), axis=0)


def gru(scale, cap, sources, targets, ticks, latest, own, edge_t, types, wg, wh, vb):
    ends = own.shape[0]
    blocks = ends // BLOCK
    rounds = ends // cap + 1
    spare = rounds * cap + 128
    whole = lambda a: pl.BlockSpec(a.shape, lambda i: (0,) * len(a.shape))
    lanes = lambda: pl.BlockSpec((1, BLOCK // 2), lambda i: (0, i))
    smem = pl.BlockSpec(memory_space=pltpu.SMEM)
    row = lambda x: x.reshape(1, -1)
    packed = jax.ShapeDtypeStruct((rounds, cap + cap // 2 + 8, 128), F32)
    return pl.pallas_call(
        lambda *r: gru_kernel(scale, cap, rounds, *r),
        out_shape=[jax.ShapeDtypeStruct((4 * PAD, ends), BF), jax.ShapeDtypeStruct((5, PAD, ends), F32),
                   jax.ShapeDtypeStruct((PAD, ends), F32), jax.ShapeDtypeStruct((8, ends), F32), packed],
        grid=(blocks,),
        in_specs=[smem] * 4 + [pl.BlockSpec((BLOCK, 256), lambda i: (i, 0)), lanes(), lanes(), lanes(),
                  pl.BlockSpec((MEM, BLOCK // 2), lambda i: (0, i)), lanes(), whole(wg), whole(wh), whole(vb)],
        out_specs=[pl.BlockSpec((4 * PAD, BLOCK), lambda i: (0, i)), pl.BlockSpec((5, PAD, BLOCK), lambda i: (0, 0, i)),
                   pl.BlockSpec((PAD, BLOCK), lambda i: (0, i)), pl.BlockSpec((8, BLOCK), lambda i: (0, i)), whole(packed)],
        scratch_shapes=[pltpu.VMEM((ends, 128), F32), pltpu.VMEM((ends, 128), F32),
                        pltpu.VMEM((spare, 128), F32), pltpu.VMEM((spare, 128), F32)],
        compiler_params=params(), name="gru", cost_estimate=cost(10),
    )(sources, targets, ticks, latest, own, row(sources), row(targets), row(ticks), edge_t, types, wg, wh, vb)


UNROLL = 5
GELU_C = math.sqrt(2.0 / math.pi)


def gelu_parts(x):
    sq = x * x
    t = jnp.tanh(GELU_C * (x + 0.044715 * (sq * x)))
    half = 0.5 * (1.0 + t)
    slope = half + (0.5 * x) * (1.0 - t * t) * (GELU_C + (GELU_C * 3.0 * 0.044715) * sq)
    return x * half, slope


def fold(x):
    total, *others = chunks(x)
    for other in others:
        total = total + other
    return total


def main_kernel(scale, core, near, gaps_t, ticks, msg, keep, ren, gap_own, labels, weights, total,
                wgc, kvm, kvct, kvc, t0t, t0, t1t, t1, t2t, t2, s0t, s0, s1t, s1, vb,
                mine, theirs,
                loss, pair, code, dcode, soft, back, mean, d_query_at, grads, g_in, g_kv, g_one, g_dec, g_qo, g_th, vacc):
    step = pl.program_id(0)
    inv_size = HALF ** -0.5

    @pl.when(step == 0)
    def _():
        for ref in (g_in, g_kv, g_one, g_dec, g_qo, g_th, vacc, loss):
            ref[...] = jnp.zeros_like(ref)

    tick2 = both(ticks[...].astype(F32))
    renewed = ren[...]
    ren_low = renewed.astype(BF)
    queries = nn(t0t[...], ren_low) + across(vb[8])
    def each(one):
        def some(g, carry):
            for v in range(UNROLL):
                one(g * UNROLL + v)
            return carry

        lax.fori_loop(0, NBR // UNROLL, some, 0)

    def look(j):
        gap16 = wide_rows((tick2 - gaps_t[pl.ds(j, 1), :].astype(F32)) * scale, 16)
        for st in range(PAD // 16):
            at = 16 * st
            for m in range(TILES):
                q = slice(256 * m, 256 * m + 256)
                rate, phase = vb[0, at : at + 16, :], vb[1, at : at + 16, :]
                x = jnp.concatenate([rate, rate], axis=1) * gap16[:, q] + jnp.concatenate([phase, phase], axis=1)
                c, s = cos_sin(x)
                code[j, at : at + 16, q] = c.astype(BF)
                dcode[j, at : at + 16, q] = s
        pair[j] = nt(kvm[...], near[j]) + nn(kvct[...], code[j])
        for h in range(2):
            acc = zeros(8, BLOCK)
            for st in range(HPAD // 8):
                at = HPAD * h + 8 * st
                acc = acc + pair[j, at : at + 8, :] * queries[at : at + 8]
            soft[2 * j + h] = wide_rows(jnp.sum(acc, axis=0, keepdims=True) * inv_size, 8)

    each(look)
    for h in range(2):
        top = soft[h]
        for j in range(1, NBR):
            top = jnp.maximum(top, soft[2 * j + h])
        norm = zeros(8, BLOCK)
        for j in range(NBR):
            e = jnp.exp(soft[2 * j + h] - top)
            soft[2 * j + h] = e
            norm = norm + e
        inv = 1.0 / norm
        for j in range(NBR):
            soft[2 * j + h] = soft[2 * j + h] * inv
    att = []
    for st in range(PAD // 8):
        at = 8 * st
        h = 0 if at < HPAD else 1
        acc = across(vb[9, at : at + 8, :])
        for j in range(NBR):
            acc = acc + soft[2 * j + h] * pair[j, PAD + at : PAD + at + 8, :]
        att.append(acc)
    att_low = jnp.concatenate(att, axis=0).astype(BF)
    projected = nn(s0t[...], att_low) + across(vb[10])
    mlp_in = jnp.concatenate([projected.astype(BF), ren_low], axis=0)
    inner = nn(t1t[...], mlp_in) + across(vb[11])
    act, act_slope = gelu_parts(inner)
    act_low = act.astype(BF)
    emb_low = (nn(s1t[...], act_low) + across(vb[12])).astype(BF)
    dec_in = jnp.concatenate([sources_of(emb_low), targets_of(emb_low)], axis=0)
    out_row = jnp.concatenate([vb[14]] * TILES, axis=1)
    dec_pre = nn(t2t[...], dec_in) + jnp.concatenate([vb[13]] * TILES, axis=1)
    dec_act, dec_slope = gelu_parts(dec_pre)
    logit = jnp.sum(dec_act * out_row, axis=0, keepdims=True)
    label = labels[...].astype(F32)
    tail = jnp.exp(-jnp.abs(logit))
    plus = jnp.maximum(logit, 0.0) + jnp.log1p(tail)
    loss[...] += fold(weights[...] * (plus - label * logit))
    d_logit = weights[...] / total[:, 0:1] * (sigmoid(logit) - label)
    d_out = d_logit * dec_act
    d_dec = (d_logit * out_row) * dec_slope
    d_dec_low = d_dec.astype(BF)
    g_dec[...] += nt(d_dec_low, dec_in)
    d_dec_in = nn(t2[...], d_dec_low)
    d_emb = mix(d_dec_in[:PAD], d_dec_in[PAD:])
    d_emb_low = d_emb.astype(BF)
    g_th[:, 0:256] += jnp.concatenate([nt(act_low, d_emb_low), zeros(PAD, 256 - PAD)], axis=1)
    d_inner = nn(s1[...], d_emb_low) * act_slope
    d_inner_low = d_inner.astype(BF)
    g_one[...] += nt(d_inner_low, mlp_in)
    d_mlp = nn(t1[...], d_inner_low)
    d_proj = d_mlp[:PAD]
    d_proj_low = d_proj.astype(BF)
    g_qo[:, 256:512] += jnp.concatenate([nt(att_low, d_proj_low), zeros(PAD, 256 - PAD)], axis=1)
    d_att = nn(s0[...], d_proj_low)
    d_query_at[...] = jnp.zeros_like(d_query_at)
    mean[...] = jnp.zeros_like(mean)

    def weigh(j):
        for h in range(2):
            acc = zeros(8, BLOCK)
            for st in range(HPAD // 8):
                at = HPAD * h + 8 * st
                acc = acc + pair[j, PAD + at : PAD + at + 8, :] * d_att[at : at + 8]
            wide = wide_rows(jnp.sum(acc, axis=0, keepdims=True), 8)
            back[2 * j + h] = wide
            mean[h] += wide * soft[2 * j + h]

    def learn(j):
        share = [soft[2 * j + h] for h in range(2)]
        slope = [(share[h] * inv_size) * (back[2 * j + h] - mean[h]) for h in range(2)]
        for st in range(PAD // 8):
            at = 8 * st
            d_query_at[at : at + 8, :] += slope[at >= HPAD] * pair[j, at : at + 8, :]
        for st in range(2 * PAD // 16):
            parts = []
            for half in range(2):
                at = 16 * st + 8 * half
                if at < PAD:
                    parts.append(slope[at >= HPAD] * queries[at : at + 8])
                else:
                    parts.append(share[at - PAD >= HPAD] * d_att[at - PAD : at - PAD + 8])
            grads[j, 16 * st : 16 * st + 16, :] = jnp.concatenate(parts, axis=0).astype(BF)
        d_code = nn(kvc[...], grads[j])
        gap8 = wide_rows((tick2 - gaps_t[pl.ds(j, 1), :].astype(F32)) * scale, 8)
        for st in range(PAD // 8):
            at = 8 * st
            d_arg = d_code[at : at + 8] * dcode[j, at : at + 8, :]
            vacc[0, at : at + 8, :] += fold(d_arg * gap8)
            vacc[1, at : at + 8, :] += fold(d_arg)
        g_kv[:, 0:256] += nn(grads[j], near[j])
        g_kv[:, 256 : 256 + PAD] += nt(grads[j], code[j])

    each(weigh)
    each(learn)
    d_query = d_query_at[...]
    d_q_low = d_query.astype(BF)
    g_qo[:, 0:256] += jnp.concatenate([nt(d_q_low, ren_low), zeros(PAD, 256 - PAD)], axis=1)
    d_ren = d_mlp[PAD:] + nn(t0[...], d_q_low)
    own_x = msg[0:PAD, :].astype(F32)
    u, r, n, hn = keep[0], keep[1], keep[2], keep[3]
    d_u = d_ren * (own_x - n) * (u * (1.0 - u))
    d_n = d_ren * (1.0 - u) * (1.0 - n * n)
    d_r = d_n * hn * (r * (1.0 - r))
    d_h = d_n * r
    gates = jnp.concatenate([d_u, d_r, d_n], axis=0).astype(BF)
    g_in[...] += nt(gates, msg[...])
    g_th[:, 256:512] += jnp.concatenate([nt(msg[0:PAD, :], d_h.astype(BF)), zeros(PAD, 256 - PAD)], axis=1)
    d_arg = nn(wgc[...], gates) * keep[4]
    vacc[0] += fold(d_arg * gap_own[0:1, :])
    vacc[1] += fold(d_arg)
    for i, item in ((2, d_u), (3, d_r), (4, d_n), (7, d_h), (8, d_query), (9, d_att), (10, d_proj), (11, d_inner),
                    (12, d_emb), (15, d_q_low.astype(F32))):
        vacc[i] += fold(item)
    vacc[13] += fold(d_dec)
    vacc[14] += fold(d_out)

    def finish(ga, gb):
        wide = cols_to(g_in[...], 768)
        for c in range(6):
            gb[528 * c : 528 * c + 528, :] = wide[:, 128 * c : 128 * c + 128]
        lane = lax.broadcasted_iota(I32, (PAD, 128), 1)
        vecs = zeros(PAD, 128)
        for i in range(16):
            column = jnp.sum(vacc[i], axis=1, keepdims=True)
            vecs = jnp.where(lane == i, column, vecs)
        flat = jnp.transpose(jnp.concatenate([vecs, zeros(256 - PAD, 128)], axis=0))
        gb[3168:3184, :] = flat[0:16, 0:128]
        gb[3184:3200, :] = flat[0:16, 128:256]
        at = 0
        for left, right, rows in ((g_kv[:, 0:PAD], g_kv[:, 256 : 256 + PAD], 352),
                                  (g_one[:, 0:PAD], g_one[:, PAD : 2 * PAD], 176),
                                  (g_dec[:, 0:PAD], g_dec[:, PAD : 2 * PAD], 176),
                                  (g_qo[:, 0:PAD], g_qo[:, 256 : 256 + PAD], 176),
                                  (g_th[:, 0:PAD], g_th[:, 256 : 256 + PAD], 176)):
            wide = jnp.concatenate([left, right, zeros(rows, 32)], axis=1)
            for c in range(3):
                ga[at : at + rows, :] = wide[:, 128 * c : 128 * c + 128]
                at += rows
        ga[3168:3200, :] = rows_to(loss[...], 32)

    @pl.when((step == pl.num_programs(0) - 1) & (core[0] == 0))
    def _():
        finish(mine, theirs)

    @pl.when((step == pl.num_programs(0) - 1) & (core[0] != 0))
    def _():
        finish(theirs, mine)


def main(scale, near, near_ticks, ticks, msg, keep, ren, gap_own, labels, weights, total, core, w):
    ends = ren.shape[1]
    blocks = ends // BLOCK
    whole = lambda a: pl.BlockSpec(a.shape, lambda i: (0,) * len(a.shape))
    lanes = lambda: pl.BlockSpec((1, BLOCK // 2), lambda i: (0, i))
    return pl.pallas_call(
        lambda *r: main_kernel(scale, *r),
        out_shape=[jax.ShapeDtypeStruct((3200, 128), F32), jax.ShapeDtypeStruct((3200, 128), F32)],
        grid=(blocks,),
        in_specs=[pl.BlockSpec(memory_space=pltpu.SMEM), pl.BlockSpec((NBR, BLOCK, 256), lambda i: (0, i, 0)), pl.BlockSpec((NBR, BLOCK), lambda i: (0, i)), lanes(),
                  pl.BlockSpec((4 * PAD, BLOCK), lambda i: (0, i)), pl.BlockSpec((5, PAD, BLOCK), lambda i: (0, 0, i)),
                  pl.BlockSpec((PAD, BLOCK), lambda i: (0, i)), pl.BlockSpec((8, BLOCK), lambda i: (0, i)), lanes(), lanes(),
                  pl.BlockSpec((1, 128), lambda i: (0, 0))] + [whole(a) for a in w],
        out_specs=[pl.BlockSpec((3200, 128), lambda i: (0, 0)), pl.BlockSpec((3200, 128), lambda i: (0, 0))],
        scratch_shapes=[pltpu.VMEM((1, 128), F32), pltpu.VMEM((NBR, 352, BLOCK), F32), pltpu.VMEM((NBR, PAD, BLOCK), BF), pltpu.VMEM((NBR, PAD, BLOCK), F32),
                        pltpu.VMEM((20, 8, BLOCK), F32), pltpu.VMEM((20, 8, BLOCK), F32), pltpu.VMEM((2, 8, BLOCK), F32),
                        pltpu.VMEM((PAD, BLOCK), F32), pltpu.VMEM((NBR, 352, BLOCK), BF),
                        pltpu.VMEM((528, 704), F32), pltpu.VMEM((352, 512), F32), pltpu.VMEM((PAD, 352), F32),
                        pltpu.VMEM((PAD, 352), F32), pltpu.VMEM((PAD, 512), F32), pltpu.VMEM((PAD, 512), F32),
                        pltpu.VMEM((16, PAD, 128), F32)],
        compiler_params=params(), name="main", cost_estimate=cost(35),
    )(core, near.reshape(NBR, ends, 256), near_ticks, ticks, msg, keep, ren, gap_own, labels, weights, total, *w)


def room(nodes, devices):
    return -(-(nodes * 9) // (devices * 8 * 16)) * 16


def turned_exactly(x):
    high = x.astype(BF)
    rest = x - high.astype(F32)
    middle = rest.astype(BF)
    low = (rest - middle.astype(F32)).astype(BF)
    unit = eye(x.shape[1])
    return (nt(unit, high) + nt(unit, middle)) + nt(unit, low)


def merge_kernel(cap, group, steps, ids, counts, rows, mem, out, left, right, second):
    step = pl.program_id(0)
    tail = cap // 2
    width = -(-cap // 128) * 128

    @pl.when(step == 0)
    def _():
        left[...] = jnp.zeros_like(left)
        right[...] = jnp.full_like(right, -1.0)

    @pl.when(step < steps)
    def _():
        for q in range(group):
            half = rows[q, cap : cap + tail, :]
            second[q, 0:tail, :] = half
            second[q, tail:cap, :] = jnp.concatenate([half[:, 64:], half[:, :64]], axis=1)
        for q in range(group):
            base = (step * group + q) * width

            def some(g, carry):
                for v in range(16):
                    i = g * 16 + v
                    node = ids[base + i]
                    left[pl.ds(node, 1), :] = rows[q, pl.ds(i, 1), :]
                    right[pl.ds(node, 1), :] = second[q, pl.ds(i, 1), :]
                return carry

            lax.fori_loop(0, lax.div(counts[step * group + q] + 15, 16), some, 0)

    @pl.when(step >= steps)
    def _():
        cols = mem.shape[1]
        base = pl.multiple_of((step - steps) * cols, cols)
        for c in range(cols // 256):
            at = base + 256 * c
            s = slice(256 * c, 256 * c + 256)
            top = turned_exactly(left[pl.ds(at, 256), :])
            low = turned_exactly(right[pl.ds(at, 256), :])
            fresh = low[MEM - 128 : MEM - 127] >= 0.0
            out[0:128, s] = jnp.where(fresh, top, mem[0:128, s])
            out[128:MEM, s] = jnp.where(fresh, low[: MEM - 128], mem[128:MEM, s])


def merge(cap, gathered, mem_t):
    blocks, height, _ = gathered.shape
    nodes = mem_t.shape[1]
    cols, group = 4096, 8
    steps = blocks // group
    numbers = gathered[:, height - 8 : height - 8 + -(-cap // 128), :].reshape(blocks, -1)
    counts = jnp.sum((numbers >= 0.0).astype(I32), axis=1)
    ids = jnp.where(numbers >= 0.0, numbers, float(nodes)).astype(I32).reshape(-1)
    smem = pl.BlockSpec(memory_space=pltpu.SMEM)
    part = lambda i: (0, jnp.maximum(i - steps, 0))
    new = pl.pallas_call(
        lambda *r: merge_kernel(cap, group, steps, *r),
        out_shape=jax.ShapeDtypeStruct((MEM, nodes), F32),
        grid=(steps + nodes // cols,),
        in_specs=[smem, smem, pl.BlockSpec((group, height, 128), lambda i: (jnp.minimum(i, steps - 1), 0, 0)),
                  pl.BlockSpec((MEM, cols), part)],
        out_specs=pl.BlockSpec((MEM, cols), part),
        scratch_shapes=[pltpu.VMEM((nodes + 8, 128), F32), pltpu.VMEM((nodes + 8, 128), F32), pltpu.VMEM((group, cap, 128), F32)],
        compiler_params=params(), name="merge", cost_estimate=cost(20),
    )(ids, counts, gathered, mem_t)
    return new, jnp.any(counts == cap)


def move(param, one, two, grad, factor, rate, decay):
    clipped = grad * factor
    one = BETA_ONE * one + (1.0 - BETA_ONE) * clipped
    two = BETA_TWO * two + (1.0 - BETA_TWO) * clipped * clipped
    step = (one * (1.0 / (1.0 - BETA_ONE**STEP))) / (jnp.sqrt(two * (1.0 / (1.0 - BETA_TWO**STEP))) + ADAM_EPS)
    return param - rate * (step + decay * param), one, two


def unsplit(x, axis):
    take = lambda a, b: lax.slice_in_dim(x, a, b, axis=axis)
    return jnp.concatenate([take(0, HALF), take(HPAD, HPAD + HALF)], axis=axis)


def adam_kernel(parts, where, *refs):
    count = sum(n for _, n in parts)
    mine, other = refs[:count], refs[count : 2 * count]
    refs = refs[2 * count :]
    state, news, (norm_out, loss_out) = refs[:18], refs[18:36], refs[36:38]
    a, b, g_gin, g_hid, g_kv, g_tall, g_sq, g_vec = refs[38:]
    core = where[0]
    at_block = 0
    for p, (first, n) in enumerate(parts):
        height = mine[at_block].shape[0]
        for k in range(n):
            at = pl.multiple_of(first + (where[1 + p] ^ k) * height, 8)
            one, two = mine[at_block], other[at_block]
            at_block += 1

            @pl.when(core == 0)
            def _():
                a[pl.ds(at, height), :] = one[...]
                b[pl.ds(at, height), :] = two[...]

            @pl.when(core != 0)
            def _():
                b[pl.ds(at, height), :] = one[...]
                a[pl.ds(at, height), :] = two[...]

    def panels(ref, at, rows, n):
        return jnp.concatenate([ref[at + c * rows : at + (c + 1) * rows, :] for c in range(n)], axis=1)

    vec = state[5]
    tall = state[3]
    wide = panels(b, 0, 528, 6)
    gates = []
    for g in range(3):
        rows = wide[PAD * g : PAD * g + MEM]
        gates.append(jnp.concatenate([rows[:, PAD * q : PAD * q + MEM] for q in range(4)], axis=1))
    g_gin[...] = jnp.concatenate(gates, axis=0)
    vecs = jnp.concatenate([b[3168:3184, :], b[3184:3200, :]], axis=1)
    kv = panels(a, 0, 352, 3)
    kv = jnp.concatenate([unsplit(kv[:PAD], 0), unsplit(kv[PAD:], 0)], axis=0)
    kv = jnp.concatenate([kv[:, :MEM], kv[:, PAD : PAD + MEM]], axis=1)
    g_kv[...] = jnp.transpose(rows_to(cols_to(kv, 384), 384))[: 2 * MEM, : 2 * MEM]
    for i, at in ((1, 1056), (2, 1584)):
        x = panels(a, at, PAD, 3)[:MEM]
        g_tall[i] = jnp.concatenate([x[:, :MEM], x[:, PAD : PAD + MEM]], axis=1)
    both = unsplit(panels(a, 2112, PAD, 3), 0)
    sum_dq = unsplit(jnp.transpose(rows_to(vecs, 128))[:PAD, 15:16], 0)
    phase = vec[1:2, :]
    phase_low = jnp.cos(phase).astype(BF).astype(F32)
    g_tall[0] = jnp.concatenate([both[:, :MEM], sum_dq * phase_low], axis=1)
    g_sq[0] = both[:, PAD : PAD + MEM]
    last = panels(a, 2640, PAD, 3)[:MEM]
    g_sq[1] = last[:, :MEM]
    shared = jnp.transpose(rows_to(cols_to(g_gin[0 : 2 * MEM, 0:MEM], 256), 384))[:MEM, : 2 * MEM]
    g_hid[...] = jnp.concatenate([shared, last[:, PAD : PAD + MEM]], axis=1)
    query_low = tall[0][:, MEM:].astype(BF).astype(F32)
    phase_in = jnp.sum(query_low * sum_dq, axis=0, keepdims=True)
    row = lambda i: vecs[i : i + 1, :MEM]
    g_vec[...] = jnp.concatenate(
        [row(0), row(1) - jnp.sin(phase) * phase_in, row(2), row(3), row(4), row(2), row(3), row(7),
         unsplit(vecs[8:9], 1), unsplit(vecs[9:10], 1)] + [row(i) for i in range(10, 15)], axis=0)
    total = jnp.zeros((1, 1), F32)
    for ref in (g_gin, g_hid, g_kv, g_vec):
        total += jnp.sum(ref[...] * ref[...], keepdims=True)
    for ref in (g_tall, g_sq):
        for i in range(ref.shape[0]):
            total += jnp.sum(ref[i] * ref[i], keepdims=True)
    norm = jnp.sqrt(total)
    factor = jnp.minimum(1.0, CLIP_AT / (norm + NORM_EPS))
    norm_out[...] = norm
    loss_out[...] = jnp.sum(a[3168:3169, :], keepdims=True)
    for i, grad in enumerate((g_gin, g_hid, g_kv, g_tall, g_sq, g_vec)):
        rate, decay = (VECTOR_RATE, 0.0) if i == 5 else (LEARN_RATE, DECAY)
        param, one, two = state[i], state[6 + i], state[12 + i]
        new = news[i], news[6 + i], news[12 + i]
        if i == 4:
            for j in range(2):
                made = move(param[:, j, :], one[:, j, :], two[:, j, :], grad[j], factor, rate, decay)
                for ref, value in zip(new, made):
                    ref[:, j, :] = value
        elif len(param.shape) == 3:
            for j in range(param.shape[0]):
                made = move(param[j], one[j], two[j], grad[j], factor, rate, decay)
                for ref, value in zip(new, made):
                    ref[j] = value
        else:
            rows = param.shape[0]
            for at in range(0, rows, 16):
                s = slice(at, min(at + 16, rows))
                made = move(param[s], one[s], two[s], grad[s], factor, rate, decay)
                for ref, value in zip(new, made):
                    ref[s] = value


def adam(where, parts, mine, other, state):
    swap = lambda x: jnp.transpose(x, (0, 2, 1))
    def ready(group):
        gin, hid, kv, tall, sq, vec = group
        return [gin.T, hid, kv, swap(tall), jnp.transpose(sq, (1, 0, 2)), vec]
    state = ready(state[0:6]) + ready(state[6:12]) + ready(state[12:18])
    count = len(mine)
    shapes = [x.shape for x in state[:6]]
    shapes[4] = (2, MEM, MEM)
    vm = pl.BlockSpec(memory_space=pltpu.VMEM)
    outs = [jax.ShapeDtypeStruct(x.shape, F32) for x in state] + [jax.ShapeDtypeStruct((1, 1), F32)] * 2
    out = pl.pallas_call(
        lambda *r: adam_kernel(parts, *r),
        out_shape=outs,
        in_specs=[pl.BlockSpec(memory_space=pltpu.SMEM)] + [vm] * (2 * count + 18),
        out_specs=[vm] * 20,
        scratch_shapes=[pltpu.VMEM((3200, 128), F32), pltpu.VMEM((3200, 128), F32)] + [pltpu.VMEM(s, F32) for s in shapes],
        compiler_params=params(), name="adam", cost_estimate=cost(14),
    )(where, *mine, *other, *state)
    back = lambda group: [group[0].T, group[1], group[2], swap(group[3]), jnp.transpose(group[4], (1, 0, 2)), group[5]]
    return out[18].reshape(()), out[19].reshape(()), back(out[0:6]) + back(out[6:12]) + back(out[12:18])


AXES = ("dp", "rep")


def levels(size):
    found, stride = [], 1
    while size > 1:
        n = size if size <= 8 else 4
        found.append((stride, n))
        stride, size = stride * n, size // n
    return found


def peers(stride, k):
    dp, rep = lax.axis_size("dp"), lax.axis_size("rep")
    return [(d * rep + r, (d ^ (k * stride)) * rep + r) for d in range(dp) for r in range(rep)]


def twin():
    dp, rep = lax.axis_size("dp"), lax.axis_size("rep")
    return [(d * rep + r, d * rep + (rep - 1 - r)) for d in range(dp) for r in range(rep)]


def send(x, pairs):
    return lax.ppermute(x, AXES, pairs)


def tree(items, join):
    while len(items) > 1:
        items = [join(items[i], items[i + 1]) for i in range(0, len(items), 2)]
    return items[0]


def place(d, stride, n):
    return lax.rem(lax.div(d, stride), n)


def reduce_level(items, d, stride, n):
    c = place(d, stride, n)
    rows = items[0].shape[0] // n
    piece = lambda k: tree([lax.dynamic_slice_in_dim(x, (c ^ k) * rows, rows, 0) for x in items], jnp.add)
    return [piece(0)] + [send(piece(k), peers(stride, k)) for k in range(1, n)]


def gather_level(x, d, stride, n):
    return [x] + [send(x, peers(stride, k)) for k in range(1, n)]


def in_order(pieces, d, stride, n):
    c = place(d, stride, n)
    lines = []
    for i in range(n):
        line = pieces[i]
        for k in range(n):
            if k != i:
                line = jnp.where((c ^ k) == i, pieces[k], line)
        lines.append(line)
    return jnp.concatenate(lines, axis=0)


def spread_latest(x, d):
    nodes = lax.broadcasted_iota(I32, x.shape, 0) < x.shape[0] - 1
    join = lambda p, q: jnp.where(nodes, jnp.maximum(p, q), p + q)
    x = join(x, send(x, twin()))
    for stride, n in levels(lax.axis_size("dp")):
        x = tree(gather_level(x, d, stride, n), join)
    return x


def sum_grads(mine, theirs, d):
    steps = levels(lax.axis_size("dp"))
    items = [mine, send(theirs, twin())]
    for level in steps:
        items = reduce_level(items, d, *level)
    x = tree(items, jnp.add)
    for level in steps[:0:-1]:
        x = in_order(gather_level(x, d, *level), d, *level)
    return x, steps[0]


def body(source, target, neighbours, neighbour_ticks, event_ticks, event_types, labels, edge_feats, weights, memory,
         node_ticks, gru_in, gru_hid, keys_values, tall_stack, squares, vectors, *moments):
    events = event_ticks.shape[0]
    nodes = memory.shape[0]
    devices = lax.axis_size("dp") * lax.axis_size("rep")
    d, core = lax.axis_index("dp"), lax.axis_index("rep")
    scale = TIME_RATE / (events * devices)
    tiles = events // 128
    order = lambda x: jnp.transpose(x, (2, 1, 0)).reshape(NBR, 2, tiles, 128).transpose(0, 2, 1, 3).reshape(NBR, 2 * events)
    near_ids = order(neighbours).reshape(-1)
    near_ticks = order(neighbour_ticks)
    row = lambda x: x.reshape(1, events)
    lines = lambda x: x.reshape(tiles, 128)
    mem_t = memory.T
    spread = first_latest(nodes, lines(source), lines(target), lines(event_ticks), lines(weights))
    spread = spread_latest(spread, d)
    latest = spread[:-1].reshape(-1).astype(I32)
    w = prep(gru_in, gru_hid, keys_values, tall_stack, squares, vectors)
    wg, wgc, wh = w[0], w[1], w[2]
    vb = w[-1]
    own, near = fetch(source, target, near_ids, mem_t, node_ticks)
    cap = room(nodes, devices)
    msg, keep, ren, gap_own, packed = gru(
        scale, cap, source, target, event_ticks, latest, own, edge_feats.T, row(event_types), wg, wh, vb)
    gathered = lax.all_gather(packed[0], AXES)
    mine, theirs = main(scale, near, near_ticks, row(event_ticks), msg, keep, ren, gap_own, row(labels), row(weights),
                        spread[-1:], core.reshape(1), [wgc] + list(w[3:]))
    piece, level = sum_grads(mine, theirs, d)
    piece, gathered = lax.optimization_barrier((piece, gathered))
    blocks = gather_level(piece, d, *level)
    new_mem, more = merge(cap, gathered, mem_t)
    *blocks, new_mem = lax.optimization_barrier((*blocks, new_mem))
    other = [send(x, twin()) for x in blocks]
    grad_norm, loss_sum, news = adam(
        jnp.stack([core, place(d, *level)]), [(0, len(blocks))], blocks, other,
        (gru_in, gru_hid, keys_values, tall_stack, squares, vectors) + moments)
    weight_sum = spread[-1, 0]

    def again(carry):
        r, _, mem_now = carry
        mem_now, more = merge(cap, lax.all_gather(lax.dynamic_index_in_dim(packed, r, 0, False), AXES), mem_now)
        return r + 1, more & (r + 1 < packed.shape[0]), mem_now

    if packed.shape[0] > 1:
        new_mem = lax.while_loop(lambda c: c[1], again, (jnp.int32(1), more, new_mem))[2]
    return (grad_norm, loss_sum, weight_sum, new_mem.T, *news)


def solution(mesh):
    split = P(AXES)
    placed = (split, split, P(AXES, None, None), P(AXES, None, None), split, split, split, P(AXES, None), split)
    return jax.shard_map(body, mesh=mesh, in_specs=placed + (P(),) * 20, out_specs=(P(),) * 22, check_vma=False)
```

```python
import math

import jax
import jax.numpy as jnp
from jax import lax
from jax.experimental import pallas as pl
from jax.experimental.pallas import tpu as pltpu
from jax.sharding import PartitionSpec as P

F32 = jnp.float32
BF = jnp.bfloat16
I32 = jnp.int32
NBR = 10
MEM = 172
PAD = 176
HALF = 86
HPAD = 88
STEP = 10
LEARN_RATE = 0.03
VECTOR_RATE = 0.3
BETA_ONE = 0.9
BETA_TWO = 0.999
ADAM_EPS = 1e-08
DECAY = 0.01
CLIP_AT = 0.005
TIME_RATE = 64.0
NORM_EPS = 1e-06
VMEM_CAP = 58 * 2**20


def params(limit=VMEM_CAP):
    return pltpu.CompilerParams(vmem_limit_bytes=limit)


def cost(us):
    return pl.CostEstimate(flops=int(us * 1e9), bytes_accessed=int(us * 3e6), transcendentals=0)


def nn(a, b):
    return lax.dot_general(a, b, (((1,), (0,)), ((), ())), preferred_element_type=F32)


def nt(a, b):
    return lax.dot_general(a, b, (((1,), (1,)), ((), ())), preferred_element_type=F32)


def zeros(rows, cols):
    return jnp.zeros((rows, cols), F32)


def rows_to(x, total):
    return jnp.concatenate([x, zeros(total - x.shape[0], x.shape[1])], axis=0)


def cols_to(x, total):
    return jnp.concatenate([x, zeros(x.shape[0], total - x.shape[1])], axis=1)


def split_rows(x):
    gap = zeros(HPAD - HALF, x.shape[1])
    return jnp.concatenate([x[:HALF], gap, x[HALF:], gap], axis=0)


def eye(n):
    return (lax.broadcasted_iota(I32, (n, n), 0) == lax.broadcasted_iota(I32, (n, n), 1)).astype(BF)


def turned(x):
    return nt(eye(x.shape[1]), x.astype(BF))


def gate_weights_kernel(gin, ghid, vec, wg, wh, vb):
    full = gin[...]
    for gate in range(3):
        rows = full[gate * MEM : (gate + 1) * MEM]
        parts = [cols_to(rows[:, q * MEM : (q + 1) * MEM], PAD) for q in range(4)]
        wg[pl.ds(gate * PAD, PAD), :] = rows_to(jnp.concatenate(parts, axis=1), PAD).astype(BF)
    hid = ghid[...]
    for gate in range(3):
        part = cols_to(rows_to(hid[:, gate * MEM : (gate + 1) * MEM], PAD), 256)
        wh[pl.ds(gate * PAD, PAD), :] = turned(part)[:PAD].astype(BF)
    cols = jnp.transpose(cols_to(rows_to(vec[...], 128), 256))
    for i in range(15):
        column = cols[:, i : i + 1]
        if i in (8, 9):
            column = split_rows(column[:MEM])
        wide = jnp.broadcast_to(column[:PAD], (PAD, 128))
        vb[i] = wide * (0.5 / math.pi) if i < 2 else wide


def gate_weights(gin, ghid, vec):
    outs = [jax.ShapeDtypeStruct((528, 704), BF), jax.ShapeDtypeStruct((528, 176), BF),
            jax.ShapeDtypeStruct((15, PAD, 128), F32)]
    return pl.pallas_call(
        gate_weights_kernel, out_shape=outs, compiler_params=params(), name="gate_weights", cost_estimate=cost(4),
    )(gin.T, ghid, vec)


def main_weights_kernel(gin, kv, tall, sq, vec, wgc, kvm, kvct, kvc, t0t, t0, t1t, t1, t2t, t2, s0t, s0, s1t, s1, steady):
    for gate in range(3):
        code = cols_to(rows_to(gin[gate * MEM : (gate + 1) * MEM, 2 * MEM : 3 * MEM], PAD), 256)
        wgc[:, gate * PAD : (gate + 1) * PAD] = turned(code)[:PAD].astype(BF)
    pairs = kv[...]
    both = turned(cols_to(pairs, 384))
    halves = jnp.concatenate([split_rows(both[:MEM]), split_rows(both[MEM : 2 * MEM])], axis=0)
    kvm[...] = cols_to(halves[:, :MEM], 256).astype(BF)
    code_rows = cols_to(halves[:, MEM:], 256)
    kvct[...] = code_rows[:, :PAD].astype(BF)
    kvc[...] = turned(code_rows)[:PAD].astype(BF)
    query = tall[0]
    query_t = cols_to(split_rows(query[:, :MEM]), 256)
    t0t[...] = query_t[:, :PAD].astype(BF)
    t0[...] = turned(query_t)[:PAD].astype(BF)
    for src, fwd, back in ((tall[1], t1t, t1), (tall[2], t2t, t2)):
        wide = rows_to(jnp.concatenate([cols_to(src[:, :MEM], PAD), cols_to(src[:, MEM:], PAD)], axis=1), PAD)
        fwd[...] = wide.astype(BF)
        back[...] = turned(cols_to(wide, 384))[: 2 * PAD].astype(BF)
    first = cols_to(split_rows(sq[:, 0, :]), 256)
    s0[...] = first[:, :PAD].astype(BF)
    s0t[...] = turned(first)[:PAD].astype(BF)
    second = cols_to(rows_to(sq[:, 1, :], PAD), 256)
    s1[...] = second[:, :PAD].astype(BF)
    s1t[...] = turned(second)[:PAD].astype(BF)
    phase_low = jnp.cos(jnp.transpose(cols_to(rows_to(vec[...], 128), 256))[:PAD, 1:2]).astype(BF).astype(F32)
    row_id = lax.broadcasted_iota(I32, (PAD, 128), 0)
    wide_phase = jnp.where(row_id < MEM, jnp.broadcast_to(phase_low, (PAD, 128)), 0.0).astype(BF)
    steady[...] = nn(cols_to(split_rows(query[:, MEM:]), PAD).astype(BF), wide_phase)


def main_weights(gin, kv, tall, sq, vec):
    bf = lambda *s: jax.ShapeDtypeStruct(s, BF)
    outs = [bf(176, 528), bf(352, 256), bf(352, 176), bf(176, 352),
            bf(176, 176), bf(176, 176), bf(176, 352), bf(352, 176), bf(176, 352), bf(352, 176),
            bf(176, 176), bf(176, 176), bf(176, 176), bf(176, 176), jax.ShapeDtypeStruct((PAD, 128), F32)]
    return pl.pallas_call(
        main_weights_kernel, out_shape=outs, compiler_params=params(), name="main_weights", cost_estimate=cost(5),
    )(gin.T, kv, jnp.transpose(tall, (0, 2, 1)), jnp.transpose(sq, (1, 0, 2)), vec)


def first_kernel(source, target, ticks, weights, out):
    tiles = source.shape[0]
    heights = out.shape[0] - 1
    nodes, orders = [], []
    for b in range(tiles):
        nodes += [source[b : b + 1, :], target[b : b + 1, :]]
        orders += [2 * ticks[b : b + 1, :], 2 * ticks[b : b + 1, :] + 1]
    count = 2 * tiles
    stack = jnp.concatenate([x.astype(F32) for x in nodes + orders], axis=0)
    cols = jnp.transpose(rows_to(stack, 128))
    lane = lax.broadcasted_iota(I32, (128, 128), 1)
    line = lax.broadcasted_iota(I32, (heights, 128), 0)
    total = zeros(heights, 384)
    for c in range(count):
        node = jnp.broadcast_to(cols[:, c : c + 1], (128, 128)).astype(I32)
        order = jnp.broadcast_to(cols[:, count + c : count + c + 1], (128, 128)).astype(I32)
        beaten = zeros(128, 128)
        for e in range(count):
            beaten = jnp.where((node == nodes[e]) & (orders[e] > order), 1.0, beaten)
        beaten = jnp.max(beaten, axis=1, keepdims=True)
        value = jnp.where(beaten > 0.0, 0, order + 1)
        here = (node & 127) == lane
        pick = lambda v: jnp.where(here, v, 0).astype(F32).astype(BF)
        right = jnp.concatenate([pick(value & 127), pick((value >> 7) & 127), pick(value >> 14)], axis=1)
        left = (jnp.broadcast_to(nodes[c] >> 7, (heights, 128)) == line).astype(BF)
        total = total + nn(left, right)
    out[0:heights, :] = total[:, :128] + 128.0 * total[:, 128:256] + 16384.0 * total[:, 256:] - 1.0
    out[heights : heights + 1, :] = jnp.broadcast_to(jnp.sum(weights[...], keepdims=True), (1, 128))


def first_latest(nodes, source, target, ticks, weights):
    return pl.pallas_call(
        first_kernel, out_shape=jax.ShapeDtypeStruct((nodes // 128 + 1, 128), F32),
        compiler_params=params(), name="latest", cost_estimate=cost(2),
    )(source, target, ticks, weights)


def copy_rows(out, at, tables, ids):
    for h, table in enumerate(tables):
        rows = jnp.concatenate([table[pl.ds(i, 1), :] for i in ids], axis=0)
        out[pl.ds(at, 16), 128 * h : 128 * h + 128] = rows.astype(BF)


def table_kernel(source, target, mem, ticks, left, right, own, wide):
    step = pl.program_id(0)
    cols = mem.shape[1]

    @pl.when(step == 0)
    def _():
        wide[...] = jnp.zeros_like(wide)

    base = pl.multiple_of(step * cols, cols)
    wide[0:MEM, :] = mem[...].astype(BF).astype(F32)
    tick = ticks[...]
    for at, part in ((PAD, tick & 127), (PAD + 1, (tick >> 7) & 127), (PAD + 2, tick >> 14)):
        wide[at : at + 1, :] = part.astype(F32)
    unit = eye(256)
    for c in range(cols // 256):
        rows = nt(unit, wide[:, 256 * c : 256 * c + 256].astype(BF))
        left[pl.ds(base + 256 * c, 256), :] = rows[:, :128]
        right[pl.ds(base + 256 * c, 256), :] = rows[:, 128:]

    @pl.when(step == pl.num_programs(0) - 1)
    def _():
        def group(b, carry):
            for role, ids in enumerate((source, target)):
                def some(g, carry):
                    for v in range(2):
                        e = g * 32 + v * 16
                        at = pl.multiple_of(b * 256 + role * 128 + e, 16)
                        copy_rows(own, at, (left, right), [ids[b * 128 + e + u] for u in range(16)])
                    return carry

                lax.fori_loop(0, 4, some, 0)
            return carry

        lax.fori_loop(0, own.shape[0] // 256, group, 0)


def build_table(source, target, mem_t, ticks):
    nodes = mem_t.shape[1]
    ends = 2 * source.shape[0]
    cols = 2048
    smem = pl.BlockSpec(memory_space=pltpu.SMEM)
    half = jax.ShapeDtypeStruct((nodes, 128), F32)
    fixed = lambda i: (0, 0)
    return pl.pallas_call(
        table_kernel,
        out_shape=[half, half, jax.ShapeDtypeStruct((ends, 256), BF)],
        grid=(nodes // cols,),
        in_specs=[smem, smem, pl.BlockSpec((MEM, cols), lambda i: (0, i)), pl.BlockSpec((1, cols), lambda i: (0, i))],
        out_specs=[pl.BlockSpec((nodes, 128), fixed), pl.BlockSpec((nodes, 128), fixed), pl.BlockSpec((ends, 256), fixed)],
        scratch_shapes=[pltpu.VMEM((256, cols), F32)],
        compiler_params=params(), name="table", cost_estimate=cost(9),
    )(source, target, mem_t, ticks.reshape(1, nodes))


def near_kernel(chunk, ids, left, right, near):
    base = pl.program_id(0) * chunk

    def group(g, carry):
        for v in range(4):
            at = pl.multiple_of(g * 64 + v * 16, 16)
            copy_rows(near, at, (left, right), [ids[base + at + u] for u in range(16)])
        return carry

    lax.fori_loop(0, chunk // 64, group, 0)


def gather_near(ids, left, right):
    nears, chunk = ids.shape[0], ids.shape[0]
    whole = lambda a: pl.BlockSpec(a.shape, lambda i: (0, 0))
    return pl.pallas_call(
        lambda *r: near_kernel(chunk, *r),
        out_shape=jax.ShapeDtypeStruct((nears, 256), BF),
        grid=(nears // chunk,),
        in_specs=[pl.BlockSpec(memory_space=pltpu.SMEM), whole(left), whole(right)],
        out_specs=pl.BlockSpec((chunk, 256), lambda i: (i, 0)),
        compiler_params=params(), name="near", cost_estimate=cost(16),
    )(ids, left, right)


ROUND = 12582912.0
SIN = (6.283185005187988, -41.34165573120117, 81.60100555419922, -76.5497817993164, 39.536705017089844)
COS = (0.9999999403953552, -19.739171981811523, 64.9345932006836, -85.2403335571289, 56.24237823486328)


def cos_sin(turns):
    e = turns - ((turns + ROUND) - ROUND)
    w = 0.25 - jnp.abs(e)
    z = w * w
    c = w * (SIN[0] + z * (SIN[1] + z * (SIN[2] + z * (SIN[3] + z * SIN[4]))))
    s = COS[0] + z * (COS[1] + z * (COS[2] + z * (COS[3] + z * COS[4])))
    return c, jnp.where(e > 0.0, -s, s)


def sigmoid(x):
    return 0.5 * jnp.tanh(0.5 * x) + 0.5


BLOCK = 512
TILES = BLOCK // 256


def across(x):
    return jnp.concatenate([x] * (2 * TILES), axis=1)


def chunks(x, width=128):
    return [x[:, at : at + width] for at in range(0, x.shape[1], width)]


def both(x):
    return jnp.concatenate([c for c in chunks(x) for _ in range(2)], axis=1)


def mix(x, y):
    return jnp.concatenate([c for pair in zip(chunks(x), chunks(y)) for c in pair], axis=1)


def sources_of(x):
    return jnp.concatenate(chunks(x)[0::2], axis=1)


def targets_of(x):
    return jnp.concatenate(chunks(x)[1::2], axis=1)


def wide_rows(x, rows):
    return jnp.broadcast_to(x, (rows, x.shape[1]))


def gru_kernel(scale, cap, rounds, nodes, sources, targets, ticks_at, latest, own, source, target, ticks, edge, types, wg, wh, vb,
               msg, keep, ren, gap_out, packed, left, right, first, second):
    step = pl.program_id(0)
    own_t = nt(eye(256), own[...])
    seen = own_t[PAD : PAD + 1] + 128.0 * own_t[PAD + 1 : PAD + 2] + 16384.0 * own_t[PAD + 2 : PAD + 3]
    gap = (both(ticks[...].astype(F32)) - seen) * scale
    row_id = lax.broadcasted_iota(I32, (PAD, BLOCK), 0)
    own_x = jnp.where(row_id < MEM, own_t[:PAD], 0.0)
    msg[0:PAD, :] = own_x.astype(BF)
    msg[PAD : 2 * PAD, :] = mix(targets_of(own_x), sources_of(own_x)).astype(BF)
    edges = rows_to(edge[...].astype(F32) * types[...].astype(F32), PAD)
    msg[3 * PAD : 4 * PAD, :] = both(edges).astype(BF)
    gap_out[...] = wide_rows(gap, 8)
    gap16 = wide_rows(gap, 16)
    for st in range(PAD // 16):
        at = 16 * st
        for m in range(TILES):
            q = slice(256 * m, 256 * m + 256)
            rate, phase = vb[0, at : at + 16, :], vb[1, at : at + 16, :]
            x = jnp.concatenate([rate, rate], axis=1) * gap16[:, q] + jnp.concatenate([phase, phase], axis=1)
            c, s = cos_sin(x)
            msg[2 * PAD + at : 2 * PAD + at + 16, q] = c.astype(BF)
            keep[4, at : at + 16, q] = s
    gates = nn(wg[...], msg[...])
    hidden = nn(wh[...], msg[0:PAD, :])
    for st in range(PAD // 8):
        at = 8 * st
        o = own_x[at : at + 8]
        pre = [gates[g * PAD + at : g * PAD + at + 8] + across(vb[2 + g, at : at + 8, :]) for g in range(3)]
        hid = [hidden[g * PAD + at : g * PAD + at + 8] + across(vb[5 + g, at : at + 8, :]) for g in range(3)]
        u = sigmoid(pre[0] + hid[0])
        r = sigmoid(pre[1] + hid[1])
        n = jnp.tanh(pre[2] + r * hid[2])
        keep[0, at : at + 8, :] = u
        keep[1, at : at + 8, :] = r
        keep[2, at : at + 8, :] = n
        keep[3, at : at + 8, :] = hid[2]
        ren[at : at + 8, :] = (1.0 - u) * n + u * o
    numbers = mix(source[...], target[...]).astype(F32)
    low = jnp.concatenate([ren[128:MEM, :], numbers, zeros(255 - MEM, BLOCK)], axis=0)
    for role in range(2 * TILES):
        at = pl.multiple_of(step * BLOCK + 128 * role, 128)
        left[pl.ds(at, 128), :] = jnp.transpose(ren[0:128, 128 * role : 128 * role + 128])
        right[pl.ds(at, 128), :] = jnp.transpose(low[:, 128 * role : 128 * role + 128])

    @pl.when(step == pl.num_programs(0) - 1)
    def _():
        pack_rows(cap, rounds, nodes, sources, targets, ticks_at, latest, left, right, packed, first, second)


def pack_rows(cap, rounds, nodes, sources, targets, ticks, latest, left, right, out, first, second):
    def chunk(b, count):
        for role, ids in enumerate((sources, targets)):
            def some(g, count):
                for v in range(32):
                    e = b * 128 + g * 32 + v
                    i = b * 256 + role * 128 + g * 32 + v
                    won = latest[ids[e]] == 2 * ticks[e] + role
                    first[pl.ds(count, 1), :] = left[pl.ds(i, 1), :]
                    second[pl.ds(count, 1), :] = right[pl.ds(i, 1), :]
                    count = count + won.astype(I32)
                return count

            count = lax.fori_loop(0, 4, some, count)
        return count

    count = lax.fori_loop(0, sources.shape[0] // 128, chunk, jnp.int32(0))
    tail = cap // 2
    lane = lax.broadcasted_iota(I32, (1, 128), 1)
    for r in range(rounds):
        at = r * cap
        out[r, 0:cap, :] = first[at : at + cap, :]
        out[r, cap : cap + tail, :] = jnp.concatenate(
            [second[at : at + tail, 0:64], second[at + tail : at + cap, 0:64]], axis=1)
        here = jnp.clip(count - at, 0, cap)
        lines = []
        for q in range(-(-cap // 128)):
            numbers = jnp.transpose(second[at + 128 * q : at + 128 * q + 128, :])[MEM - 128 : MEM - 127]
            lines.append(jnp.where(lane + 128 * q < here, numbers, float(nodes)))
        lines.append(jnp.full((1, 128), here, I32).astype(F32))
        lines += [zeros(1, 128)] * (8 - len(lines))
        out[r, cap + tail :, :] = jnp.concatenate(lines, axis=0)


def gru(scale, cap, sources, targets, ticks, latest, own, edge_t, types, wg, wh, vb):
    ends, nodes = own.shape[0], latest.shape[0]
    blocks = ends // BLOCK
    rounds = ends // cap + 1
    spare = rounds * cap + 128
    whole = lambda a: pl.BlockSpec(a.shape, lambda i: (0,) * len(a.shape))
    lanes = lambda: pl.BlockSpec((1, BLOCK // 2), lambda i: (0, i))
    smem = pl.BlockSpec(memory_space=pltpu.SMEM)
    row = lambda x: x.reshape(1, -1)
    packed = jax.ShapeDtypeStruct((rounds, cap + cap // 2 + 8, 128), F32)
    return pl.pallas_call(
        lambda *r: gru_kernel(scale, cap, rounds, nodes, *r),
        out_shape=[jax.ShapeDtypeStruct((4 * PAD, ends), BF), jax.ShapeDtypeStruct((5, PAD, ends), F32),
                   jax.ShapeDtypeStruct((PAD, ends), F32), jax.ShapeDtypeStruct((8, ends), F32), packed],
        grid=(blocks,),
        in_specs=[smem] * 4 + [pl.BlockSpec((BLOCK, 256), lambda i: (i, 0)), lanes(), lanes(), lanes(),
                  pl.BlockSpec((MEM, BLOCK // 2), lambda i: (0, i)), lanes(), whole(wg), whole(wh), whole(vb)],
        out_specs=[pl.BlockSpec((4 * PAD, BLOCK), lambda i: (0, i)), pl.BlockSpec((5, PAD, BLOCK), lambda i: (0, 0, i)),
                   pl.BlockSpec((PAD, BLOCK), lambda i: (0, i)), pl.BlockSpec((8, BLOCK), lambda i: (0, i)), whole(packed)],
        scratch_shapes=[pltpu.VMEM((ends, 128), F32), pltpu.VMEM((ends, 128), F32),
                        pltpu.VMEM((spare, 128), F32), pltpu.VMEM((spare, 128), F32)],
        compiler_params=params(), name="gru", cost_estimate=cost(10),
    )(sources, targets, ticks, latest, own, row(sources), row(targets), row(ticks), edge_t, types, wg, wh, vb)


UNROLL = 5
GELU_C = math.sqrt(2.0 / math.pi)


def gelu_parts(x):
    sq = x * x
    t = jnp.tanh(GELU_C * (x + 0.044715 * (sq * x)))
    half = 0.5 * (1.0 + t)
    slope = half + (0.5 * x) * (1.0 - t * t) * (GELU_C + (GELU_C * 3.0 * 0.044715) * sq)
    return x * half, slope


def fold(x):
    total, *others = chunks(x)
    for other in others:
        total = total + other
    return total


def main_kernel(scale, core, near, gaps_t, ticks, msg, keep, ren, gap_own, labels, weights, total,
                wgc, kvm, kvct, kvc, t0t, t0, t1t, t1, t2t, t2, s0t, s0, s1t, s1, steady, vb,
                mine, theirs,
                loss, pair, code, dcode, soft, back, mean, d_query_at, grads, g_in, g_kv, g_one, g_dec, g_qo, g_th, vacc):
    step = pl.program_id(0)
    inv_size = HALF ** -0.5

    @pl.when(step == 0)
    def _():
        for ref in (g_in, g_kv, g_one, g_dec, g_qo, g_th, vacc, loss):
            ref[...] = jnp.zeros_like(ref)

    tick2 = both(ticks[...].astype(F32))
    renewed = ren[...]
    ren_low = renewed.astype(BF)
    queries = nn(t0t[...], ren_low) + across(vb[8] + steady[...])
    def each(one):
        def some(g, carry):
            for v in range(UNROLL):
                one(g * UNROLL + v)
            return carry

        lax.fori_loop(0, NBR // UNROLL, some, 0)

    def look(j):
        gap16 = wide_rows((tick2 - gaps_t[pl.ds(j, 1), :].astype(F32)) * scale, 16)
        for st in range(PAD // 16):
            at = 16 * st
            for m in range(TILES):
                q = slice(256 * m, 256 * m + 256)
                rate, phase = vb[0, at : at + 16, :], vb[1, at : at + 16, :]
                x = jnp.concatenate([rate, rate], axis=1) * gap16[:, q] + jnp.concatenate([phase, phase], axis=1)
                c, s = cos_sin(x)
                code[j, at : at + 16, q] = c.astype(BF)
                dcode[j, at : at + 16, q] = s
        pair[j] = nt(kvm[...], near[j]) + nn(kvct[...], code[j])
        for h in range(2):
            acc = zeros(8, BLOCK)
            for st in range(HPAD // 8):
                at = HPAD * h + 8 * st
                acc = acc + pair[j, at : at + 8, :] * queries[at : at + 8]
            soft[2 * j + h] = wide_rows(jnp.sum(acc, axis=0, keepdims=True) * inv_size, 8)

    each(look)
    for h in range(2):
        top = soft[h]
        for j in range(1, NBR):
            top = jnp.maximum(top, soft[2 * j + h])
        norm = zeros(8, BLOCK)
        for j in range(NBR):
            e = jnp.exp(soft[2 * j + h] - top)
            soft[2 * j + h] = e
            norm = norm + e
        inv = 1.0 / norm
        for j in range(NBR):
            soft[2 * j + h] = soft[2 * j + h] * inv
    att = []
    for st in range(PAD // 8):
        at = 8 * st
        h = 0 if at < HPAD else 1
        acc = across(vb[9, at : at + 8, :])
        for j in range(NBR):
            acc = acc + soft[2 * j + h] * pair[j, PAD + at : PAD + at + 8, :]
        att.append(acc)
    att_low = jnp.concatenate(att, axis=0).astype(BF)
    projected = nn(s0t[...], att_low) + across(vb[10])
    mlp_in = jnp.concatenate([projected.astype(BF), ren_low], axis=0)
    inner = nn(t1t[...], mlp_in) + across(vb[11])
    act, act_slope = gelu_parts(inner)
    act_low = act.astype(BF)
    emb_low = (nn(s1t[...], act_low) + across(vb[12])).astype(BF)
    dec_in = jnp.concatenate([sources_of(emb_low), targets_of(emb_low)], axis=0)
    out_row = jnp.concatenate([vb[14]] * TILES, axis=1)
    dec_pre = nn(t2t[...], dec_in) + jnp.concatenate([vb[13]] * TILES, axis=1)
    dec_act, dec_slope = gelu_parts(dec_pre)
    logit = jnp.sum(dec_act * out_row, axis=0, keepdims=True)
    label = labels[...].astype(F32)
    tail = jnp.exp(-jnp.abs(logit))
    plus = jnp.maximum(logit, 0.0) + jnp.log1p(tail)
    loss[...] += fold(weights[...] * (plus - label * logit))
    d_logit = weights[...] / total[:, 0:1] * (sigmoid(logit) - label)
    d_out = d_logit * dec_act
    d_dec = (d_logit * out_row) * dec_slope
    d_dec_low = d_dec.astype(BF)
    g_dec[...] += nt(d_dec_low, dec_in)
    d_dec_in = nn(t2[...], d_dec_low)
    d_emb = mix(d_dec_in[:PAD], d_dec_in[PAD:])
    d_emb_low = d_emb.astype(BF)
    g_th[:, 0:256] += jnp.concatenate([nt(act_low, d_emb_low), zeros(PAD, 256 - PAD)], axis=1)
    d_inner = nn(s1[...], d_emb_low) * act_slope
    d_inner_low = d_inner.astype(BF)
    g_one[...] += nt(d_inner_low, mlp_in)
    d_mlp = nn(t1[...], d_inner_low)
    d_proj = d_mlp[:PAD]
    d_proj_low = d_proj.astype(BF)
    g_qo[:, 256:512] += jnp.concatenate([nt(att_low, d_proj_low), zeros(PAD, 256 - PAD)], axis=1)
    d_att = nn(s0[...], d_proj_low)
    d_query_at[...] = jnp.zeros_like(d_query_at)
    mean[...] = jnp.zeros_like(mean)

    def weigh(j):
        for h in range(2):
            acc = zeros(8, BLOCK)
            for st in range(HPAD // 8):
                at = HPAD * h + 8 * st
                acc = acc + pair[j, PAD + at : PAD + at + 8, :] * d_att[at : at + 8]
            wide = wide_rows(jnp.sum(acc, axis=0, keepdims=True), 8)
            back[2 * j + h] = wide
            mean[h] += wide * soft[2 * j + h]

    def learn(j):
        share = [soft[2 * j + h] for h in range(2)]
        slope = [(share[h] * inv_size) * (back[2 * j + h] - mean[h]) for h in range(2)]
        for st in range(PAD // 8):
            at = 8 * st
            d_query_at[at : at + 8, :] += slope[at >= HPAD] * pair[j, at : at + 8, :]
        for st in range(2 * PAD // 16):
            parts = []
            for half in range(2):
                at = 16 * st + 8 * half
                if at < PAD:
                    parts.append(slope[at >= HPAD] * queries[at : at + 8])
                else:
                    parts.append(share[at - PAD >= HPAD] * d_att[at - PAD : at - PAD + 8])
            grads[j, 16 * st : 16 * st + 16, :] = jnp.concatenate(parts, axis=0).astype(BF)
        d_code = nn(kvc[...], grads[j])
        gap8 = wide_rows((tick2 - gaps_t[pl.ds(j, 1), :].astype(F32)) * scale, 8)
        for st in range(PAD // 8):
            at = 8 * st
            d_arg = d_code[at : at + 8] * dcode[j, at : at + 8, :]
            vacc[0, at : at + 8, :] += fold(d_arg * gap8)
            vacc[1, at : at + 8, :] += fold(d_arg)
        g_kv[:, 0:256] += nn(grads[j], near[j])
        g_kv[:, 256 : 256 + PAD] += nt(grads[j], code[j])

    each(weigh)
    each(learn)
    d_query = d_query_at[...]
    d_q_low = d_query.astype(BF)
    g_qo[:, 0:256] += jnp.concatenate([nt(d_q_low, ren_low), zeros(PAD, 256 - PAD)], axis=1)
    d_ren = d_mlp[PAD:] + nn(t0[...], d_q_low)
    own_x = msg[0:PAD, :].astype(F32)
    u, r, n, hn = keep[0], keep[1], keep[2], keep[3]
    d_u = d_ren * (own_x - n) * (u * (1.0 - u))
    d_n = d_ren * (1.0 - u) * (1.0 - n * n)
    d_r = d_n * hn * (r * (1.0 - r))
    d_h = d_n * r
    gates = jnp.concatenate([d_u, d_r, d_n], axis=0).astype(BF)
    g_in[...] += nt(gates, msg[...])
    g_th[:, 256:512] += jnp.concatenate([nt(msg[0:PAD, :], d_h.astype(BF)), zeros(PAD, 256 - PAD)], axis=1)
    d_arg = nn(wgc[...], gates) * keep[4]
    vacc[0] += fold(d_arg * gap_own[0:1, :])
    vacc[1] += fold(d_arg)
    for i, item in ((2, d_u), (3, d_r), (4, d_n), (7, d_h), (8, d_query), (9, d_att), (10, d_proj), (11, d_inner),
                    (12, d_emb), (15, d_q_low.astype(F32))):
        vacc[i] += fold(item)
    vacc[13] += fold(d_dec)
    vacc[14] += fold(d_out)

    def finish(ga, gb):
        wide = cols_to(g_in[...], 768)
        for c in range(6):
            gb[528 * c : 528 * c + 528, :] = wide[:, 128 * c : 128 * c + 128]
        lane = lax.broadcasted_iota(I32, (PAD, 128), 1)
        vecs = zeros(PAD, 128)
        for i in range(16):
            column = jnp.sum(vacc[i], axis=1, keepdims=True)
            vecs = jnp.where(lane == i, column, vecs)
        flat = jnp.transpose(jnp.concatenate([vecs, zeros(256 - PAD, 128)], axis=0))
        gb[3168:3184, :] = flat[0:16, 0:128]
        gb[3184:3200, :] = flat[0:16, 128:256]
        at = 0
        for left, right, rows in ((g_kv[:, 0:PAD], g_kv[:, 256 : 256 + PAD], 352),
                                  (g_one[:, 0:PAD], g_one[:, PAD : 2 * PAD], 176),
                                  (g_dec[:, 0:PAD], g_dec[:, PAD : 2 * PAD], 176),
                                  (g_qo[:, 0:PAD], g_qo[:, 256 : 256 + PAD], 176),
                                  (g_th[:, 0:PAD], g_th[:, 256 : 256 + PAD], 176)):
            wide = jnp.concatenate([left, right, zeros(rows, 32)], axis=1)
            for c in range(3):
                ga[at : at + rows, :] = wide[:, 128 * c : 128 * c + 128]
                at += rows
        ga[3168:3200, :] = rows_to(loss[...], 32)

    @pl.when((step == pl.num_programs(0) - 1) & (core[0] == 0))
    def _():
        finish(mine, theirs)

    @pl.when((step == pl.num_programs(0) - 1) & (core[0] != 0))
    def _():
        finish(theirs, mine)


def main(scale, near, near_ticks, ticks, msg, keep, ren, gap_own, labels, weights, total, core, w):
    ends = ren.shape[1]
    blocks = ends // BLOCK
    whole = lambda a: pl.BlockSpec(a.shape, lambda i: (0,) * len(a.shape))
    lanes = lambda: pl.BlockSpec((1, BLOCK // 2), lambda i: (0, i))
    return pl.pallas_call(
        lambda *r: main_kernel(scale, *r),
        out_shape=[jax.ShapeDtypeStruct((3200, 128), F32), jax.ShapeDtypeStruct((3200, 128), F32)],
        grid=(blocks,),
        in_specs=[pl.BlockSpec(memory_space=pltpu.SMEM), pl.BlockSpec((NBR, BLOCK, 256), lambda i: (0, i, 0)), pl.BlockSpec((NBR, BLOCK), lambda i: (0, i)), lanes(),
                  pl.BlockSpec((4 * PAD, BLOCK), lambda i: (0, i)), pl.BlockSpec((5, PAD, BLOCK), lambda i: (0, 0, i)),
                  pl.BlockSpec((PAD, BLOCK), lambda i: (0, i)), pl.BlockSpec((8, BLOCK), lambda i: (0, i)), lanes(), lanes(),
                  pl.BlockSpec((1, 128), lambda i: (0, 0))] + [whole(a) for a in w],
        out_specs=[pl.BlockSpec((3200, 128), lambda i: (0, 0)), pl.BlockSpec((3200, 128), lambda i: (0, 0))],
        scratch_shapes=[pltpu.VMEM((1, 128), F32), pltpu.VMEM((NBR, 352, BLOCK), F32), pltpu.VMEM((NBR, PAD, BLOCK), BF), pltpu.VMEM((NBR, PAD, BLOCK), F32),
                        pltpu.VMEM((20, 8, BLOCK), F32), pltpu.VMEM((20, 8, BLOCK), F32), pltpu.VMEM((2, 8, BLOCK), F32),
                        pltpu.VMEM((PAD, BLOCK), F32), pltpu.VMEM((NBR, 352, BLOCK), BF),
                        pltpu.VMEM((528, 704), F32), pltpu.VMEM((352, 512), F32), pltpu.VMEM((PAD, 352), F32),
                        pltpu.VMEM((PAD, 352), F32), pltpu.VMEM((PAD, 512), F32), pltpu.VMEM((PAD, 512), F32),
                        pltpu.VMEM((16, PAD, 128), F32)],
        compiler_params=params(), name="main", cost_estimate=cost(35),
    )(core, near.reshape(NBR, ends, 256), near_ticks, ticks, msg, keep, ren, gap_own, labels, weights, total, *w)


def room(nodes, devices):
    return -(-(nodes * 9) // (devices * 8 * 16)) * 16


def turned_exactly(x):
    high = x.astype(BF)
    rest = x - high.astype(F32)
    middle = rest.astype(BF)
    low = (rest - middle.astype(F32)).astype(BF)
    unit = eye(x.shape[1])
    return (nt(unit, high) + nt(unit, middle)) + nt(unit, low)


def lay_rows(cap, number, rows, left, right, second):
    tail = cap // 2
    width = -(-cap // 128) * 128

    def block(q, most):
        half = rows[q, cap : cap + tail, :]
        second[0:tail, :] = half
        second[tail:cap, :] = jnp.concatenate([half[:, 64:], half[:, :64]], axis=1)
        here = number(q, width)

        def some(g, carry):
            for v in range(16):
                i = g * 16 + v
                node = number(q, i)
                left[pl.ds(node, 1), :] = rows[q, pl.ds(i, 1), :]
                right[pl.ds(node, 1), :] = second[pl.ds(i, 1), :]
            return carry

        lax.fori_loop(0, lax.div(here + 15, 16), some, 0)
        return jnp.maximum(most, here)

    return lax.fori_loop(0, rows.shape[0], block, jnp.int32(0))


def lay_kernel(cap, count, *refs):
    arrays, (left, right, most, joined, second, sems), rest = refs[:count], refs[count : count + 6], refs[count + 6 :]
    wholes, lists = rest[:count], rest[count:]
    lines = cap + cap // 2
    copies = []
    for a, (rows, whole) in enumerate(zip(arrays, wholes)):
        whole[...] = rows[:, lines:, :].astype(I32)
        copies.append(pltpu.make_async_copy(whole, lists[a], sems.at[a]))
        copies[a].start()
    right[...] = jnp.full_like(right, -1.0)
    for a, rows in enumerate(arrays):
        blocks = rows.shape[0]
        joined[a * blocks : (a + 1) * blocks] = rows[...]
    largest = jnp.int32(0)
    for a, rows in enumerate(arrays):
        copies[a].wait()
        number = lambda q, i: lists[a][q, lax.shift_right_logical(i, 7), i & 127]
        largest = jnp.maximum(largest, lay_rows(cap, number, rows, left, right, second))
    most[0] = largest


def row_numbers(cap, x):
    first, height = cap + cap // 2, -(-cap // 128) + 1
    return x[:, first : first + height, :].astype(I32).reshape(-1)


def lay(cap, nodes, arrays):
    vm, smem = pl.BlockSpec(memory_space=pltpu.VMEM), pl.BlockSpec(memory_space=pltpu.SMEM)
    table = jax.ShapeDtypeStruct((nodes + 8, 128), F32)
    count = len(arrays)
    blocks, height, _ = arrays[0].shape
    return pl.pallas_call(
        lambda *r: lay_kernel(cap, count, *r),
        out_shape=[table, table, jax.ShapeDtypeStruct((1,), I32), jax.ShapeDtypeStruct((count * blocks, height, 128), F32)],
        in_specs=[vm] * count, out_specs=[vm, vm, smem, vm],
        scratch_shapes=[pltpu.VMEM((cap, 128), F32), pltpu.SemaphoreType.DMA((count,))]
        + [kind((blocks, 8, 128), I32) for kind in (pltpu.VMEM, pltpu.SMEM) for _ in arrays],
        compiler_params=params(), name="lay", cost_estimate=cost(14),
    )(*arrays)


def merge_kernel(cap, numbers, rows, far_left, far_right, before, mem, out, full, left, right, second, sems):
    step = pl.program_id(0)

    @pl.when(step == 0)
    def _():
        copies = [pltpu.make_async_copy(far_left, left, sems.at[0]), pltpu.make_async_copy(far_right, right, sems.at[1])]
        for copy in copies:
            copy.start()
        for copy in copies:
            copy.wait()
        width = -(-cap // 128) * 128 + 128
        most = lay_rows(cap, lambda q, i: numbers[q * width + i], rows, left, right, second)
        full[0] = (jnp.maximum(most, before[0]) == cap).astype(I32)

    cols = mem.shape[1]
    base = pl.multiple_of(step * cols, cols)
    for c in range(cols // 256):
        at = base + 256 * c
        s = slice(256 * c, 256 * c + 256)
        top = turned_exactly(left[pl.ds(at, 256), :])
        low = turned_exactly(right[pl.ds(at, 256), :])
        fresh = low[MEM - 128 : MEM - 127] >= 0.0
        out[0:128, s] = jnp.where(fresh, top, mem[0:128, s])
        out[128:MEM, s] = jnp.where(fresh, low[: MEM - 128], mem[128:MEM, s])


def merge(cap, laid, rows, mem_t):
    nodes = mem_t.shape[1]
    cols = 2048
    part = pl.BlockSpec((MEM, cols), lambda i: (0, i))
    smem, far = pl.BlockSpec(memory_space=pltpu.SMEM), pl.BlockSpec(memory_space=pl.ANY)
    new, full = pl.pallas_call(
        lambda *r: merge_kernel(cap, *r),
        out_shape=[jax.ShapeDtypeStruct((MEM, nodes), F32), jax.ShapeDtypeStruct((1,), I32)],
        grid=(nodes // cols,),
        in_specs=[smem, pl.BlockSpec(rows.shape, lambda i: (0, 0, 0)), far, far, smem, part],
        out_specs=[part, smem],
        scratch_shapes=[pltpu.VMEM((nodes + 8, 128), F32), pltpu.VMEM((nodes + 8, 128), F32), pltpu.VMEM((cap, 128), F32),
                        pltpu.SemaphoreType.DMA((2,))],
        compiler_params=params(), name="merge", cost_estimate=cost(18),
    )(row_numbers(cap, rows), rows, *laid, mem_t)
    return new, full[0] > 0


def move(param, one, two, grad, factor, rate, decay):
    clipped = grad * factor
    one = BETA_ONE * one + (1.0 - BETA_ONE) * clipped
    two = BETA_TWO * two + (1.0 - BETA_TWO) * clipped * clipped
    step = (one * (1.0 / (1.0 - BETA_ONE**STEP))) / (jnp.sqrt(two * (1.0 / (1.0 - BETA_TWO**STEP))) + ADAM_EPS)
    return param - rate * (step + decay * param), one, two


def unsplit(x, axis):
    take = lambda a, b: lax.slice_in_dim(x, a, b, axis=axis)
    return jnp.concatenate([take(0, HALF), take(HPAD, HPAD + HALF)], axis=axis)


def adam_kernel(parts, where, *refs):
    count = sum(n for _, n in parts)
    mine, other = refs[:count], refs[count : 2 * count]
    refs = refs[2 * count :]
    far, out, (norm_out, loss_out) = refs[:18], refs[18:36], refs[36:38]
    a, b, g_gin, g_hid, g_kv, g_tall, g_sq, g_vec = refs[38:46]
    state, sems_in, sems_out = refs[46:64], refs[64], refs[65]
    fetches = [pltpu.make_async_copy(far[i], state[i], sems_in.at[i]) for i in range(18)]
    stores = [pltpu.make_async_copy(state[i], out[i], sems_out.at[i]) for i in range(18)]
    for i in (5, 3, 0, 6, 12, 1, 7, 13, 2, 8, 14, 9, 15, 4, 10, 16, 11, 17):
        fetches[i].start()
    core = where[0]
    at_block = 0
    for p, (first, n) in enumerate(parts):
        height = mine[at_block].shape[0]
        for k in range(n):
            at = pl.multiple_of(first + (where[1 + p] ^ k) * height, 8)
            one, two = mine[at_block], other[at_block]
            at_block += 1

            @pl.when(core == 0)
            def _():
                a[pl.ds(at, height), :] = one[...]
                b[pl.ds(at, height), :] = two[...]

            @pl.when(core != 0)
            def _():
                b[pl.ds(at, height), :] = one[...]
                a[pl.ds(at, height), :] = two[...]

    def panels(ref, at, rows, n):
        return jnp.concatenate([ref[at + c * rows : at + (c + 1) * rows, :] for c in range(n)], axis=1)

    vec, tall = state[5], state[3]
    wide = panels(b, 0, 528, 6)
    gates = []
    for g in range(3):
        rows = wide[PAD * g : PAD * g + MEM]
        gates.append(jnp.concatenate([rows[:, PAD * q : PAD * q + MEM] for q in range(4)], axis=1))
    g_gin[...] = jnp.concatenate(gates, axis=0)
    vecs = jnp.concatenate([b[3168:3184, :], b[3184:3200, :]], axis=1)
    kv = panels(a, 0, 352, 3)
    kv = jnp.concatenate([unsplit(kv[:PAD], 0), unsplit(kv[PAD:], 0)], axis=0)
    kv = jnp.concatenate([kv[:, :MEM], kv[:, PAD : PAD + MEM]], axis=1)
    g_kv[...] = jnp.transpose(rows_to(cols_to(kv, 384), 384))[: 2 * MEM, : 2 * MEM]
    for i, at in ((1, 1056), (2, 1584)):
        x = panels(a, at, PAD, 3)[:MEM]
        g_tall[i] = jnp.concatenate([x[:, :MEM], x[:, PAD : PAD + MEM]], axis=1)
    both = unsplit(panels(a, 2112, PAD, 3), 0)
    sum_dq = unsplit(jnp.transpose(rows_to(vecs, 128))[:PAD, 15:16], 0)
    fetches[5].wait()
    fetches[3].wait()
    phase = vec[1:2, :]
    phase_low = jnp.cos(phase).astype(BF).astype(F32)
    g_tall[0] = jnp.concatenate([both[:, :MEM], sum_dq * phase_low], axis=1)
    g_sq[0] = both[:, PAD : PAD + MEM]
    last = panels(a, 2640, PAD, 3)[:MEM]
    g_sq[1] = last[:, :MEM]
    shared = jnp.transpose(rows_to(cols_to(g_gin[0 : 2 * MEM, 0:MEM], 256), 384))[:MEM, : 2 * MEM]
    g_hid[...] = jnp.concatenate([shared, last[:, PAD : PAD + MEM]], axis=1)
    query_low = tall[0][:, MEM:].astype(BF).astype(F32)
    phase_in = jnp.sum(query_low * sum_dq, axis=0, keepdims=True)
    row = lambda i: vecs[i : i + 1, :MEM]
    g_vec[...] = jnp.concatenate(
        [row(0), row(1) - jnp.sin(phase) * phase_in, row(2), row(3), row(4), row(2), row(3), row(7),
         unsplit(vecs[8:9], 1), unsplit(vecs[9:10], 1)] + [row(i) for i in range(10, 15)], axis=0)
    total = jnp.zeros((1, 1), F32)
    for ref in (g_gin, g_hid, g_kv, g_vec):
        total += jnp.sum(ref[...] * ref[...], keepdims=True)
    for ref in (g_tall, g_sq):
        for i in range(ref.shape[0]):
            total += jnp.sum(ref[i] * ref[i], keepdims=True)
    norm = jnp.sqrt(total)
    factor = jnp.minimum(1.0, CLIP_AT / (norm + NORM_EPS))
    norm_out[...] = norm
    loss_out[...] = jnp.sum(a[3168:3169, :], keepdims=True)
    for i, grad in enumerate((g_gin, g_hid, g_kv, g_tall, g_sq, g_vec)):
        rate, decay = (VECTOR_RATE, 0.0) if i == 5 else (LEARN_RATE, DECAY)
        new = param, one, two = state[i], state[6 + i], state[12 + i]
        for at in (i, 6 + i, 12 + i):
            if at not in (3, 5):
                fetches[at].wait()
        if i == 4:
            for j in range(2):
                made = move(param[:, j, :], one[:, j, :], two[:, j, :], grad[j], factor, rate, decay)
                for ref, value in zip(new, made):
                    ref[:, j, :] = value
        elif len(param.shape) == 3:
            for j in range(param.shape[0]):
                made = move(param[j], one[j], two[j], grad[j], factor, rate, decay)
                for ref, value in zip(new, made):
                    ref[j] = value
        else:
            rows = param.shape[0]
            for at in range(0, rows, 16):
                s = slice(at, min(at + 16, rows))
                made = move(param[s], one[s], two[s], grad[s], factor, rate, decay)
                for ref, value in zip(new, made):
                    ref[s] = value
        for at in (i, 6 + i, 12 + i):
            stores[at].start()
    for store in stores:
        store.wait()


def adam(where, parts, mine, other, state):
    swap = lambda x: jnp.transpose(x, (0, 2, 1))
    def ready(group):
        gin, hid, kv, tall, sq, vec = group
        return [gin.T, hid, kv, swap(tall), jnp.transpose(sq, (1, 0, 2)), vec]
    state = ready(state[0:6]) + ready(state[6:12]) + ready(state[12:18])
    count = len(mine)
    shapes = [x.shape for x in state[:6]]
    shapes[4] = (2, MEM, MEM)
    vm, far = pl.BlockSpec(memory_space=pltpu.VMEM), pl.BlockSpec(memory_space=pl.ANY)
    outs = [jax.ShapeDtypeStruct(x.shape, F32) for x in state] + [jax.ShapeDtypeStruct((1, 1), F32)] * 2
    out = pl.pallas_call(
        lambda *r: adam_kernel(parts, *r),
        out_shape=outs,
        in_specs=[pl.BlockSpec(memory_space=pltpu.SMEM)] + [vm] * (2 * count) + [far] * 18,
        out_specs=[far] * 18 + [vm] * 2,
        scratch_shapes=[pltpu.VMEM((3200, 128), F32), pltpu.VMEM((3200, 128), F32)] + [pltpu.VMEM(s, F32) for s in shapes]
        + [pltpu.VMEM(x.shape, F32) for x in state] + [pltpu.SemaphoreType.DMA((18,))] * 2,
        compiler_params=params(), name="adam", cost_estimate=cost(14),
    )(where, *mine, *other, *state)
    back = lambda group: [group[0].T, group[1], group[2], swap(group[3]), jnp.transpose(group[4], (1, 0, 2)), group[5]]
    return out[18].reshape(()), out[19].reshape(()), back(out[0:6]) + back(out[6:12]) + back(out[12:18])


AXES = ("dp", "rep")


def levels(size):
    found, stride = [], 1
    while size > 1:
        n = size if size <= 8 else 4
        found.append((stride, n))
        stride, size = stride * n, size // n
    return found


def peers(stride, k):
    dp, rep = lax.axis_size("dp"), lax.axis_size("rep")
    return [(d * rep + r, (d ^ (k * stride)) * rep + r) for d in range(dp) for r in range(rep)]


def twin():
    dp, rep = lax.axis_size("dp"), lax.axis_size("rep")
    return [(d * rep + r, d * rep + (rep - 1 - r)) for d in range(dp) for r in range(rep)]


def send(x, pairs):
    return lax.ppermute(x, AXES, pairs)


def tree(items, join):
    while len(items) > 1:
        items = [join(items[i], items[i + 1]) for i in range(0, len(items), 2)]
    return items[0]


def place(d, stride, n):
    return lax.rem(lax.div(d, stride), n)


def reduce_level(items, d, stride, n):
    c = place(d, stride, n)
    rows = items[0].shape[0] // n
    piece = lambda k: tree([lax.dynamic_slice_in_dim(x, (c ^ k) * rows, rows, 0) for x in items], jnp.add)
    return [piece(0)] + [send(piece(k), peers(stride, k)) for k in range(1, n)]


def gather_level(x, d, stride, n):
    return [x] + [send(x, peers(stride, k)) for k in range(1, n)]


def in_order(pieces, d, stride, n):
    c = place(d, stride, n)
    lines = []
    for i in range(n):
        line = pieces[i]
        for k in range(n):
            if k != i:
                line = jnp.where((c ^ k) == i, pieces[k], line)
        lines.append(line)
    return jnp.concatenate(lines, axis=0)


def spread_latest(x, d):
    nodes = lax.broadcasted_iota(I32, x.shape, 0) < x.shape[0] - 1
    join = lambda p, q: jnp.where(nodes, jnp.maximum(p, q), p + q)
    x = join(x, send(x, twin()))
    for stride, n in levels(lax.axis_size("dp")):
        x = tree(gather_level(x, d, stride, n), join)
    return x


def spread_upper(x, d):
    for level in levels(lax.axis_size("dp"))[:0:-1]:
        x = jnp.concatenate(gather_level(x, d, *level), axis=0)
    return x


def tie(*xs):
    return lax.optimization_barrier(xs)


def body(source, target, neighbours, neighbour_ticks, event_ticks, event_types, labels, edge_feats, weights, memory,
         node_ticks, gru_in, gru_hid, keys_values, tall_stack, squares, vectors, *moments):
    events = event_ticks.shape[0]
    nodes = memory.shape[0]
    devices = lax.axis_size("dp") * lax.axis_size("rep")
    d, core = lax.axis_index("dp"), lax.axis_index("rep")
    scale = TIME_RATE / (events * devices)
    tiles = events // 128
    order = lambda x: jnp.transpose(x, (2, 1, 0)).reshape(NBR, 2, tiles, 128).transpose(0, 2, 1, 3).reshape(NBR, 2 * events)
    near_ids = order(neighbours).reshape(-1)
    near_ticks = order(neighbour_ticks)
    row = lambda x: x.reshape(1, events)
    lines = lambda x: x.reshape(tiles, 128)
    mem_t = memory.T
    spread = first_latest(nodes, lines(source), lines(target), lines(event_ticks), lines(weights))
    spread = spread_latest(spread, d)
    latest = spread[:-1].reshape(-1).astype(I32)
    wg, wh, vb = gate_weights(gru_in, gru_hid, vectors)
    left, right, own = build_table(source, target, mem_t, node_ticks)
    cap = room(nodes, devices)
    msg, keep, ren, gap_own, packed = gru(
        scale, cap, source, target, event_ticks, latest, own, edge_feats.T, row(event_types), wg, wh, vb)
    height = packed.shape[1]
    low, *upper = levels(lax.axis_size("dp"))
    first_round, left, right = tie(packed[0], left, right)
    rows = spread_upper(first_round, d)
    near = gather_near(near_ids, left, right)
    rows, near, vec_late = tie(rows, near, vectors)
    w = main_weights(gru_in, keys_values, tall_stack, squares, vec_late)
    held = gather_level(rows, d, *low)
    mine, theirs = main(scale, near, near_ticks, row(event_ticks), msg, keep, ren, gap_own, row(labels), row(weights),
                        spread[-1:], core.reshape(1), list(w) + [vb])
    mine, theirs, *held = tie(mine, theirs, *held)
    got = send(theirs, twin())
    items = reduce_level([mine, got], d, *low)
    as_rows = lambda x: x.reshape(-1, height, 128)
    items[0], *held = tie(items[0], *held)
    laid = lay(cap, nodes, [as_rows(x) for x in held])
    joined = tie(*items, *laid)
    items, laid, joined = list(joined[: len(items)]), joined[len(items) : -1], joined[-1]
    swapped = send(joined, twin())
    for level in upper:
        items = reduce_level(items, d, *level)
    *items, swapped = tie(*items, swapped)
    piece = tree(items, jnp.add)
    for level in upper[::-1]:
        piece = in_order(gather_level(piece, d, *level), d, *level)
    piece, swapped = tie(piece, swapped)
    blocks = gather_level(piece, d, *low)
    new_mem, more = merge(cap, laid, swapped, mem_t)
    *blocks, new_mem = tie(*blocks, new_mem)
    other = [send(x, twin()) for x in blocks]
    grad_norm, loss_sum, news = adam(
        jnp.stack([core, place(d, *low)]), [(0, len(blocks))], blocks, other,
        (gru_in, gru_hid, keys_values, tall_stack, squares, vectors) + moments)
    weight_sum = spread[-1, 0]

    def again(carry):
        r, _, mem_now = carry
        rows = spread_upper(lax.dynamic_index_in_dim(packed, r, 0, False), d)
        held = gather_level(rows, d, *low)
        *laid, joined = lay(cap, nodes, [as_rows(x) for x in held])
        mem_now, more = merge(cap, laid, send(joined, twin()), mem_now)
        return r + 1, more & (r + 1 < packed.shape[0]), mem_now

    if packed.shape[0] > 1:
        new_mem = lax.while_loop(lambda c: c[1], again, (jnp.int32(1), more, new_mem))[2]
    return (grad_norm, loss_sum, weight_sum, new_mem.T, *news)


def solution(mesh):
    split = P(AXES)
    placed = (split, split, P(AXES, None, None), P(AXES, None, None), split, split, split, P(AXES, None), split)
    return jax.shard_map(body, mesh=mesh, in_specs=placed + (P(),) * 20, out_specs=(P(),) * 22, check_vma=False)
```

```python
import math

import jax
import jax.numpy as jnp
from jax import lax
from jax.experimental import pallas as pl
from jax.experimental.pallas import tpu as pltpu
from jax.sharding import PartitionSpec as P

F32 = jnp.float32
BF = jnp.bfloat16
I32 = jnp.int32
NBR = 10
MEM = 172
PAD = 176
HALF = 86
HPAD = 88
STEP = 10
LEARN_RATE = 0.03
VECTOR_RATE = 0.3
BETA_ONE = 0.9
BETA_TWO = 0.999
ADAM_EPS = 1e-08
DECAY = 0.01
CLIP_AT = 0.005
TIME_RATE = 64.0
NORM_EPS = 1e-06
VMEM_CAP = 58 * 2**20


def params(limit=VMEM_CAP):
    return pltpu.CompilerParams(vmem_limit_bytes=limit)


def cost(us):
    return pl.CostEstimate(flops=int(us * 1e9), bytes_accessed=int(us * 3e6), transcendentals=0)


def nn(a, b):
    return lax.dot_general(a, b, (((1,), (0,)), ((), ())), preferred_element_type=F32)


def nt(a, b):
    return lax.dot_general(a, b, (((1,), (1,)), ((), ())), preferred_element_type=F32)


def zeros(rows, cols):
    return jnp.zeros((rows, cols), F32)


def rows_to(x, total):
    return jnp.concatenate([x, zeros(total - x.shape[0], x.shape[1])], axis=0)


def cols_to(x, total):
    return jnp.concatenate([x, zeros(x.shape[0], total - x.shape[1])], axis=1)


def split_rows(x):
    gap = zeros(HPAD - HALF, x.shape[1])
    return jnp.concatenate([x[:HALF], gap, x[HALF:], gap], axis=0)


def eye(n):
    return (lax.broadcasted_iota(I32, (n, n), 0) == lax.broadcasted_iota(I32, (n, n), 1)).astype(BF)


def turned(x):
    return nt(eye(x.shape[1]), x.astype(BF))


def gate_weights_kernel(gin, ghid, vec, wg, wh, vb):
    full = gin[...]
    for gate in range(3):
        rows = full[gate * MEM : (gate + 1) * MEM]
        parts = [cols_to(rows[:, q * MEM : (q + 1) * MEM], PAD) for q in range(4)]
        wg[pl.ds(gate * PAD, PAD), :] = rows_to(jnp.concatenate(parts, axis=1), PAD).astype(BF)
    hid = ghid[...]
    for gate in range(3):
        part = cols_to(rows_to(hid[:, gate * MEM : (gate + 1) * MEM], PAD), 256)
        wh[pl.ds(gate * PAD, PAD), :] = turned(part)[:PAD].astype(BF)
    cols = jnp.transpose(cols_to(rows_to(vec[...], 128), 256))
    for i in range(15):
        column = cols[:, i : i + 1]
        if i in (8, 9):
            column = split_rows(column[:MEM])
        wide = jnp.broadcast_to(column[:PAD], (PAD, 128))
        vb[i] = wide * (0.5 / math.pi) if i < 2 else wide


def gate_weights(gin, ghid, vec):
    outs = [jax.ShapeDtypeStruct((528, 704), BF), jax.ShapeDtypeStruct((528, 176), BF),
            jax.ShapeDtypeStruct((15, PAD, 128), F32)]
    return pl.pallas_call(
        gate_weights_kernel, out_shape=outs, compiler_params=params(), name="gate_weights", cost_estimate=cost(4),
    )(gin.T, ghid, vec)


def main_weights_kernel(gin, kv, tall, sq, vec, wgc, kvm, kvct, kvc, t0t, t0, t1t, t1, t2t, t2, s0t, s0, s1t, s1, steady):
    for gate in range(3):
        code = cols_to(rows_to(gin[gate * MEM : (gate + 1) * MEM, 2 * MEM : 3 * MEM], PAD), 256)
        wgc[:, gate * PAD : (gate + 1) * PAD] = turned(code)[:PAD].astype(BF)
    pairs = kv[...]
    both = turned(cols_to(pairs, 384))
    halves = jnp.concatenate([split_rows(both[:MEM]), split_rows(both[MEM : 2 * MEM])], axis=0)
    kvm[...] = cols_to(halves[:, :MEM], 256).astype(BF)
    code_rows = cols_to(halves[:, MEM:], 256)
    kvct[...] = code_rows[:, :PAD].astype(BF)
    kvc[...] = turned(code_rows)[:PAD].astype(BF)
    query = tall[0]
    query_t = cols_to(split_rows(query[:, :MEM]), 256)
    t0t[...] = query_t[:, :PAD].astype(BF)
    t0[...] = turned(query_t)[:PAD].astype(BF)
    for src, fwd, back in ((tall[1], t1t, t1), (tall[2], t2t, t2)):
        wide = rows_to(jnp.concatenate([cols_to(src[:, :MEM], PAD), cols_to(src[:, MEM:], PAD)], axis=1), PAD)
        fwd[...] = wide.astype(BF)
        back[...] = turned(cols_to(wide, 384))[: 2 * PAD].astype(BF)
    first = cols_to(split_rows(sq[:, 0, :]), 256)
    s0[...] = first[:, :PAD].astype(BF)
    s0t[...] = turned(first)[:PAD].astype(BF)
    second = cols_to(rows_to(sq[:, 1, :], PAD), 256)
    s1[...] = second[:, :PAD].astype(BF)
    s1t[...] = turned(second)[:PAD].astype(BF)
    phase_low = jnp.cos(jnp.transpose(cols_to(rows_to(vec[...], 128), 256))[:PAD, 1:2]).astype(BF).astype(F32)
    row_id = lax.broadcasted_iota(I32, (PAD, 128), 0)
    wide_phase = jnp.where(row_id < MEM, jnp.broadcast_to(phase_low, (PAD, 128)), 0.0).astype(BF)
    steady[...] = nn(cols_to(split_rows(query[:, MEM:]), PAD).astype(BF), wide_phase)


def main_weights(gin, kv, tall, sq, vec):
    bf = lambda *s: jax.ShapeDtypeStruct(s, BF)
    outs = [bf(176, 528), bf(352, 256), bf(352, 176), bf(176, 352),
            bf(176, 176), bf(176, 176), bf(176, 352), bf(352, 176), bf(176, 352), bf(352, 176),
            bf(176, 176), bf(176, 176), bf(176, 176), bf(176, 176), jax.ShapeDtypeStruct((PAD, 128), F32)]
    return pl.pallas_call(
        main_weights_kernel, out_shape=outs, compiler_params=params(), name="main_weights", cost_estimate=cost(5),
    )(gin.T, kv, jnp.transpose(tall, (0, 2, 1)), jnp.transpose(sq, (1, 0, 2)), vec)


def first_kernel(source, target, ticks, weights, out):
    tiles = source.shape[0]
    heights = out.shape[0] - 1
    nodes, orders = [], []
    for b in range(tiles):
        nodes += [source[b : b + 1, :], target[b : b + 1, :]]
        orders += [2 * ticks[b : b + 1, :], 2 * ticks[b : b + 1, :] + 1]
    count = 2 * tiles
    stack = jnp.concatenate([x.astype(F32) for x in nodes + orders], axis=0)
    cols = jnp.transpose(rows_to(stack, 128))
    lane = lax.broadcasted_iota(I32, (128, 128), 1)
    line = lax.broadcasted_iota(I32, (heights, 128), 0)
    total = zeros(heights, 384)
    for c in range(count):
        node = jnp.broadcast_to(cols[:, c : c + 1], (128, 128)).astype(I32)
        order = jnp.broadcast_to(cols[:, count + c : count + c + 1], (128, 128)).astype(I32)
        beaten = zeros(128, 128)
        for e in range(count):
            beaten = jnp.where((node == nodes[e]) & (orders[e] > order), 1.0, beaten)
        beaten = jnp.max(beaten, axis=1, keepdims=True)
        value = jnp.where(beaten > 0.0, 0, order + 1)
        here = (node & 127) == lane
        pick = lambda v: jnp.where(here, v, 0).astype(F32).astype(BF)
        right = jnp.concatenate([pick(value & 127), pick((value >> 7) & 127), pick(value >> 14)], axis=1)
        left = (jnp.broadcast_to(nodes[c] >> 7, (heights, 128)) == line).astype(BF)
        total = total + nn(left, right)
    out[0:heights, :] = total[:, :128] + 128.0 * total[:, 128:256] + 16384.0 * total[:, 256:] - 1.0
    out[heights : heights + 1, :] = jnp.broadcast_to(jnp.sum(weights[...], keepdims=True), (1, 128))


def first_latest(nodes, source, target, ticks, weights):
    return pl.pallas_call(
        first_kernel, out_shape=jax.ShapeDtypeStruct((nodes // 128 + 1, 128), F32),
        compiler_params=params(), name="latest", cost_estimate=cost(2),
    )(source, target, ticks, weights)


def copy_rows(out, at, tables, ids):
    for h, table in enumerate(tables):
        rows = jnp.concatenate([table[pl.ds(i, 1), :] for i in ids], axis=0)
        out[pl.ds(at, 16), 128 * h : 128 * h + 128] = rows.astype(BF)


def table_kernel(source, target, mem, ticks, far_left, far_right, own, wide, left, right, sems):
    step = pl.program_id(0)
    cols = mem.shape[1]
    steps = far_left.shape[0] // cols

    def copies(at):
        part = pl.ds(pl.multiple_of(at * cols, cols), cols)
        return [pltpu.make_async_copy(near.at[part], far.at[part], sems.at[h, at])
                for h, (near, far) in enumerate(((left, far_left), (right, far_right)))]

    @pl.when(step == 0)
    def _():
        wide[...] = jnp.zeros_like(wide)

    base = pl.multiple_of(step * cols, cols)
    wide[0:MEM, :] = mem[...].astype(BF).astype(F32)
    tick = ticks[...]
    for at, part in ((PAD, tick & 127), (PAD + 1, (tick >> 7) & 127), (PAD + 2, tick >> 14)):
        wide[at : at + 1, :] = part.astype(F32)
    unit = eye(256)
    for c in range(cols // 256):
        rows = nt(unit, wide[:, 256 * c : 256 * c + 256].astype(BF))
        left[pl.ds(base + 256 * c, 256), :] = rows[:, :128]
        right[pl.ds(base + 256 * c, 256), :] = rows[:, 128:]
    for copy in copies(step):
        copy.start()

    @pl.when(step == steps - 1)
    def _():
        def group(b, carry):
            for role, ids in enumerate((source, target)):
                def some(g, carry):
                    for v in range(2):
                        e = g * 32 + v * 16
                        at = pl.multiple_of(b * 256 + role * 128 + e, 16)
                        copy_rows(own, at, (left, right), [ids[b * 128 + e + u] for u in range(16)])
                    return carry

                lax.fori_loop(0, 4, some, 0)
            return carry

        lax.fori_loop(0, own.shape[0] // 256, group, 0)
        for at in range(steps):
            for copy in copies(at):
                copy.wait()


def build_table(source, target, mem_t, ticks):
    nodes = mem_t.shape[1]
    ends = 2 * source.shape[0]
    cols = 2048
    smem = pl.BlockSpec(memory_space=pltpu.SMEM)
    half = jax.ShapeDtypeStruct((nodes, 128), F32)
    fixed = lambda i: (0, 0)
    return pl.pallas_call(
        table_kernel,
        out_shape=[half, half, jax.ShapeDtypeStruct((ends, 256), BF)],
        grid=(nodes // cols,),
        in_specs=[smem, smem, pl.BlockSpec((MEM, cols), lambda i: (0, i)), pl.BlockSpec((1, cols), lambda i: (0, i))],
        out_specs=[pl.BlockSpec(memory_space=pl.ANY), pl.BlockSpec(memory_space=pl.ANY), pl.BlockSpec((ends, 256), fixed)],
        scratch_shapes=[pltpu.VMEM((256, cols), F32), pltpu.VMEM((nodes, 128), F32), pltpu.VMEM((nodes, 128), F32),
                        pltpu.SemaphoreType.DMA((2, nodes // cols))],
        compiler_params=params(), name="table", cost_estimate=cost(9),
    )(source, target, mem_t, ticks.reshape(1, nodes))


def near_kernel(chunk, ids, left, right, near):
    base = pl.program_id(0) * chunk

    def group(g, carry):
        for v in range(4):
            at = pl.multiple_of(g * 64 + v * 16, 16)
            copy_rows(near, at, (left, right), [ids[base + at + u] for u in range(16)])
        return carry

    lax.fori_loop(0, chunk // 64, group, 0)


def gather_near(ids, left, right):
    nears, chunk = ids.shape[0], ids.shape[0]
    whole = lambda a: pl.BlockSpec(a.shape, lambda i: (0, 0))
    return pl.pallas_call(
        lambda *r: near_kernel(chunk, *r),
        out_shape=jax.ShapeDtypeStruct((nears, 256), BF),
        grid=(nears // chunk,),
        in_specs=[pl.BlockSpec(memory_space=pltpu.SMEM), whole(left), whole(right)],
        out_specs=pl.BlockSpec((chunk, 256), lambda i: (i, 0)),
        compiler_params=params(), name="near", cost_estimate=cost(16),
    )(ids, left, right)


ROUND = 12582912.0
SIN = (6.283185005187988, -41.34165573120117, 81.60100555419922, -76.5497817993164, 39.536705017089844)
COS = (0.9999999403953552, -19.739171981811523, 64.9345932006836, -85.2403335571289, 56.24237823486328)


def cos_sin(turns):
    e = turns - ((turns + ROUND) - ROUND)
    w = 0.25 - jnp.abs(e)
    z = w * w
    c = w * (SIN[0] + z * (SIN[1] + z * (SIN[2] + z * (SIN[3] + z * SIN[4]))))
    s = COS[0] + z * (COS[1] + z * (COS[2] + z * (COS[3] + z * COS[4])))
    return c, jnp.where(e > 0.0, -s, s)


def sigmoid(x):
    return 0.5 * jnp.tanh(0.5 * x) + 0.5


BLOCK = 512
TILES = BLOCK // 256


def across(x):
    return jnp.concatenate([x] * (2 * TILES), axis=1)


def chunks(x, width=128):
    return [x[:, at : at + width] for at in range(0, x.shape[1], width)]


def both(x):
    return jnp.concatenate([c for c in chunks(x) for _ in range(2)], axis=1)


def mix(x, y):
    return jnp.concatenate([c for pair in zip(chunks(x), chunks(y)) for c in pair], axis=1)


def sources_of(x):
    return jnp.concatenate(chunks(x)[0::2], axis=1)


def targets_of(x):
    return jnp.concatenate(chunks(x)[1::2], axis=1)


def wide_rows(x, rows):
    return jnp.broadcast_to(x, (rows, x.shape[1]))


def gru_kernel(scale, cap, rounds, nodes, sources, targets, ticks_at, latest, own, source, target, ticks, edge, types, wg, wh, vb,
               msg, keep, ren, gap_out, packed, left, right, first, second):
    step = pl.program_id(0)
    own_t = nt(eye(256), own[...])
    seen = own_t[PAD : PAD + 1] + 128.0 * own_t[PAD + 1 : PAD + 2] + 16384.0 * own_t[PAD + 2 : PAD + 3]
    gap = (both(ticks[...].astype(F32)) - seen) * scale
    row_id = lax.broadcasted_iota(I32, (PAD, BLOCK), 0)
    own_x = jnp.where(row_id < MEM, own_t[:PAD], 0.0)
    msg[0:PAD, :] = own_x.astype(BF)
    msg[PAD : 2 * PAD, :] = mix(targets_of(own_x), sources_of(own_x)).astype(BF)
    edges = rows_to(edge[...].astype(F32) * types[...].astype(F32), PAD)
    msg[3 * PAD : 4 * PAD, :] = both(edges).astype(BF)
    gap_out[...] = wide_rows(gap, 8)
    gap16 = wide_rows(gap, 16)
    for st in range(PAD // 16):
        at = 16 * st
        for m in range(TILES):
            q = slice(256 * m, 256 * m + 256)
            rate, phase = vb[0, at : at + 16, :], vb[1, at : at + 16, :]
            x = jnp.concatenate([rate, rate], axis=1) * gap16[:, q] + jnp.concatenate([phase, phase], axis=1)
            c, s = cos_sin(x)
            msg[2 * PAD + at : 2 * PAD + at + 16, q] = c.astype(BF)
            keep[4, at : at + 16, q] = s
    gates = nn(wg[...], msg[...])
    hidden = nn(wh[...], msg[0:PAD, :])
    for st in range(PAD // 8):
        at = 8 * st
        o = own_x[at : at + 8]
        pre = [gates[g * PAD + at : g * PAD + at + 8] + across(vb[2 + g, at : at + 8, :]) for g in range(3)]
        hid = [hidden[g * PAD + at : g * PAD + at + 8] + across(vb[5 + g, at : at + 8, :]) for g in range(3)]
        u = sigmoid(pre[0] + hid[0])
        r = sigmoid(pre[1] + hid[1])
        n = jnp.tanh(pre[2] + r * hid[2])
        keep[0, at : at + 8, :] = u
        keep[1, at : at + 8, :] = r
        keep[2, at : at + 8, :] = n
        keep[3, at : at + 8, :] = hid[2]
        ren[at : at + 8, :] = (1.0 - u) * n + u * o
    numbers = mix(source[...], target[...]).astype(F32)
    low = jnp.concatenate([ren[128:MEM, :], numbers, zeros(255 - MEM, BLOCK)], axis=0)
    for role in range(2 * TILES):
        at = pl.multiple_of(step * BLOCK + 128 * role, 128)
        left[pl.ds(at, 128), :] = jnp.transpose(ren[0:128, 128 * role : 128 * role + 128])
        right[pl.ds(at, 128), :] = jnp.transpose(low[:, 128 * role : 128 * role + 128])

    @pl.when(step == pl.num_programs(0) - 1)
    def _():
        pack_rows(cap, rounds, nodes, sources, targets, ticks_at, latest, left, right, packed, first, second)


def pack_rows(cap, rounds, nodes, sources, targets, ticks, latest, left, right, out, first, second):
    def chunk(b, count):
        for role, ids in enumerate((sources, targets)):
            def some(g, count):
                for v in range(32):
                    e = b * 128 + g * 32 + v
                    i = b * 256 + role * 128 + g * 32 + v
                    won = latest[ids[e]] == 2 * ticks[e] + role
                    first[pl.ds(count, 1), :] = left[pl.ds(i, 1), :]
                    second[pl.ds(count, 1), :] = right[pl.ds(i, 1), :]
                    count = count + won.astype(I32)
                return count

            count = lax.fori_loop(0, 4, some, count)
        return count

    count = lax.fori_loop(0, sources.shape[0] // 128, chunk, jnp.int32(0))
    tail = cap // 2
    lane = lax.broadcasted_iota(I32, (1, 128), 1)
    for r in range(rounds):
        at = r * cap
        out[r, 0:cap, :] = first[at : at + cap, :]
        out[r, cap : cap + tail, :] = jnp.concatenate(
            [second[at : at + tail, 0:64], second[at + tail : at + cap, 0:64]], axis=1)
        here = jnp.clip(count - at, 0, cap)
        lines = []
        for q in range(-(-cap // 128)):
            numbers = jnp.transpose(second[at + 128 * q : at + 128 * q + 128, :])[MEM - 128 : MEM - 127]
            lines.append(jnp.where(lane + 128 * q < here, numbers, float(nodes)))
        lines.append(jnp.full((1, 128), here, I32).astype(F32))
        lines += [zeros(1, 128)] * (8 - len(lines))
        out[r, cap + tail :, :] = jnp.concatenate(lines, axis=0)


def gru(scale, cap, sources, targets, ticks, latest, own, edge_t, types, wg, wh, vb):
    ends, nodes = own.shape[0], latest.shape[0]
    blocks = ends // BLOCK
    rounds = ends // cap + 1
    spare = rounds * cap + 128
    whole = lambda a: pl.BlockSpec(a.shape, lambda i: (0,) * len(a.shape))
    lanes = lambda: pl.BlockSpec((1, BLOCK // 2), lambda i: (0, i))
    smem = pl.BlockSpec(memory_space=pltpu.SMEM)
    row = lambda x: x.reshape(1, -1)
    packed = jax.ShapeDtypeStruct((rounds, cap + cap // 2 + 8, 128), F32)
    return pl.pallas_call(
        lambda *r: gru_kernel(scale, cap, rounds, nodes, *r),
        out_shape=[jax.ShapeDtypeStruct((4 * PAD, ends), BF), jax.ShapeDtypeStruct((5, PAD, ends), F32),
                   jax.ShapeDtypeStruct((PAD, ends), F32), jax.ShapeDtypeStruct((8, ends), F32), packed],
        grid=(blocks,),
        in_specs=[smem] * 4 + [pl.BlockSpec((BLOCK, 256), lambda i: (i, 0)), lanes(), lanes(), lanes(),
                  pl.BlockSpec((MEM, BLOCK // 2), lambda i: (0, i)), lanes(), whole(wg), whole(wh), whole(vb)],
        out_specs=[pl.BlockSpec((4 * PAD, BLOCK), lambda i: (0, i)), pl.BlockSpec((5, PAD, BLOCK), lambda i: (0, 0, i)),
                   pl.BlockSpec((PAD, BLOCK), lambda i: (0, i)), pl.BlockSpec((8, BLOCK), lambda i: (0, i)), whole(packed)],
        scratch_shapes=[pltpu.VMEM((ends, 128), F32), pltpu.VMEM((ends, 128), F32),
                        pltpu.VMEM((spare, 128), F32), pltpu.VMEM((spare, 128), F32)],
        compiler_params=params(), name="gru", cost_estimate=cost(10),
    )(sources, targets, ticks, latest, own, row(sources), row(targets), row(ticks), edge_t, types, wg, wh, vb)


UNROLL = 10
ROWS = 2944
VECTORS = 2904
GELU_C = math.sqrt(2.0 / math.pi)


def gelu_parts(x):
    sq = x * x
    t = jnp.tanh(GELU_C * (x + 0.044715 * (sq * x)))
    half = 0.5 * (1.0 + t)
    slope = half + (0.5 * x) * (1.0 - t * t) * (GELU_C + (GELU_C * 3.0 * 0.044715) * sq)
    return x * half, slope


def fold(x):
    total, *others = chunks(x)
    for other in others:
        total = total + other
    return total


def main_kernel(scale, core, near, gaps_t, ticks, msg, keep, ren, gap_own, labels, weights, total,
                wgc, kvm, kvct, kvc, t0t, t0, t1t, t1, t2t, t2, s0t, s0, s1t, s1, steady, vb,
                mine, theirs,
                loss, pair, code, dcode, soft, back, mean, d_query_at, grads, g_in, g_kv, g_one, g_dec, g_qo, g_th, vacc):
    step = pl.program_id(0)
    inv_size = HALF ** -0.5

    @pl.when(step == 0)
    def _():
        for ref in (g_in, g_kv, g_one, g_dec, g_qo, g_th, vacc, loss):
            ref[...] = jnp.zeros_like(ref)

    tick2 = both(ticks[...].astype(F32))
    renewed = ren[...]
    ren_low = renewed.astype(BF)
    queries = nn(t0t[...], ren_low) + across(vb[8] + steady[...])
    def each(one):
        def some(g, carry):
            for v in range(UNROLL):
                one(g * UNROLL + v)
            return carry

        lax.fori_loop(0, NBR // UNROLL, some, 0)

    def look(j):
        gap16 = wide_rows((tick2 - gaps_t[pl.ds(j, 1), :].astype(F32)) * scale, 16)
        for st in range(PAD // 16):
            at = 16 * st
            for m in range(TILES):
                q = slice(256 * m, 256 * m + 256)
                rate, phase = vb[0, at : at + 16, :], vb[1, at : at + 16, :]
                x = jnp.concatenate([rate, rate], axis=1) * gap16[:, q] + jnp.concatenate([phase, phase], axis=1)
                c, s = cos_sin(x)
                code[j, at : at + 16, q] = c.astype(BF)
                dcode[j, at : at + 16, q] = s
        pair[j] = nt(kvm[...], near[j]) + nn(kvct[...], code[j])
        for h in range(2):
            acc = zeros(8, BLOCK)
            for st in range(HPAD // 8):
                at = HPAD * h + 8 * st
                acc = acc + pair[j, at : at + 8, :] * queries[at : at + 8]
            soft[2 * j + h] = wide_rows(jnp.sum(acc, axis=0, keepdims=True) * inv_size, 8)

    each(look)
    for h in range(2):
        top = soft[h]
        for j in range(1, NBR):
            top = jnp.maximum(top, soft[2 * j + h])
        norm = zeros(8, BLOCK)
        for j in range(NBR):
            e = jnp.exp(soft[2 * j + h] - top)
            soft[2 * j + h] = e
            norm = norm + e
        inv = 1.0 / norm
        for j in range(NBR):
            soft[2 * j + h] = soft[2 * j + h] * inv
    att = []
    for st in range(PAD // 8):
        at = 8 * st
        h = 0 if at < HPAD else 1
        acc = across(vb[9, at : at + 8, :])
        for j in range(NBR):
            acc = acc + soft[2 * j + h] * pair[j, PAD + at : PAD + at + 8, :]
        att.append(acc)
    att_low = jnp.concatenate(att, axis=0).astype(BF)
    projected = nn(s0t[...], att_low) + across(vb[10])
    mlp_in = jnp.concatenate([projected.astype(BF), ren_low], axis=0)
    inner = nn(t1t[...], mlp_in) + across(vb[11])
    act, act_slope = gelu_parts(inner)
    act_low = act.astype(BF)
    emb_low = (nn(s1t[...], act_low) + across(vb[12])).astype(BF)
    dec_in = jnp.concatenate([sources_of(emb_low), targets_of(emb_low)], axis=0)
    out_row = jnp.concatenate([vb[14]] * TILES, axis=1)
    dec_pre = nn(t2t[...], dec_in) + jnp.concatenate([vb[13]] * TILES, axis=1)
    dec_act, dec_slope = gelu_parts(dec_pre)
    logit = jnp.sum(dec_act * out_row, axis=0, keepdims=True)
    label = labels[...].astype(F32)
    tail = jnp.exp(-jnp.abs(logit))
    plus = jnp.maximum(logit, 0.0) + jnp.log1p(tail)
    loss[...] += fold(weights[...] * (plus - label * logit))
    d_logit = weights[...] / total[:, 0:1] * (sigmoid(logit) - label)
    d_out = d_logit * dec_act
    d_dec = (d_logit * out_row) * dec_slope
    d_dec_low = d_dec.astype(BF)
    g_dec[...] += nt(d_dec_low, dec_in)
    d_dec_in = nn(t2[...], d_dec_low)
    d_emb = mix(d_dec_in[:PAD], d_dec_in[PAD:])
    d_emb_low = d_emb.astype(BF)
    g_th[:, 0:256] += jnp.concatenate([nt(act_low, d_emb_low), zeros(PAD, 256 - PAD)], axis=1)
    d_inner = nn(s1[...], d_emb_low) * act_slope
    d_inner_low = d_inner.astype(BF)
    g_one[...] += nt(d_inner_low, mlp_in)
    d_mlp = nn(t1[...], d_inner_low)
    d_proj = d_mlp[:PAD]
    d_proj_low = d_proj.astype(BF)
    g_qo[:, 256:512] += jnp.concatenate([nt(att_low, d_proj_low), zeros(PAD, 256 - PAD)], axis=1)
    d_att = nn(s0[...], d_proj_low)
    d_query_at[...] = jnp.zeros_like(d_query_at)
    mean[...] = jnp.zeros_like(mean)

    def weigh(j):
        for h in range(2):
            acc = zeros(8, BLOCK)
            for st in range(HPAD // 8):
                at = HPAD * h + 8 * st
                acc = acc + pair[j, PAD + at : PAD + at + 8, :] * d_att[at : at + 8]
            wide = wide_rows(jnp.sum(acc, axis=0, keepdims=True), 8)
            back[2 * j + h] = wide
            mean[h] += wide * soft[2 * j + h]

    def learn(j):
        share = [soft[2 * j + h] for h in range(2)]
        slope = [(share[h] * inv_size) * (back[2 * j + h] - mean[h]) for h in range(2)]
        for st in range(PAD // 8):
            at = 8 * st
            d_query_at[at : at + 8, :] += slope[at >= HPAD] * pair[j, at : at + 8, :]
        for st in range(2 * PAD // 16):
            parts = []
            for half in range(2):
                at = 16 * st + 8 * half
                if at < PAD:
                    parts.append(slope[at >= HPAD] * queries[at : at + 8])
                else:
                    parts.append(share[at - PAD >= HPAD] * d_att[at - PAD : at - PAD + 8])
            grads[j, 16 * st : 16 * st + 16, :] = jnp.concatenate(parts, axis=0).astype(BF)
        d_code = nn(kvc[...], grads[j])
        gap8 = wide_rows((tick2 - gaps_t[pl.ds(j, 1), :].astype(F32)) * scale, 8)
        for st in range(PAD // 8):
            at = 8 * st
            d_arg = d_code[at : at + 8] * dcode[j, at : at + 8, :]
            vacc[0, at : at + 8, :] += fold(d_arg * gap8)
            vacc[1, at : at + 8, :] += fold(d_arg)
        g_kv[:, 0:256] += nn(grads[j], near[j])
        g_kv[:, 256 : 256 + PAD] += nt(grads[j], code[j])

    each(weigh)
    each(learn)
    d_query = d_query_at[...]
    d_q_low = d_query.astype(BF)
    g_qo[:, 0:256] += jnp.concatenate([nt(d_q_low, ren_low), zeros(PAD, 256 - PAD)], axis=1)
    d_ren = d_mlp[PAD:] + nn(t0[...], d_q_low)
    own_x = msg[0:PAD, :].astype(F32)
    u, r, n, hn = keep[0], keep[1], keep[2], keep[3]
    d_u = d_ren * (own_x - n) * (u * (1.0 - u))
    d_n = d_ren * (1.0 - u) * (1.0 - n * n)
    d_r = d_n * hn * (r * (1.0 - r))
    d_h = d_n * r
    gates = jnp.concatenate([d_u, d_r, d_n], axis=0).astype(BF)
    g_in[...] += nt(gates, msg[...])
    g_th[:, 256:512] += jnp.concatenate([nt(msg[0:PAD, :], d_h.astype(BF)), zeros(PAD, 256 - PAD)], axis=1)
    d_arg = nn(wgc[...], gates) * keep[4]
    vacc[0] += fold(d_arg * gap_own[0:1, :])
    vacc[1] += fold(d_arg)
    for i, item in ((2, d_u), (3, d_r), (4, d_n), (7, d_h), (8, d_query), (9, d_att), (10, d_proj), (11, d_inner),
                    (12, d_emb), (15, d_q_low.astype(F32))):
        vacc[i] += fold(item)
    vacc[13] += fold(d_dec)
    vacc[14] += fold(d_out)

    def finish(ga, gb):
        def panels(out, x):
            rows, lanes = x.shape
            whole = lanes // 128
            for c in range(whole):
                out[rows * c : rows * c + rows, :] = x[:, 128 * c : 128 * c + 128]
            last = x[:, 128 * whole :]
            out[rows * whole : rows * whole + rows // 2, :] = jnp.concatenate([last[: rows // 2], last[rows // 2 :]], axis=1)

        panels(gb, g_in[...])
        lane = lax.broadcasted_iota(I32, (PAD, 128), 1)
        vecs = zeros(PAD, 128)
        for i in range(16):
            column = jnp.sum(vacc[i], axis=1, keepdims=True)
            vecs = jnp.where(lane == i, column, vecs)
        flat = jnp.transpose(jnp.concatenate([vecs, zeros(256 - PAD, 128)], axis=0))
        gb[VECTORS : VECTORS + 16, :] = flat[0:16, 0:128]
        gb[VECTORS + 16 : VECTORS + 32, :] = flat[0:16, 128:256]
        gb[VECTORS + 32 :, :] = zeros(ROWS - VECTORS - 32, 128)
        units = [g_kv[at : at + PAD, c : c + PAD] for at in (0, PAD) for c in (0, 256)]
        units += [g_one[...], g_dec[...]]
        units += [ref[:, c : c + PAD] for ref in (g_qo, g_th) for c in (0, 256)]
        panels(ga, jnp.concatenate(units, axis=1))
        ga[VECTORS:, :] = rows_to(loss[...], ROWS - VECTORS)

    @pl.when((step == pl.num_programs(0) - 1) & (core[0] == 0))
    def _():
        finish(mine, theirs)

    @pl.when((step == pl.num_programs(0) - 1) & (core[0] != 0))
    def _():
        finish(theirs, mine)


def main(scale, near, near_ticks, ticks, msg, keep, ren, gap_own, labels, weights, total, core, w):
    ends = ren.shape[1]
    blocks = ends // BLOCK
    whole = lambda a: pl.BlockSpec(a.shape, lambda i: (0,) * len(a.shape))
    lanes = lambda: pl.BlockSpec((1, BLOCK // 2), lambda i: (0, i))
    return pl.pallas_call(
        lambda *r: main_kernel(scale, *r),
        out_shape=[jax.ShapeDtypeStruct((ROWS, 128), F32), jax.ShapeDtypeStruct((ROWS, 128), F32)],
        grid=(blocks,),
        in_specs=[pl.BlockSpec(memory_space=pltpu.SMEM), pl.BlockSpec((NBR, BLOCK, 256), lambda i: (0, i, 0)), pl.BlockSpec((NBR, BLOCK), lambda i: (0, i)), lanes(),
                  pl.BlockSpec((4 * PAD, BLOCK), lambda i: (0, i)), pl.BlockSpec((5, PAD, BLOCK), lambda i: (0, 0, i)),
                  pl.BlockSpec((PAD, BLOCK), lambda i: (0, i)), pl.BlockSpec((8, BLOCK), lambda i: (0, i)), lanes(), lanes(),
                  pl.BlockSpec((1, 128), lambda i: (0, 0))] + [whole(a) for a in w],
        out_specs=[pl.BlockSpec((ROWS, 128), lambda i: (0, 0)), pl.BlockSpec((ROWS, 128), lambda i: (0, 0))],
        scratch_shapes=[pltpu.VMEM((1, 128), F32), pltpu.VMEM((NBR, 352, BLOCK), F32), pltpu.VMEM((NBR, PAD, BLOCK), BF), pltpu.VMEM((NBR, PAD, BLOCK), F32),
                        pltpu.VMEM((20, 8, BLOCK), F32), pltpu.VMEM((20, 8, BLOCK), F32), pltpu.VMEM((2, 8, BLOCK), F32),
                        pltpu.VMEM((PAD, BLOCK), F32), pltpu.VMEM((NBR, 352, BLOCK), BF),
                        pltpu.VMEM((528, 704), F32), pltpu.VMEM((352, 512), F32), pltpu.VMEM((PAD, 352), F32),
                        pltpu.VMEM((PAD, 352), F32), pltpu.VMEM((PAD, 512), F32), pltpu.VMEM((PAD, 512), F32),
                        pltpu.VMEM((16, PAD, 128), F32)],
        compiler_params=params(), name="main", cost_estimate=cost(35),
    )(core, near.reshape(NBR, ends, 256), near_ticks, ticks, msg, keep, ren, gap_own, labels, weights, total, *w)


def room(nodes, devices):
    return -(-(nodes * 9) // (devices * 8 * 16)) * 16


def turned_exactly(x):
    high = x.astype(BF)
    rest = x - high.astype(F32)
    middle = rest.astype(BF)
    low = (rest - middle.astype(F32)).astype(BF)
    unit = eye(x.shape[1])
    return (nt(unit, high) + nt(unit, middle)) + nt(unit, low)


def fetch_numbers(cap, rows, whole, numbers, sem):
    whole[...] = rows[:, cap + cap // 2 :, :].astype(I32)
    copy = pltpu.make_async_copy(whole, numbers, sem)
    copy.start()
    return copy


def lay_rows(cap, rows, numbers, left, right, second):
    tail = cap // 2

    def block(q, most):
        half = rows[q, cap : cap + tail, :]
        second[0:tail, :] = half
        second[tail:cap, :] = jnp.concatenate([half[:, 64:], half[:, :64]], axis=1)
        here = numbers[q, -(-cap // 128), 0]

        def some(g, carry):
            few = numbers.at[q, lax.shift_right_logical(g, 3), pl.ds((g & 7) * 16, 16)]
            for v in range(16):
                i = g * 16 + v
                node = few[v]
                left[pl.ds(node, 1), :] = rows[q, pl.ds(i, 1), :]
                right[pl.ds(node, 1), :] = second[pl.ds(i, 1), :]
            return carry

        lax.fori_loop(0, lax.div(here + 15, 16), some, 0)
        return jnp.maximum(most, here)

    return lax.fori_loop(0, rows.shape[0], block, jnp.int32(0))


def lay_kernel(cap, count, *refs):
    arrays, (left, right, most, joined, second, sems), rest = refs[:count], refs[count : count + 6], refs[count + 6 :]
    wholes, lists = rest[:count], rest[count:]
    copies = [fetch_numbers(cap, arrays[a], wholes[a], lists[a], sems.at[a]) for a in range(count)]
    right[...] = jnp.full_like(right, -1.0)
    for a, rows in enumerate(arrays):
        blocks = rows.shape[0]
        joined[a * blocks : (a + 1) * blocks] = rows[...]
    largest = jnp.int32(0)
    for a, rows in enumerate(arrays):
        copies[a].wait()
        largest = jnp.maximum(largest, lay_rows(cap, rows, lists[a], left, right, second))
    most[0] = largest


def lay(cap, nodes, arrays):
    vm, smem = pl.BlockSpec(memory_space=pltpu.VMEM), pl.BlockSpec(memory_space=pltpu.SMEM)
    table = jax.ShapeDtypeStruct((nodes + 8, 128), F32)
    count = len(arrays)
    blocks, height, _ = arrays[0].shape
    return pl.pallas_call(
        lambda *r: lay_kernel(cap, count, *r),
        out_shape=[table, table, jax.ShapeDtypeStruct((1,), I32), jax.ShapeDtypeStruct((count * blocks, height, 128), F32)],
        in_specs=[vm] * count, out_specs=[vm, vm, smem, vm],
        scratch_shapes=[pltpu.VMEM((cap, 128), F32), pltpu.SemaphoreType.DMA((count,))]
        + [kind((blocks, 8, 128), I32) for kind in (pltpu.VMEM, pltpu.SMEM) for _ in arrays],
        compiler_params=params(), name="lay", cost_estimate=cost(14),
    )(*arrays)


def merge_kernel(cap, rows, far_left, far_right, before, mem, out, full, left, right, second, sems, whole, numbers):
    step = pl.program_id(0)

    @pl.when(step == 0)
    def _():
        copies = [pltpu.make_async_copy(far_left, left, sems.at[0]), pltpu.make_async_copy(far_right, right, sems.at[1])]
        for copy in copies:
            copy.start()
        copies.append(fetch_numbers(cap, rows, whole, numbers, sems.at[2]))
        for copy in copies:
            copy.wait()
        most = lay_rows(cap, rows, numbers, left, right, second)
        full[0] = (jnp.maximum(most, before[0]) == cap).astype(I32)

    cols = mem.shape[1]
    base = pl.multiple_of(step * cols, cols)
    for c in range(cols // 256):
        at = base + 256 * c
        s = slice(256 * c, 256 * c + 256)
        top = turned_exactly(left[pl.ds(at, 256), :])
        low = turned_exactly(right[pl.ds(at, 256), :])
        fresh = low[MEM - 128 : MEM - 127] >= 0.0
        out[0:128, s] = jnp.where(fresh, top, mem[0:128, s])
        out[128:MEM, s] = jnp.where(fresh, low[: MEM - 128], mem[128:MEM, s])


def merge(cap, laid, rows, mem_t):
    nodes = mem_t.shape[1]
    cols = 2048
    part = pl.BlockSpec((MEM, cols), lambda i: (0, i))
    smem, far = pl.BlockSpec(memory_space=pltpu.SMEM), pl.BlockSpec(memory_space=pl.ANY)
    new, full = pl.pallas_call(
        lambda *r: merge_kernel(cap, *r),
        out_shape=[jax.ShapeDtypeStruct((MEM, nodes), F32), jax.ShapeDtypeStruct((1,), I32)],
        grid=(nodes // cols,),
        in_specs=[pl.BlockSpec(rows.shape, lambda i: (0, 0, 0)), far, far, smem, part],
        out_specs=[part, smem],
        scratch_shapes=[pltpu.VMEM((nodes + 8, 128), F32), pltpu.VMEM((nodes + 8, 128), F32), pltpu.VMEM((cap, 128), F32),
                        pltpu.SemaphoreType.DMA((3,))] + [kind((rows.shape[0], 8, 128), I32) for kind in (pltpu.VMEM, pltpu.SMEM)],
        compiler_params=params(), name="merge", cost_estimate=cost(18),
    )(rows, *laid, mem_t)
    return new, full[0] > 0


def move(param, one, two, grad, factor, rate, decay):
    clipped = grad * factor
    one = BETA_ONE * one + (1.0 - BETA_ONE) * clipped
    two = BETA_TWO * two + (1.0 - BETA_TWO) * clipped * clipped
    step = (one * (1.0 / (1.0 - BETA_ONE**STEP))) / (jnp.sqrt(two * (1.0 / (1.0 - BETA_TWO**STEP))) + ADAM_EPS)
    return param - rate * (step + decay * param), one, two


def unsplit(x, axis):
    take = lambda a, b: lax.slice_in_dim(x, a, b, axis=axis)
    return jnp.concatenate([take(0, HALF), take(HPAD, HPAD + HALF)], axis=axis)


def adam_kernel(parts, where, *refs):
    count = sum(n for _, n in parts)
    mine, other = refs[:count], refs[count : 2 * count]
    refs = refs[2 * count :]
    far, out, (norm_out, loss_out) = refs[:18], refs[18:36], refs[36:38]
    a, b, g_gin, g_hid, g_kv, g_tall, g_sq, g_vec = refs[38:46]
    state, sems_in, sems_out = refs[46:64], refs[64], refs[65]
    fetches = [pltpu.make_async_copy(far[i], state[i], sems_in.at[i]) for i in range(18)]
    stores = [pltpu.make_async_copy(state[i], out[i], sems_out.at[i]) for i in range(18)]
    for i in (5, 3, 0, 6, 12, 1, 7, 13, 2, 8, 14, 9, 15, 4, 10, 16, 11, 17):
        fetches[i].start()
    core = where[0]
    at_block = 0
    for p, (first, n) in enumerate(parts):
        height = mine[at_block].shape[0]
        for k in range(n):
            at = pl.multiple_of(first + (where[1 + p] ^ k) * height, 8)
            one, two = mine[at_block], other[at_block]
            at_block += 1

            @pl.when(core == 0)
            def _():
                a[pl.ds(at, height), :] = one[...]
                b[pl.ds(at, height), :] = two[...]

            @pl.when(core != 0)
            def _():
                b[pl.ds(at, height), :] = one[...]
                a[pl.ds(at, height), :] = two[...]

    def panels(ref, rows, lanes):
        whole = lanes // 128
        parts = [ref[c * rows : (c + 1) * rows, :] for c in range(whole)]
        last = ref[whole * rows : whole * rows + rows // 2, :]
        return jnp.concatenate(parts + [jnp.concatenate([last[:, :64], last[:, 64:]], axis=0)], axis=1)

    vec, tall = state[5], state[3]
    wide = panels(b, 528, 704)
    gates = []
    for g in range(3):
        rows = wide[PAD * g : PAD * g + MEM]
        gates.append(jnp.concatenate([rows[:, PAD * q : PAD * q + MEM] for q in range(4)], axis=1))
    g_gin[...] = jnp.concatenate(gates, axis=0)
    vecs = jnp.concatenate([b[VECTORS : VECTORS + 16, :], b[VECTORS + 16 : VECTORS + 32, :]], axis=1)
    units = panels(a, PAD, 12 * PAD)
    unit = lambda i: units[:, PAD * i : PAD * i + MEM]
    kv = jnp.concatenate([jnp.concatenate([unsplit(unit(2 * i), 0), unsplit(unit(2 * i + 1), 0)], axis=1) for i in range(2)], axis=0)
    g_kv[...] = jnp.transpose(rows_to(cols_to(kv, 384), 384))[: 2 * MEM, : 2 * MEM]
    for i in (1, 2):
        g_tall[i] = jnp.concatenate([unit(2 + 2 * i)[:MEM], unit(3 + 2 * i)[:MEM]], axis=1)
    sum_dq = unsplit(jnp.transpose(rows_to(vecs, 128))[:PAD, 15:16], 0)
    fetches[5].wait()
    fetches[3].wait()
    phase = vec[1:2, :]
    phase_low = jnp.cos(phase).astype(BF).astype(F32)
    g_tall[0] = jnp.concatenate([unsplit(unit(8), 0), sum_dq * phase_low], axis=1)
    g_sq[0] = unsplit(unit(9), 0)
    g_sq[1] = unit(10)[:MEM]
    shared = jnp.transpose(rows_to(cols_to(g_gin[0 : 2 * MEM, 0:MEM], 256), 384))[:MEM, : 2 * MEM]
    g_hid[...] = jnp.concatenate([shared, unit(11)[:MEM]], axis=1)
    query_low = tall[0][:, MEM:].astype(BF).astype(F32)
    phase_in = jnp.sum(query_low * sum_dq, axis=0, keepdims=True)
    row = lambda i: vecs[i : i + 1, :MEM]
    g_vec[...] = jnp.concatenate(
        [row(0), row(1) - jnp.sin(phase) * phase_in, row(2), row(3), row(4), row(2), row(3), row(7),
         unsplit(vecs[8:9], 1), unsplit(vecs[9:10], 1)] + [row(i) for i in range(10, 15)], axis=0)
    total = jnp.zeros((1, 1), F32)
    for ref in (g_gin, g_hid, g_kv, g_vec):
        total += jnp.sum(ref[...] * ref[...], keepdims=True)
    for ref in (g_tall, g_sq):
        for i in range(ref.shape[0]):
            total += jnp.sum(ref[i] * ref[i], keepdims=True)
    norm = jnp.sqrt(total)
    factor = jnp.minimum(1.0, CLIP_AT / (norm + NORM_EPS))
    norm_out[...] = norm
    loss_out[...] = jnp.sum(a[VECTORS : VECTORS + 1, :], keepdims=True)
    for i, grad in enumerate((g_gin, g_hid, g_kv, g_tall, g_sq, g_vec)):
        rate, decay = (VECTOR_RATE, 0.0) if i == 5 else (LEARN_RATE, DECAY)
        new = param, one, two = state[i], state[6 + i], state[12 + i]
        for at in (i, 6 + i, 12 + i):
            if at not in (3, 5):
                fetches[at].wait()
        if i == 4:
            for j in range(2):
                made = move(param[:, j, :], one[:, j, :], two[:, j, :], grad[j], factor, rate, decay)
                for ref, value in zip(new, made):
                    ref[:, j, :] = value
        elif len(param.shape) == 3:
            for j in range(param.shape[0]):
                made = move(param[j], one[j], two[j], grad[j], factor, rate, decay)
                for ref, value in zip(new, made):
                    ref[j] = value
        else:
            rows = param.shape[0]
            for at in range(0, rows, 16):
                s = slice(at, min(at + 16, rows))
                made = move(param[s], one[s], two[s], grad[s], factor, rate, decay)
                for ref, value in zip(new, made):
                    ref[s] = value
        for at in (i, 6 + i, 12 + i):
            stores[at].start()
    for store in stores:
        store.wait()


def adam(where, parts, mine, other, state):
    swap = lambda x: jnp.transpose(x, (0, 2, 1))
    def ready(group):
        gin, hid, kv, tall, sq, vec = group
        return [gin.T, hid, kv, swap(tall), jnp.transpose(sq, (1, 0, 2)), vec]
    state = ready(state[0:6]) + ready(state[6:12]) + ready(state[12:18])
    count = len(mine)
    shapes = [x.shape for x in state[:6]]
    shapes[4] = (2, MEM, MEM)
    vm, far = pl.BlockSpec(memory_space=pltpu.VMEM), pl.BlockSpec(memory_space=pl.ANY)
    outs = [jax.ShapeDtypeStruct(x.shape, F32) for x in state] + [jax.ShapeDtypeStruct((1, 1), F32)] * 2
    out = pl.pallas_call(
        lambda *r: adam_kernel(parts, *r),
        out_shape=outs,
        in_specs=[pl.BlockSpec(memory_space=pltpu.SMEM)] + [vm] * (2 * count) + [far] * 18,
        out_specs=[far] * 18 + [vm] * 2,
        scratch_shapes=[pltpu.VMEM((ROWS, 128), F32)] * 2 + [pltpu.VMEM(s, F32) for s in shapes]
        + [pltpu.VMEM(x.shape, F32) for x in state] + [pltpu.SemaphoreType.DMA((18,))] * 2,
        compiler_params=params(), name="adam", cost_estimate=cost(14),
    )(where, *mine, *other, *state)
    back = lambda group: [group[0].T, group[1], group[2], swap(group[3]), jnp.transpose(group[4], (1, 0, 2)), group[5]]
    return out[18].reshape(()), out[19].reshape(()), back(out[0:6]) + back(out[6:12]) + back(out[12:18])


AXES = ("dp", "rep")


def levels(size):
    found, stride = [], 1
    while size > 1:
        n = size if size <= 8 else 4
        found.append((stride, n))
        stride, size = stride * n, size // n
    return found


def peers(stride, k):
    dp, rep = lax.axis_size("dp"), lax.axis_size("rep")
    return [(d * rep + r, (d ^ (k * stride)) * rep + r) for d in range(dp) for r in range(rep)]


def twin():
    dp, rep = lax.axis_size("dp"), lax.axis_size("rep")
    return [(d * rep + r, d * rep + (rep - 1 - r)) for d in range(dp) for r in range(rep)]


def send(x, pairs):
    return lax.ppermute(x, AXES, pairs)


def tree(items, join):
    while len(items) > 1:
        items = [join(items[i], items[i + 1]) for i in range(0, len(items), 2)]
    return items[0]


def place(d, stride, n):
    return lax.rem(lax.div(d, stride), n)


def reduce_level(items, d, stride, n):
    c = place(d, stride, n)
    rows = items[0].shape[0] // n
    piece = lambda k: tree([lax.dynamic_slice_in_dim(x, (c ^ k) * rows, rows, 0) for x in items], jnp.add)
    return [piece(0)] + [send(piece(k), peers(stride, k)) for k in range(1, n)]


def gather_level(x, d, stride, n):
    return [x] + [send(x, peers(stride, k)) for k in range(1, n)]


def in_order(pieces, d, stride, n):
    c = place(d, stride, n)
    lines = []
    for i in range(n):
        line = pieces[i]
        for k in range(n):
            if k != i:
                line = jnp.where((c ^ k) == i, pieces[k], line)
        lines.append(line)
    return jnp.concatenate(lines, axis=0)


def spread_latest(x, d):
    nodes = lax.broadcasted_iota(I32, x.shape, 0) < x.shape[0] - 1
    join = lambda p, q: jnp.where(nodes, jnp.maximum(p, q), p + q)
    x = join(x, send(x, twin()))
    for stride, n in levels(lax.axis_size("dp")):
        x = tree(gather_level(x, d, stride, n), join)
    return x


def spread_upper(x, d):
    for level in levels(lax.axis_size("dp"))[:0:-1]:
        x = jnp.concatenate(gather_level(x, d, *level), axis=0)
    return x


def tie(*xs):
    return lax.optimization_barrier(xs)


def body(source, target, neighbours, neighbour_ticks, event_ticks, event_types, labels, edge_feats, weights, memory,
         node_ticks, gru_in, gru_hid, keys_values, tall_stack, squares, vectors, *moments):
    events = event_ticks.shape[0]
    nodes = memory.shape[0]
    devices = lax.axis_size("dp") * lax.axis_size("rep")
    d, core = lax.axis_index("dp"), lax.axis_index("rep")
    scale = TIME_RATE / (events * devices)
    tiles = events // 128
    order = lambda x: jnp.transpose(x, (2, 1, 0)).reshape(NBR, 2, tiles, 128).transpose(0, 2, 1, 3).reshape(NBR, 2 * events)
    near_ids = order(neighbours).reshape(-1)
    near_ticks = order(neighbour_ticks)
    row = lambda x: x.reshape(1, events)
    lines = lambda x: x.reshape(tiles, 128)
    mem_t = memory.T
    spread = first_latest(nodes, lines(source), lines(target), lines(event_ticks), lines(weights))
    spread = spread_latest(spread, d)
    latest = spread[:-1].reshape(-1).astype(I32)
    wg, wh, vb = gate_weights(gru_in, gru_hid, vectors)
    left, right, own = build_table(source, target, mem_t, node_ticks)
    cap = room(nodes, devices)
    msg, keep, ren, gap_own, packed = gru(
        scale, cap, source, target, event_ticks, latest, own, edge_feats.T, row(event_types), wg, wh, vb)
    height = packed.shape[1]
    low, *upper = levels(lax.axis_size("dp"))
    first_round, left, right = tie(packed[0], left, right)
    rows = spread_upper(first_round, d)
    near = gather_near(near_ids, left, right)
    rows, near, vec_late = tie(rows, near, vectors)
    w = main_weights(gru_in, keys_values, tall_stack, squares, vec_late)
    held = gather_level(rows, d, *low)
    mine, theirs = main(scale, near, near_ticks, row(event_ticks), msg, keep, ren, gap_own, row(labels), row(weights),
                        spread[-1:], core.reshape(1), list(w) + [vb])
    mine, theirs, *held = tie(mine, theirs, *held)
    got = send(theirs, twin())
    items = reduce_level([mine, got], d, *low)
    as_rows = lambda x: x.reshape(-1, height, 128)
    items[0], *held = tie(items[0], *held)
    laid = lay(cap, nodes, [as_rows(x) for x in held])
    joined = tie(*items, *laid)
    items, laid, joined = list(joined[: len(items)]), joined[len(items) : -1], joined[-1]
    swapped = send(joined, twin())
    for level in upper:
        items = reduce_level(items, d, *level)
    *items, swapped = tie(*items, swapped)
    piece = tree(items, jnp.add)
    for level in upper[::-1]:
        piece = in_order(gather_level(piece, d, *level), d, *level)
    piece, swapped = tie(piece, swapped)
    blocks = gather_level(piece, d, *low)
    new_mem, more = merge(cap, laid, swapped, mem_t)
    *blocks, new_mem = tie(*blocks, new_mem)
    other = [send(x, twin()) for x in blocks]
    grad_norm, loss_sum, news = adam(
        jnp.stack([core, place(d, *low)]), [(0, len(blocks))], blocks, other,
        (gru_in, gru_hid, keys_values, tall_stack, squares, vectors) + moments)
    weight_sum = spread[-1, 0]

    def again(carry):
        r, _, mem_now = carry
        rows = spread_upper(lax.dynamic_index_in_dim(packed, r, 0, False), d)
        held = gather_level(rows, d, *low)
        *laid, joined = lay(cap, nodes, [as_rows(x) for x in held])
        mem_now, more = merge(cap, laid, send(joined, twin()), mem_now)
        return r + 1, more & (r + 1 < packed.shape[0]), mem_now

    if packed.shape[0] > 1:
        new_mem = lax.while_loop(lambda c: c[1], again, (jnp.int32(1), more, new_mem))[2]
    return (grad_norm, loss_sum, weight_sum, new_mem.T, *news)


def solution(mesh):
    split = P(AXES)
    placed = (split, split, P(AXES, None, None), P(AXES, None, None), split, split, split, P(AXES, None), split)
    return jax.shard_map(body, mesh=mesh, in_specs=placed + (P(),) * 20, out_specs=(P(),) * 22, check_vma=False)
```

```python
import math

import jax
import jax.numpy as jnp
from jax import lax
from jax.experimental import pallas as pl
from jax.experimental.pallas import tpu as pltpu
from jax.sharding import PartitionSpec as P

F32 = jnp.float32
BF = jnp.bfloat16
I32 = jnp.int32
NBR = 10
MEM = 172
PAD = 176
HALF = 86
HPAD = 88
STEP = 10
LEARN_RATE = 0.03
VECTOR_RATE = 0.3
BETA_ONE = 0.9
BETA_TWO = 0.999
ADAM_EPS = 1e-08
DECAY = 0.01
CLIP_AT = 0.005
TIME_RATE = 64.0
NORM_EPS = 1e-06
VMEM_CAP = 58 * 2**20


def params(limit=VMEM_CAP):
    return pltpu.CompilerParams(vmem_limit_bytes=limit)


def cost(us):
    return pl.CostEstimate(flops=int(us * 1e9), bytes_accessed=int(us * 3e6), transcendentals=0)


def nn(a, b):
    return lax.dot_general(a, b, (((1,), (0,)), ((), ())), preferred_element_type=F32)


def nt(a, b):
    return lax.dot_general(a, b, (((1,), (1,)), ((), ())), preferred_element_type=F32)


def zeros(rows, cols):
    return jnp.zeros((rows, cols), F32)


def rows_to(x, total):
    return jnp.concatenate([x, zeros(total - x.shape[0], x.shape[1])], axis=0)


def cols_to(x, total):
    return jnp.concatenate([x, zeros(x.shape[0], total - x.shape[1])], axis=1)


def split_rows(x):
    gap = zeros(HPAD - HALF, x.shape[1])
    return jnp.concatenate([x[:HALF], gap, x[HALF:], gap], axis=0)


def eye(n):
    return (lax.broadcasted_iota(I32, (n, n), 0) == lax.broadcasted_iota(I32, (n, n), 1)).astype(BF)


def turned(x):
    return nt(eye(x.shape[1]), x.astype(BF))


def wide_vectors(vec, vb):
    cols = jnp.transpose(cols_to(rows_to(vec[...], 128), 256))
    for i in range(15):
        column = cols[:, i : i + 1]
        if i in (8, 9):
            column = split_rows(column[:MEM])
        wide = jnp.broadcast_to(column[:PAD], (PAD, 128))
        vb[i] = wide * (0.5 / math.pi) if i < 2 else wide


def gate_weights(gin, ghid, vec, wg, wh, vb):
    full = gin[...]
    for gate in range(3):
        rows = full[gate * MEM : (gate + 1) * MEM]
        parts = [cols_to(rows[:, q * MEM : (q + 1) * MEM], PAD) for q in range(4)]
        wg[pl.ds(gate * PAD, PAD), :] = rows_to(jnp.concatenate(parts, axis=1), PAD).astype(BF)
    hid = ghid[...]
    for gate in range(3):
        part = cols_to(rows_to(hid[:, gate * MEM : (gate + 1) * MEM], PAD), 256)
        wh[pl.ds(gate * PAD, PAD), :] = turned(part)[:PAD].astype(BF)
    wide_vectors(vec, vb)


def main_weights_kernel(gin, kv, tall, sq, vec, wgc, kvm, kvct, kvc, t0t, t0, t1t, t1, t2t, t2, s0t, s0, s1t, s1, steady, vb):
    for gate in range(3):
        code = cols_to(rows_to(gin[gate * MEM : (gate + 1) * MEM, 2 * MEM : 3 * MEM], PAD), 256)
        wgc[:, gate * PAD : (gate + 1) * PAD] = turned(code)[:PAD].astype(BF)
    pairs = kv[...]
    both = turned(cols_to(pairs, 384))
    halves = jnp.concatenate([split_rows(both[:MEM]), split_rows(both[MEM : 2 * MEM])], axis=0)
    kvm[...] = cols_to(halves[:, :MEM], 256).astype(BF)
    code_rows = cols_to(halves[:, MEM:], 256)
    kvct[...] = code_rows[:, :PAD].astype(BF)
    kvc[...] = turned(code_rows)[:PAD].astype(BF)
    query = tall[0]
    query_t = cols_to(split_rows(query[:, :MEM]), 256)
    t0t[...] = query_t[:, :PAD].astype(BF)
    t0[...] = turned(query_t)[:PAD].astype(BF)
    for src, fwd, back in ((tall[1], t1t, t1), (tall[2], t2t, t2)):
        wide = rows_to(jnp.concatenate([cols_to(src[:, :MEM], PAD), cols_to(src[:, MEM:], PAD)], axis=1), PAD)
        fwd[...] = wide.astype(BF)
        back[...] = turned(cols_to(wide, 384))[: 2 * PAD].astype(BF)
    first = cols_to(split_rows(sq[:, 0, :]), 256)
    s0[...] = first[:, :PAD].astype(BF)
    s0t[...] = turned(first)[:PAD].astype(BF)
    second = cols_to(rows_to(sq[:, 1, :], PAD), 256)
    s1[...] = second[:, :PAD].astype(BF)
    s1t[...] = turned(second)[:PAD].astype(BF)
    phase_low = jnp.cos(jnp.transpose(cols_to(rows_to(vec[...], 128), 256))[:PAD, 1:2]).astype(BF).astype(F32)
    row_id = lax.broadcasted_iota(I32, (PAD, 128), 0)
    wide_phase = jnp.where(row_id < MEM, jnp.broadcast_to(phase_low, (PAD, 128)), 0.0).astype(BF)
    steady[...] = nn(cols_to(split_rows(query[:, MEM:]), PAD).astype(BF), wide_phase)
    wide_vectors(vec, vb)


def main_weights(gin, kv, tall, sq, vec):
    bf = lambda *s: jax.ShapeDtypeStruct(s, BF)
    outs = [bf(176, 528), bf(352, 256), bf(352, 176), bf(176, 352),
            bf(176, 176), bf(176, 176), bf(176, 352), bf(352, 176), bf(176, 352), bf(352, 176),
            bf(176, 176), bf(176, 176), bf(176, 176), bf(176, 176), jax.ShapeDtypeStruct((PAD, 128), F32),
            jax.ShapeDtypeStruct((15, PAD, 128), F32)]
    return pl.pallas_call(
        main_weights_kernel, out_shape=outs, compiler_params=params(), name="main_weights", cost_estimate=cost(5),
    )(gin.T, kv, jnp.transpose(tall, (0, 2, 1)), jnp.transpose(sq, (1, 0, 2)), vec)


def first_kernel(source, target, ticks, weights, out):
    tiles = source.shape[0]
    heights = out.shape[0] - 1
    nodes, orders = [], []
    for b in range(tiles):
        nodes += [source[b : b + 1, :], target[b : b + 1, :]]
        orders += [2 * ticks[b : b + 1, :], 2 * ticks[b : b + 1, :] + 1]
    count = 2 * tiles
    stack = jnp.concatenate([x.astype(F32) for x in nodes + orders], axis=0)
    cols = jnp.transpose(rows_to(stack, 128))
    lane = lax.broadcasted_iota(I32, (128, 128), 1)
    line = lax.broadcasted_iota(I32, (heights, 128), 0)
    total = zeros(heights, 384)
    for c in range(count):
        node = jnp.broadcast_to(cols[:, c : c + 1], (128, 128)).astype(I32)
        order = jnp.broadcast_to(cols[:, count + c : count + c + 1], (128, 128)).astype(I32)
        beaten = zeros(128, 128)
        for e in range(count):
            beaten = jnp.where((node == nodes[e]) & (orders[e] > order), 1.0, beaten)
        beaten = jnp.max(beaten, axis=1, keepdims=True)
        value = jnp.where(beaten > 0.0, 0, order + 1)
        here = (node & 127) == lane
        pick = lambda v: jnp.where(here, v, 0).astype(F32).astype(BF)
        right = jnp.concatenate([pick(value & 127), pick((value >> 7) & 127), pick(value >> 14)], axis=1)
        left = (jnp.broadcast_to(nodes[c] >> 7, (heights, 128)) == line).astype(BF)
        total = total + nn(left, right)
    out[0:heights, :] = total[:, :128] + 128.0 * total[:, 128:256] + 16384.0 * total[:, 256:] - 1.0
    out[heights : heights + 1, :] = jnp.broadcast_to(jnp.sum(weights[...], keepdims=True), (1, 128))


def first_latest(nodes, source, target, ticks, weights):
    return pl.pallas_call(
        first_kernel, out_shape=jax.ShapeDtypeStruct((nodes // 128 + 1, 128), F32),
        compiler_params=params(), name="latest", cost_estimate=cost(2),
    )(source, target, ticks, weights)


def copy_rows(out, at, tables, ids):
    for h, table in enumerate(tables):
        rows = jnp.concatenate([table[pl.ds(i, 1), :] for i in ids], axis=0)
        out[pl.ds(at, 16), 128 * h : 128 * h + 128] = rows.astype(BF)


def table_kernel(source, target, mem, ticks, far_left, far_right, own, wide, left, right, sems):
    step = pl.program_id(0)
    cols = mem.shape[1]
    steps = far_left.shape[0] // cols

    def copies(at):
        part = pl.ds(pl.multiple_of(at * cols, cols), cols)
        return [pltpu.make_async_copy(near.at[part], far.at[part], sems.at[h, at])
                for h, (near, far) in enumerate(((left, far_left), (right, far_right)))]

    @pl.when(step == 0)
    def _():
        wide[...] = jnp.zeros_like(wide)

    base = pl.multiple_of(step * cols, cols)
    wide[0:MEM, :] = mem[...].astype(BF).astype(F32)
    tick = ticks[...]
    for at, part in ((PAD, tick & 127), (PAD + 1, (tick >> 7) & 127), (PAD + 2, tick >> 14)):
        wide[at : at + 1, :] = part.astype(F32)
    unit = eye(256)
    for c in range(cols // 256):
        rows = nt(unit, wide[:, 256 * c : 256 * c + 256].astype(BF))
        left[pl.ds(base + 256 * c, 256), :] = rows[:, :128]
        right[pl.ds(base + 256 * c, 256), :] = rows[:, 128:]
    for copy in copies(step):
        copy.start()

    @pl.when(step == steps - 1)
    def _():
        def group(b, carry):
            for role, ids in enumerate((source, target)):
                def some(g, carry):
                    for v in range(2):
                        e = g * 32 + v * 16
                        at = pl.multiple_of(b * 256 + role * 128 + e, 16)
                        copy_rows(own, at, (left, right), [ids[b * 128 + e + u] for u in range(16)])
                    return carry

                lax.fori_loop(0, 4, some, 0)
            return carry

        lax.fori_loop(0, own.shape[0] // 256, group, 0)
        for at in range(steps):
            for copy in copies(at):
                copy.wait()


def build_table(source, target, mem_t, ticks):
    nodes = mem_t.shape[1]
    ends = 2 * source.shape[0]
    cols = 2048
    smem = pl.BlockSpec(memory_space=pltpu.SMEM)
    half = jax.ShapeDtypeStruct((nodes, 128), F32)
    fixed = lambda i: (0, 0)
    return pl.pallas_call(
        table_kernel,
        out_shape=[half, half, jax.ShapeDtypeStruct((ends, 256), BF)],
        grid=(nodes // cols,),
        in_specs=[smem, smem, pl.BlockSpec((MEM, cols), lambda i: (0, i)), pl.BlockSpec((1, cols), lambda i: (0, i))],
        out_specs=[pl.BlockSpec(memory_space=pl.ANY), pl.BlockSpec(memory_space=pl.ANY), pl.BlockSpec((ends, 256), fixed)],
        scratch_shapes=[pltpu.VMEM((256, cols), F32), pltpu.VMEM((nodes, 128), F32), pltpu.VMEM((nodes, 128), F32),
                        pltpu.SemaphoreType.DMA((2, nodes // cols))],
        compiler_params=params(), name="table", cost_estimate=cost(9),
    )(source, target, mem_t, ticks.reshape(1, nodes))


def near_kernel(chunk, ids, left, right, near):
    base = pl.program_id(0) * chunk

    def group(g, carry):
        for v in range(4):
            at = pl.multiple_of(g * 64 + v * 16, 16)
            copy_rows(near, at, (left, right), [ids[base + at + u] for u in range(16)])
        return carry

    lax.fori_loop(0, chunk // 64, group, 0)


def gather_near(ids, left, right):
    nears, chunk = ids.shape[0], ids.shape[0]
    whole = lambda a: pl.BlockSpec(a.shape, lambda i: (0, 0))
    return pl.pallas_call(
        lambda *r: near_kernel(chunk, *r),
        out_shape=jax.ShapeDtypeStruct((nears, 256), BF),
        grid=(nears // chunk,),
        in_specs=[pl.BlockSpec(memory_space=pltpu.SMEM), whole(left), whole(right)],
        out_specs=pl.BlockSpec((chunk, 256), lambda i: (i, 0)),
        compiler_params=params(), name="near", cost_estimate=cost(16),
    )(ids, left, right)


ROUND = 12582912.0
SIN = (6.283185005187988, -41.34165573120117, 81.60100555419922, -76.5497817993164, 39.536705017089844)
COS = (0.9999999403953552, -19.739171981811523, 64.9345932006836, -85.2403335571289, 56.24237823486328)


def cos_sin(turns):
    e = turns - ((turns + ROUND) - ROUND)
    w = 0.25 - jnp.abs(e)
    z = w * w
    c = w * (SIN[0] + z * (SIN[1] + z * (SIN[2] + z * (SIN[3] + z * SIN[4]))))
    s = COS[0] + z * (COS[1] + z * (COS[2] + z * (COS[3] + z * COS[4])))
    return c, jnp.where(e > 0.0, -s, s)


def sigmoid(x):
    return 0.5 * jnp.tanh(0.5 * x) + 0.5


BLOCK = 512
TILES = BLOCK // 256


def across(x):
    return jnp.concatenate([x] * (2 * TILES), axis=1)


def chunks(x, width=128):
    return [x[:, at : at + width] for at in range(0, x.shape[1], width)]


def both(x):
    return jnp.concatenate([c for c in chunks(x) for _ in range(2)], axis=1)


def mix(x, y):
    return jnp.concatenate([c for pair in zip(chunks(x), chunks(y)) for c in pair], axis=1)


def sources_of(x):
    return jnp.concatenate(chunks(x)[0::2], axis=1)


def targets_of(x):
    return jnp.concatenate(chunks(x)[1::2], axis=1)


def wide_rows(x, rows):
    return jnp.broadcast_to(x, (rows, x.shape[1]))


SECOND = 48


def round_height(cap):
    return cap + SECOND * (cap // 128) + cap % 128 // 2 + 8


def gru_kernel(scale, own, source, target, ticks, edge, types, gin, ghid, vec,
               msg, keep, ren, gap_out, left, right, wg, wh, vb):
    step = pl.program_id(0)

    @pl.when(step == 0)
    def _():
        gate_weights(gin, ghid, vec, wg, wh, vb)

    own_t = nt(eye(256), own[...])
    seen = own_t[PAD : PAD + 1] + 128.0 * own_t[PAD + 1 : PAD + 2] + 16384.0 * own_t[PAD + 2 : PAD + 3]
    gap = (both(ticks[...].astype(F32)) - seen) * scale
    row_id = lax.broadcasted_iota(I32, (PAD, BLOCK), 0)
    own_x = jnp.where(row_id < MEM, own_t[:PAD], 0.0)
    msg[0:PAD, :] = own_x.astype(BF)
    msg[PAD : 2 * PAD, :] = mix(targets_of(own_x), sources_of(own_x)).astype(BF)
    edges = rows_to(edge[...].astype(F32) * types[...].astype(F32), PAD)
    msg[3 * PAD : 4 * PAD, :] = both(edges).astype(BF)
    gap_out[...] = wide_rows(gap, 8)
    gap16 = wide_rows(gap, 16)
    for st in range(PAD // 16):
        at = 16 * st
        for m in range(TILES):
            q = slice(256 * m, 256 * m + 256)
            rate, phase = vb[0, at : at + 16, :], vb[1, at : at + 16, :]
            x = jnp.concatenate([rate, rate], axis=1) * gap16[:, q] + jnp.concatenate([phase, phase], axis=1)
            c, s = cos_sin(x)
            msg[2 * PAD + at : 2 * PAD + at + 16, q] = c.astype(BF)
            keep[4, at : at + 16, q] = s
    gates = nn(wg[...], msg[...])
    hidden = nn(wh[...], msg[0:PAD, :])
    for st in range(PAD // 8):
        at = 8 * st
        o = own_x[at : at + 8]
        pre = [gates[g * PAD + at : g * PAD + at + 8] + across(vb[2 + g, at : at + 8, :]) for g in range(3)]
        hid = [hidden[g * PAD + at : g * PAD + at + 8] + across(vb[5 + g, at : at + 8, :]) for g in range(3)]
        u = sigmoid(pre[0] + hid[0])
        r = sigmoid(pre[1] + hid[1])
        n = jnp.tanh(pre[2] + r * hid[2])
        keep[0, at : at + 8, :] = u
        keep[1, at : at + 8, :] = r
        keep[2, at : at + 8, :] = n
        keep[3, at : at + 8, :] = hid[2]
        ren[at : at + 8, :] = (1.0 - u) * n + u * o
    numbers = mix(source[...], target[...]).astype(F32)
    low = jnp.concatenate([ren[128:MEM, :], numbers, zeros(255 - MEM, BLOCK)], axis=0)
    for role in range(2 * TILES):
        left[128 * role : 128 * role + 128, :] = jnp.transpose(ren[0:128, 128 * role : 128 * role + 128])
        right[128 * role : 128 * role + 128, :] = jnp.transpose(low[:, 128 * role : 128 * role + 128])


def pack_rows(cap, rounds, nodes, sources, targets, ticks, latest, left, right, out, first, second):
    def chunk(b, count):
        def some(g, count):
            for v in range(16):
                e = b * 128 + g * 16 + v
                i = b * 256 + g * 16 + v
                order = 2 * ticks[e]
                for role, ids in enumerate((sources, targets)):
                    first[pl.ds(count, 1), :] = left[pl.ds(i + 128 * role, 1), :]
                    second[pl.ds(count, 1), :] = right[pl.ds(i + 128 * role, 1), :]
                    count = count + (latest[ids[e]] == order + role).astype(I32)
            return count

        return lax.fori_loop(0, 8, some, count)

    count = lax.fori_loop(0, sources.shape[0] // 128, chunk, jnp.int32(0))
    tiles = cap // 128
    rest = cap - 128 * tiles
    lane = lax.broadcasted_iota(I32, (1, 128), 1)
    for r in range(rounds):
        at = r * cap
        out[r, 0:cap, :] = first[at : at + cap, :]
        here = jnp.clip(count - at, 0, cap)
        lines = []
        for q in range(-(-cap // 128)):
            columns = jnp.transpose(second[at + 128 * q : at + 128 * q + 128, :])
            if q < tiles:
                out[r, cap + SECOND * q : cap + SECOND * q + SECOND, :] = columns[0:SECOND]
            lines.append(jnp.where(lane + 128 * q < here, columns[MEM - 128 : MEM - 127], float(nodes)))
        line, base = cap + SECOND * tiles, at + 128 * tiles
        if rest:
            out[r, line : line + rest // 2, :] = jnp.concatenate(
                [second[base : base + rest // 2, 0:64], second[base + rest // 2 : base + rest, 0:64]], axis=1)
        lines.append(jnp.full((1, 128), here, I32).astype(F32))
        lines += [zeros(1, 128)] * (8 - len(lines))
        out[r, line + rest // 2 :, :] = jnp.concatenate(lines, axis=0)


def pack(cap, sources, targets, ticks, latest, left, right):
    ends, nodes = left.shape[0], latest.shape[0]
    rounds = ends // cap + 1
    spare = rounds * cap + 128
    smem, vm = pl.BlockSpec(memory_space=pltpu.SMEM), pl.BlockSpec(memory_space=pltpu.VMEM)
    return pl.pallas_call(
        lambda *r: pack_rows(cap, rounds, nodes, *r),
        out_shape=jax.ShapeDtypeStruct((rounds, round_height(cap), 128), F32),
        in_specs=[smem] * 4 + [vm, vm], out_specs=vm,
        scratch_shapes=[pltpu.VMEM((spare, 128), F32), pltpu.VMEM((spare, 128), F32)],
        compiler_params=params(), name="pack", cost_estimate=cost(5),
    )(sources, targets, ticks, latest, left, right)


def gru(scale, sources, targets, ticks, own, edge_t, types, gin, ghid, vec):
    ends = own.shape[0]
    blocks = ends // BLOCK
    whole = lambda a: pl.BlockSpec(a.shape, lambda i: (0,) * len(a.shape))
    lanes = lambda: pl.BlockSpec((1, BLOCK // 2), lambda i: (0, i))
    row = lambda x: x.reshape(1, -1)
    gin = gin.T
    half = jax.ShapeDtypeStruct((ends, 128), F32)
    return pl.pallas_call(
        lambda *r: gru_kernel(scale, *r),
        out_shape=[jax.ShapeDtypeStruct((4 * PAD, ends), BF), jax.ShapeDtypeStruct((5, PAD, ends), F32),
                   jax.ShapeDtypeStruct((PAD, ends), F32), jax.ShapeDtypeStruct((8, ends), F32), half, half],
        grid=(blocks,),
        in_specs=[pl.BlockSpec((BLOCK, 256), lambda i: (i, 0)), lanes(), lanes(), lanes(),
                  pl.BlockSpec((MEM, BLOCK // 2), lambda i: (0, i)), lanes(), whole(gin), whole(ghid), whole(vec)],
        out_specs=[pl.BlockSpec((4 * PAD, BLOCK), lambda i: (0, i)), pl.BlockSpec((5, PAD, BLOCK), lambda i: (0, 0, i)),
                   pl.BlockSpec((PAD, BLOCK), lambda i: (0, i)), pl.BlockSpec((8, BLOCK), lambda i: (0, i)),
                   pl.BlockSpec((BLOCK, 128), lambda i: (i, 0)), pl.BlockSpec((BLOCK, 128), lambda i: (i, 0))],
        scratch_shapes=[pltpu.VMEM((528, 704), BF), pltpu.VMEM((528, 176), BF), pltpu.VMEM((15, PAD, 128), F32)],
        compiler_params=params(), name="gru", cost_estimate=cost(8),
    )(own, row(sources), row(targets), row(ticks), edge_t, types, gin, ghid, vec)


UNROLL = 10
ROWS = 2944
VECTORS = 2904
GELU_C = math.sqrt(2.0 / math.pi)


def gelu_parts(x):
    sq = x * x
    t = jnp.tanh(GELU_C * (x + 0.044715 * (sq * x)))
    half = 0.5 * (1.0 + t)
    slope = half + (0.5 * x) * (1.0 - t * t) * (GELU_C + (GELU_C * 3.0 * 0.044715) * sq)
    return x * half, slope


def fold(x):
    total, *others = chunks(x)
    for other in others:
        total = total + other
    return total


def main_kernel(scale, core, near, gaps_t, ticks, msg, keep, ren, gap_own, labels, weights, total,
                wgc, kvm, kvct, kvc, t0t, t0, t1t, t1, t2t, t2, s0t, s0, s1t, s1, steady, vb,
                mine, theirs,
                loss, pair, code, dcode, soft, back, mean, d_query_at, grads, g_in, g_kv, g_one, g_dec, g_qo, g_th, vacc):
    step = pl.program_id(0)
    inv_size = HALF ** -0.5

    @pl.when(step == 0)
    def _():
        for ref in (g_in, g_kv, g_one, g_dec, g_qo, g_th, vacc, loss):
            ref[...] = jnp.zeros_like(ref)

    tick2 = both(ticks[...].astype(F32))
    renewed = ren[...]
    ren_low = renewed.astype(BF)
    queries = nn(t0t[...], ren_low) + across(vb[8] + steady[...])
    def each(one):
        def some(g, carry):
            for v in range(UNROLL):
                one(g * UNROLL + v)
            return carry

        lax.fori_loop(0, NBR // UNROLL, some, 0)

    def look(j):
        gap16 = wide_rows((tick2 - gaps_t[pl.ds(j, 1), :].astype(F32)) * scale, 16)
        for st in range(PAD // 16):
            at = 16 * st
            for m in range(TILES):
                q = slice(256 * m, 256 * m + 256)
                rate, phase = vb[0, at : at + 16, :], vb[1, at : at + 16, :]
                x = jnp.concatenate([rate, rate], axis=1) * gap16[:, q] + jnp.concatenate([phase, phase], axis=1)
                c, s = cos_sin(x)
                code[j, at : at + 16, q] = c.astype(BF)
                dcode[j, at : at + 16, q] = s
        pair[j] = nt(kvm[...], near[j]) + nn(kvct[...], code[j])
        for h in range(2):
            acc = zeros(8, BLOCK)
            for st in range(HPAD // 8):
                at = HPAD * h + 8 * st
                acc = acc + pair[j, at : at + 8, :] * queries[at : at + 8]
            soft[2 * j + h] = wide_rows(jnp.sum(acc, axis=0, keepdims=True) * inv_size, 8)

    each(look)
    for h in range(2):
        top = soft[h]
        for j in range(1, NBR):
            top = jnp.maximum(top, soft[2 * j + h])
        norm = zeros(8, BLOCK)
        for j in range(NBR):
            e = jnp.exp(soft[2 * j + h] - top)
            soft[2 * j + h] = e
            norm = norm + e
        inv = 1.0 / norm
        for j in range(NBR):
            soft[2 * j + h] = soft[2 * j + h] * inv
    att = []
    for st in range(PAD // 8):
        at = 8 * st
        h = 0 if at < HPAD else 1
        acc = across(vb[9, at : at + 8, :])
        for j in range(NBR):
            acc = acc + soft[2 * j + h] * pair[j, PAD + at : PAD + at + 8, :]
        att.append(acc)
    att_low = jnp.concatenate(att, axis=0).astype(BF)
    projected = nn(s0t[...], att_low) + across(vb[10])
    mlp_in = jnp.concatenate([projected.astype(BF), ren_low], axis=0)
    inner = nn(t1t[...], mlp_in) + across(vb[11])
    act, act_slope = gelu_parts(inner)
    act_low = act.astype(BF)
    emb_low = (nn(s1t[...], act_low) + across(vb[12])).astype(BF)
    dec_in = jnp.concatenate([sources_of(emb_low), targets_of(emb_low)], axis=0)
    out_row = jnp.concatenate([vb[14]] * TILES, axis=1)
    dec_pre = nn(t2t[...], dec_in) + jnp.concatenate([vb[13]] * TILES, axis=1)
    dec_act, dec_slope = gelu_parts(dec_pre)
    logit = jnp.sum(dec_act * out_row, axis=0, keepdims=True)
    label = labels[...].astype(F32)
    tail = jnp.exp(-jnp.abs(logit))
    plus = jnp.maximum(logit, 0.0) + jnp.log1p(tail)
    loss[...] += fold(weights[...] * (plus - label * logit))
    d_logit = weights[...] / total[:, 0:1] * (sigmoid(logit) - label)
    d_out = d_logit * dec_act
    d_dec = (d_logit * out_row) * dec_slope
    d_dec_low = d_dec.astype(BF)
    g_dec[...] += nt(d_dec_low, dec_in)
    d_dec_in = nn(t2[...], d_dec_low)
    d_emb = mix(d_dec_in[:PAD], d_dec_in[PAD:])
    d_emb_low = d_emb.astype(BF)
    g_th[:, 0:256] += jnp.concatenate([nt(act_low, d_emb_low), zeros(PAD, 256 - PAD)], axis=1)
    d_inner = nn(s1[...], d_emb_low) * act_slope
    d_inner_low = d_inner.astype(BF)
    g_one[...] += nt(d_inner_low, mlp_in)
    d_mlp = nn(t1[...], d_inner_low)
    d_proj = d_mlp[:PAD]
    d_proj_low = d_proj.astype(BF)
    g_qo[:, 256:512] += jnp.concatenate([nt(att_low, d_proj_low), zeros(PAD, 256 - PAD)], axis=1)
    d_att = nn(s0[...], d_proj_low)
    d_query_at[...] = jnp.zeros_like(d_query_at)
    mean[...] = jnp.zeros_like(mean)

    def weigh(j):
        for h in range(2):
            acc = zeros(8, BLOCK)
            for st in range(HPAD // 8):
                at = HPAD * h + 8 * st
                acc = acc + pair[j, PAD + at : PAD + at + 8, :] * d_att[at : at + 8]
            wide = wide_rows(jnp.sum(acc, axis=0, keepdims=True), 8)
            back[2 * j + h] = wide
            mean[h] += wide * soft[2 * j + h]

    def learn(j):
        share = [soft[2 * j + h] for h in range(2)]
        slope = [(share[h] * inv_size) * (back[2 * j + h] - mean[h]) for h in range(2)]
        for st in range(PAD // 8):
            at = 8 * st
            d_query_at[at : at + 8, :] += slope[at >= HPAD] * pair[j, at : at + 8, :]
        for st in range(2 * PAD // 16):
            parts = []
            for half in range(2):
                at = 16 * st + 8 * half
                if at < PAD:
                    parts.append(slope[at >= HPAD] * queries[at : at + 8])
                else:
                    parts.append(share[at - PAD >= HPAD] * d_att[at - PAD : at - PAD + 8])
            grads[j, 16 * st : 16 * st + 16, :] = jnp.concatenate(parts, axis=0).astype(BF)
        d_code = nn(kvc[...], grads[j])
        gap8 = wide_rows((tick2 - gaps_t[pl.ds(j, 1), :].astype(F32)) * scale, 8)
        for st in range(PAD // 8):
            at = 8 * st
            d_arg = d_code[at : at + 8] * dcode[j, at : at + 8, :]
            vacc[0, at : at + 8, :] += fold(d_arg * gap8)
            vacc[1, at : at + 8, :] += fold(d_arg)
        g_kv[:, 0:256] += nn(grads[j], near[j])
        g_kv[:, 256 : 256 + PAD] += nt(grads[j], code[j])

    each(weigh)
    each(learn)
    d_query = d_query_at[...]
    d_q_low = d_query.astype(BF)
    g_qo[:, 0:256] += jnp.concatenate([nt(d_q_low, ren_low), zeros(PAD, 256 - PAD)], axis=1)
    d_ren = d_mlp[PAD:] + nn(t0[...], d_q_low)
    own_x = msg[0:PAD, :].astype(F32)
    u, r, n, hn = keep[0], keep[1], keep[2], keep[3]
    d_u = d_ren * (own_x - n) * (u * (1.0 - u))
    d_n = d_ren * (1.0 - u) * (1.0 - n * n)
    d_r = d_n * hn * (r * (1.0 - r))
    d_h = d_n * r
    gates = jnp.concatenate([d_u, d_r, d_n], axis=0).astype(BF)
    g_in[...] += nt(gates, msg[...])
    g_th[:, 256:512] += jnp.concatenate([nt(msg[0:PAD, :], d_h.astype(BF)), zeros(PAD, 256 - PAD)], axis=1)
    d_arg = nn(wgc[...], gates) * keep[4]
    vacc[0] += fold(d_arg * gap_own[0:1, :])
    vacc[1] += fold(d_arg)
    for i, item in ((2, d_u), (3, d_r), (4, d_n), (7, d_h), (8, d_query), (9, d_att), (10, d_proj), (11, d_inner),
                    (12, d_emb), (15, d_q_low.astype(F32))):
        vacc[i] += fold(item)
    vacc[13] += fold(d_dec)
    vacc[14] += fold(d_out)

    def finish(ga, gb):
        def panels(out, x):
            rows, lanes = x.shape
            whole = lanes // 128
            for c in range(whole):
                out[rows * c : rows * c + rows, :] = x[:, 128 * c : 128 * c + 128]
            last = x[:, 128 * whole :]
            out[rows * whole : rows * whole + rows // 2, :] = jnp.concatenate([last[: rows // 2], last[rows // 2 :]], axis=1)

        panels(gb, g_in[...])
        lane = lax.broadcasted_iota(I32, (PAD, 128), 1)
        vecs = zeros(PAD, 128)
        for i in range(16):
            column = jnp.sum(vacc[i], axis=1, keepdims=True)
            vecs = jnp.where(lane == i, column, vecs)
        flat = jnp.transpose(jnp.concatenate([vecs, zeros(256 - PAD, 128)], axis=0))
        gb[VECTORS : VECTORS + 16, :] = flat[0:16, 0:128]
        gb[VECTORS + 16 : VECTORS + 32, :] = flat[0:16, 128:256]
        gb[VECTORS + 32 :, :] = zeros(ROWS - VECTORS - 32, 128)
        units = [g_kv[at : at + PAD, c : c + PAD] for at in (0, PAD) for c in (0, 256)]
        units += [g_one[...], g_dec[...]]
        units += [ref[:, c : c + PAD] for ref in (g_qo, g_th) for c in (0, 256)]
        panels(ga, jnp.concatenate(units, axis=1))
        ga[VECTORS:, :] = rows_to(loss[...], ROWS - VECTORS)

    @pl.when((step == pl.num_programs(0) - 1) & (core[0] == 0))
    def _():
        finish(mine, theirs)

    @pl.when((step == pl.num_programs(0) - 1) & (core[0] != 0))
    def _():
        finish(theirs, mine)


def main(scale, near, near_ticks, ticks, msg, keep, ren, gap_own, labels, weights, total, core, w):
    ends = ren.shape[1]
    blocks = ends // BLOCK
    whole = lambda a: pl.BlockSpec(a.shape, lambda i: (0,) * len(a.shape))
    lanes = lambda: pl.BlockSpec((1, BLOCK // 2), lambda i: (0, i))
    return pl.pallas_call(
        lambda *r: main_kernel(scale, *r),
        out_shape=[jax.ShapeDtypeStruct((ROWS, 128), F32), jax.ShapeDtypeStruct((ROWS, 128), F32)],
        grid=(blocks,),
        in_specs=[pl.BlockSpec(memory_space=pltpu.SMEM), pl.BlockSpec((NBR, BLOCK, 256), lambda i: (0, i, 0)), pl.BlockSpec((NBR, BLOCK), lambda i: (0, i)), lanes(),
                  pl.BlockSpec((4 * PAD, BLOCK), lambda i: (0, i)), pl.BlockSpec((5, PAD, BLOCK), lambda i: (0, 0, i)),
                  pl.BlockSpec((PAD, BLOCK), lambda i: (0, i)), pl.BlockSpec((8, BLOCK), lambda i: (0, i)), lanes(), lanes(),
                  pl.BlockSpec((1, 128), lambda i: (0, 0))] + [whole(a) for a in w],
        out_specs=[pl.BlockSpec((ROWS, 128), lambda i: (0, 0)), pl.BlockSpec((ROWS, 128), lambda i: (0, 0))],
        scratch_shapes=[pltpu.VMEM((1, 128), F32), pltpu.VMEM((NBR, 352, BLOCK), F32), pltpu.VMEM((NBR, PAD, BLOCK), BF), pltpu.VMEM((NBR, PAD, BLOCK), F32),
                        pltpu.VMEM((20, 8, BLOCK), F32), pltpu.VMEM((20, 8, BLOCK), F32), pltpu.VMEM((2, 8, BLOCK), F32),
                        pltpu.VMEM((PAD, BLOCK), F32), pltpu.VMEM((NBR, 352, BLOCK), BF),
                        pltpu.VMEM((528, 704), F32), pltpu.VMEM((352, 512), F32), pltpu.VMEM((PAD, 352), F32),
                        pltpu.VMEM((PAD, 352), F32), pltpu.VMEM((PAD, 512), F32), pltpu.VMEM((PAD, 512), F32),
                        pltpu.VMEM((16, PAD, 128), F32)],
        compiler_params=params(), name="main", cost_estimate=cost(35),
    )(core, near.reshape(NBR, ends, 256), near_ticks, ticks, msg, keep, ren, gap_own, labels, weights, total, *w)


def room(nodes, devices):
    return -(-(nodes * 9) // (devices * 8 * 16)) * 16


def turned_exactly(x):
    high = x.astype(BF)
    rest = x - high.astype(F32)
    middle = rest.astype(BF)
    low = (rest - middle.astype(F32)).astype(BF)
    unit = eye(x.shape[1])
    return (nt(unit, high) + nt(unit, middle)) + nt(unit, low)


def fetch_numbers(cap, rows, whole, numbers, sem):
    whole[...] = rows[:, round_height(cap) - 8 :, :].astype(I32)
    copy = pltpu.make_async_copy(whole, numbers, sem)
    copy.start()
    return copy


def lay_rows(cap, rows, numbers, left, right, second):
    tiles = cap // 128
    line, tail = cap + SECOND * tiles, cap % 128 // 2

    def block(q, most):
        for t in range(tiles):
            columns = rows[q, cap + SECOND * t : cap + SECOND * t + SECOND, :]
            second[128 * t : 128 * t + 128, :] = jnp.transpose(rows_to(columns, 128))
        if tail:
            half = rows[q, line : line + tail, :]
            second[128 * tiles : 128 * tiles + tail, :] = half
            second[128 * tiles + tail : cap, :] = jnp.concatenate([half[:, 64:], half[:, :64]], axis=1)
        here = numbers[q, -(-cap // 128), 0]

        def some(g, carry):
            few = numbers.at[q, lax.shift_right_logical(g, 3), pl.ds((g & 7) * 16, 16)]
            for v in range(16):
                i = g * 16 + v
                node = few[v]
                left[pl.ds(node, 1), :] = rows[q, pl.ds(i, 1), :]
                right[pl.ds(node, 1), :] = second[pl.ds(i, 1), :]
            return carry

        lax.fori_loop(0, lax.div(here + 15, 16), some, 0)
        return jnp.maximum(most, here)

    return lax.fori_loop(0, rows.shape[0], block, jnp.int32(0))


def lay_kernel(cap, count, *refs):
    arrays, (left, right, most, joined, second, sems), rest = refs[:count], refs[count : count + 6], refs[count + 6 :]
    wholes, lists = rest[:count], rest[count:]
    copies = [fetch_numbers(cap, arrays[a], wholes[a], lists[a], sems.at[a]) for a in range(count)]
    right[...] = jnp.full_like(right, -1.0)
    for a, rows in enumerate(arrays):
        blocks = rows.shape[0]
        joined[a * blocks : (a + 1) * blocks] = rows[...]
    largest = jnp.int32(0)
    for a, rows in enumerate(arrays):
        copies[a].wait()
        largest = jnp.maximum(largest, lay_rows(cap, rows, lists[a], left, right, second))
    most[0] = largest


def lay(cap, nodes, arrays):
    vm, smem = pl.BlockSpec(memory_space=pltpu.VMEM), pl.BlockSpec(memory_space=pltpu.SMEM)
    table = jax.ShapeDtypeStruct((nodes + 8, 128), F32)
    count = len(arrays)
    blocks, height, _ = arrays[0].shape
    return pl.pallas_call(
        lambda *r: lay_kernel(cap, count, *r),
        out_shape=[table, table, jax.ShapeDtypeStruct((1,), I32), jax.ShapeDtypeStruct((count * blocks, height, 128), F32)],
        in_specs=[vm] * count, out_specs=[vm, vm, smem, vm],
        scratch_shapes=[pltpu.VMEM((cap, 128), F32), pltpu.SemaphoreType.DMA((count,))]
        + [kind((blocks, 8, 128), I32) for kind in (pltpu.VMEM, pltpu.SMEM) for _ in arrays],
        compiler_params=params(), name="lay", cost_estimate=cost(14),
    )(*arrays)


def merge_kernel(cap, far_rows, far_left, far_right, before, mem, out, full, left, right, second, sems, rows, whole, numbers):
    step = pl.program_id(0)

    @pl.when(step == 0)
    def _():
        copies = [pltpu.make_async_copy(far, near, sems.at[i])
                  for i, (far, near) in enumerate(((far_rows, rows), (far_left, left), (far_right, right)))]
        for copy in copies:
            copy.start()
        copies[0].wait()
        copies.append(fetch_numbers(cap, rows, whole, numbers, sems.at[3]))
        for copy in copies[1:]:
            copy.wait()
        most = lay_rows(cap, rows, numbers, left, right, second)
        full[0] = (jnp.maximum(most, before[0]) == cap).astype(I32)

    cols = mem.shape[1]
    base = pl.multiple_of(step * cols, cols)
    for c in range(cols // 256):
        at = base + 256 * c
        s = slice(256 * c, 256 * c + 256)
        top = turned_exactly(left[pl.ds(at, 256), :])
        low = turned_exactly(right[pl.ds(at, 256), :][:, :64])
        fresh = low[MEM - 128 : MEM - 127] >= 0.0
        out[0:128, s] = jnp.where(fresh, top, mem[0:128, s])
        out[128:MEM, s] = jnp.where(fresh, low[: MEM - 128], mem[128:MEM, s])


def merge(cap, laid, rows, mem_t):
    nodes = mem_t.shape[1]
    cols = 2048
    part = pl.BlockSpec((MEM, cols), lambda i: (0, i))
    smem, far = pl.BlockSpec(memory_space=pltpu.SMEM), pl.BlockSpec(memory_space=pl.ANY)
    new, full = pl.pallas_call(
        lambda *r: merge_kernel(cap, *r),
        out_shape=[jax.ShapeDtypeStruct((MEM, nodes), F32), jax.ShapeDtypeStruct((1,), I32)],
        grid=(nodes // cols,),
        in_specs=[far, far, far, smem, part],
        out_specs=[part, smem],
        scratch_shapes=[pltpu.VMEM((nodes + 8, 128), F32), pltpu.VMEM((nodes + 8, 128), F32), pltpu.VMEM((cap, 128), F32),
                        pltpu.SemaphoreType.DMA((4,)), pltpu.VMEM(rows.shape, F32)]
        + [kind((rows.shape[0], 8, 128), I32) for kind in (pltpu.VMEM, pltpu.SMEM)],
        compiler_params=params(), name="merge", cost_estimate=cost(18),
    )(rows, *laid, mem_t)
    return new, full[0] > 0


def move(param, one, two, grad, factor, rate, decay):
    clipped = grad * factor
    one = BETA_ONE * one + (1.0 - BETA_ONE) * clipped
    two = BETA_TWO * two + (1.0 - BETA_TWO) * clipped * clipped
    step = (one * (1.0 / (1.0 - BETA_ONE**STEP))) / (jnp.sqrt(two * (1.0 / (1.0 - BETA_TWO**STEP))) + ADAM_EPS)
    return param - rate * (step + decay * param), one, two


def unsplit(x, axis):
    take = lambda a, b: lax.slice_in_dim(x, a, b, axis=axis)
    return jnp.concatenate([take(0, HALF), take(HPAD, HPAD + HALF)], axis=axis)


def adam_kernel(parts, where, *refs):
    count = sum(n for _, n in parts)
    mine, other = refs[:count], refs[count : 2 * count]
    refs = refs[2 * count :]
    far, out, (norm_out, loss_out) = refs[:18], refs[18:36], refs[36:38]
    a, b, g_gin, g_hid, g_kv, g_tall, g_sq, g_vec = refs[38:46]
    state, sems_in, sems_out = refs[46:64], refs[64], refs[65]
    fetches = [pltpu.make_async_copy(far[i], state[i], sems_in.at[i]) for i in range(18)]
    stores = [pltpu.make_async_copy(state[i], out[i], sems_out.at[i]) for i in range(18)]
    for i in (5, 3, 0, 6, 12, 1, 7, 13, 2, 8, 14, 9, 15, 4, 10, 16, 11, 17):
        fetches[i].start()
    core = where[0]
    at_block = 0
    for p, (first, n) in enumerate(parts):
        height = mine[at_block].shape[0]
        for k in range(n):
            at = pl.multiple_of(first + (where[1 + p] ^ k) * height, 8)
            one, two = mine[at_block], other[at_block]
            at_block += 1

            @pl.when(core == 0)
            def _():
                a[pl.ds(at, height), :] = one[...]
                b[pl.ds(at, height), :] = two[...]

            @pl.when(core != 0)
            def _():
                b[pl.ds(at, height), :] = one[...]
                a[pl.ds(at, height), :] = two[...]

    def panels(ref, rows, lanes):
        whole = lanes // 128
        parts = [ref[c * rows : (c + 1) * rows, :] for c in range(whole)]
        last = ref[whole * rows : whole * rows + rows // 2, :]
        return jnp.concatenate(parts + [jnp.concatenate([last[:, :64], last[:, 64:]], axis=0)], axis=1)

    vec, tall = state[5], state[3]
    wide = panels(b, 528, 704)
    gates = []
    for g in range(3):
        rows = wide[PAD * g : PAD * g + MEM]
        gates.append(jnp.concatenate([rows[:, PAD * q : PAD * q + MEM] for q in range(4)], axis=1))
    g_gin[...] = jnp.concatenate(gates, axis=0)
    vecs = jnp.concatenate([b[VECTORS : VECTORS + 16, :], b[VECTORS + 16 : VECTORS + 32, :]], axis=1)
    units = panels(a, PAD, 12 * PAD)
    unit = lambda i: units[:, PAD * i : PAD * i + MEM]
    kv = jnp.concatenate([jnp.concatenate([unsplit(unit(2 * i), 0), unsplit(unit(2 * i + 1), 0)], axis=1) for i in range(2)], axis=0)
    g_kv[...] = jnp.transpose(rows_to(cols_to(kv, 384), 384))[: 2 * MEM, : 2 * MEM]
    for i in (1, 2):
        g_tall[i] = jnp.concatenate([unit(2 + 2 * i)[:MEM], unit(3 + 2 * i)[:MEM]], axis=1)
    sum_dq = unsplit(jnp.transpose(rows_to(vecs, 128))[:PAD, 15:16], 0)
    fetches[5].wait()
    fetches[3].wait()
    phase = vec[1:2, :]
    phase_low = jnp.cos(phase).astype(BF).astype(F32)
    g_tall[0] = jnp.concatenate([unsplit(unit(8), 0), sum_dq * phase_low], axis=1)
    g_sq[0] = unsplit(unit(9), 0)
    g_sq[1] = unit(10)[:MEM]
    shared = jnp.transpose(rows_to(cols_to(g_gin[0 : 2 * MEM, 0:MEM], 256), 384))[:MEM, : 2 * MEM]
    g_hid[...] = jnp.concatenate([shared, unit(11)[:MEM]], axis=1)
    query_low = tall[0][:, MEM:].astype(BF).astype(F32)
    phase_in = jnp.sum(query_low * sum_dq, axis=0, keepdims=True)
    row = lambda i: vecs[i : i + 1, :MEM]
    g_vec[...] = jnp.concatenate(
        [row(0), row(1) - jnp.sin(phase) * phase_in, row(2), row(3), row(4), row(2), row(3), row(7),
         unsplit(vecs[8:9], 1), unsplit(vecs[9:10], 1)] + [row(i) for i in range(10, 15)], axis=0)
    total = jnp.zeros((1, 1), F32)
    for ref in (g_gin, g_hid, g_kv, g_vec):
        total += jnp.sum(ref[...] * ref[...], keepdims=True)
    for ref in (g_tall, g_sq):
        for i in range(ref.shape[0]):
            total += jnp.sum(ref[i] * ref[i], keepdims=True)
    norm = jnp.sqrt(total)
    factor = jnp.minimum(1.0, CLIP_AT / (norm + NORM_EPS))
    norm_out[...] = norm
    loss_out[...] = jnp.sum(a[VECTORS : VECTORS + 1, :], keepdims=True)
    for i, grad in enumerate((g_gin, g_hid, g_kv, g_tall, g_sq, g_vec)):
        rate, decay = (VECTOR_RATE, 0.0) if i == 5 else (LEARN_RATE, DECAY)
        new = param, one, two = state[i], state[6 + i], state[12 + i]
        for at in (i, 6 + i, 12 + i):
            if at not in (3, 5):
                fetches[at].wait()
        if i == 4:
            for j in range(2):
                made = move(param[:, j, :], one[:, j, :], two[:, j, :], grad[j], factor, rate, decay)
                for ref, value in zip(new, made):
                    ref[:, j, :] = value
        elif len(param.shape) == 3:
            for j in range(param.shape[0]):
                made = move(param[j], one[j], two[j], grad[j], factor, rate, decay)
                for ref, value in zip(new, made):
                    ref[j] = value
        else:
            rows = param.shape[0]
            for at in range(0, rows, 16):
                s = slice(at, min(at + 16, rows))
                made = move(param[s], one[s], two[s], grad[s], factor, rate, decay)
                for ref, value in zip(new, made):
                    ref[s] = value
        for at in (i, 6 + i, 12 + i):
            stores[at].start()
    for store in stores:
        store.wait()


def adam(where, parts, mine, other, state):
    swap = lambda x: jnp.transpose(x, (0, 2, 1))
    def ready(group):
        gin, hid, kv, tall, sq, vec = group
        return [gin.T, hid, kv, swap(tall), jnp.transpose(sq, (1, 0, 2)), vec]
    state = ready(state[0:6]) + ready(state[6:12]) + ready(state[12:18])
    count = len(mine)
    shapes = [x.shape for x in state[:6]]
    shapes[4] = (2, MEM, MEM)
    vm, far = pl.BlockSpec(memory_space=pltpu.VMEM), pl.BlockSpec(memory_space=pl.ANY)
    outs = [jax.ShapeDtypeStruct(x.shape, F32) for x in state] + [jax.ShapeDtypeStruct((1, 1), F32)] * 2
    out = pl.pallas_call(
        lambda *r: adam_kernel(parts, *r),
        out_shape=outs,
        in_specs=[pl.BlockSpec(memory_space=pltpu.SMEM)] + [vm] * (2 * count) + [far] * 18,
        out_specs=[far] * 18 + [vm] * 2,
        scratch_shapes=[pltpu.VMEM((ROWS, 128), F32)] * 2 + [pltpu.VMEM(s, F32) for s in shapes]
        + [pltpu.VMEM(x.shape, F32) for x in state] + [pltpu.SemaphoreType.DMA((18,))] * 2,
        compiler_params=params(), name="adam", cost_estimate=cost(14),
    )(where, *mine, *other, *state)
    back = lambda group: [group[0].T, group[1], group[2], swap(group[3]), jnp.transpose(group[4], (1, 0, 2)), group[5]]
    return out[18].reshape(()), out[19].reshape(()), back(out[0:6]) + back(out[6:12]) + back(out[12:18])


AXES = ("dp", "rep")


def levels(size):
    found, stride = [], 1
    while size > 1:
        n = size if size <= 8 else 4
        found.append((stride, n))
        stride, size = stride * n, size // n
    return found


def peers(stride, k):
    dp, rep = lax.axis_size("dp"), lax.axis_size("rep")
    return [(d * rep + r, (d ^ (k * stride)) * rep + r) for d in range(dp) for r in range(rep)]


def twin():
    dp, rep = lax.axis_size("dp"), lax.axis_size("rep")
    return [(d * rep + r, d * rep + (rep - 1 - r)) for d in range(dp) for r in range(rep)]


def send(x, pairs):
    return lax.ppermute(x, AXES, pairs)


def tree(items, join):
    while len(items) > 1:
        items = [join(items[i], items[i + 1]) for i in range(0, len(items), 2)]
    return items[0]


def place(d, stride, n):
    return lax.rem(lax.div(d, stride), n)


def reduce_level(items, d, stride, n):
    c = place(d, stride, n)
    rows = items[0].shape[0] // n
    piece = lambda k: tree([lax.dynamic_slice_in_dim(x, (c ^ k) * rows, rows, 0) for x in items], jnp.add)
    return [piece(0)] + [send(piece(k), peers(stride, k)) for k in range(1, n)]


def gather_level(x, d, stride, n):
    return [x] + [send(x, peers(stride, k)) for k in range(1, n)]


def in_order(pieces, d, stride, n):
    c = place(d, stride, n)
    lines = []
    for i in range(n):
        line = pieces[i]
        for k in range(n):
            if k != i:
                line = jnp.where((c ^ k) == i, pieces[k], line)
        lines.append(line)
    return jnp.concatenate(lines, axis=0)


def join_latest(p, q):
    nodes = lax.broadcasted_iota(I32, p.shape, 0) < p.shape[0] - 1
    return jnp.where(nodes, jnp.maximum(p, q), p + q)


def spread_latest(x, d, found):
    for level in found:
        x = tree(gather_level(x, d, *level), join_latest)
    return x


def spread_upper(x, d):
    for level in levels(lax.axis_size("dp"))[:0:-1]:
        x = jnp.concatenate(gather_level(x, d, *level), axis=0)
    return x


def tie(*xs):
    return lax.optimization_barrier(xs)


def body(source, target, neighbours, neighbour_ticks, event_ticks, event_types, labels, edge_feats, weights, memory,
         node_ticks, gru_in, gru_hid, keys_values, tall_stack, squares, vectors, *moments):
    events = event_ticks.shape[0]
    nodes = memory.shape[0]
    devices = lax.axis_size("dp") * lax.axis_size("rep")
    d, core = lax.axis_index("dp"), lax.axis_index("rep")
    scale = TIME_RATE / (events * devices)
    tiles = events // 128
    order = lambda x: jnp.transpose(x, (2, 1, 0)).reshape(NBR, 2, tiles, 128).transpose(0, 2, 1, 3).reshape(NBR, 2 * events)
    near_ids = order(neighbours).reshape(-1)
    near_ticks = order(neighbour_ticks)
    row = lambda x: x.reshape(1, events)
    lines = lambda x: x.reshape(tiles, 128)
    mem_t = memory.T
    spread = first_latest(nodes, lines(source), lines(target), lines(event_ticks), lines(weights))
    low, *upper = levels(lax.axis_size("dp"))
    spread = join_latest(spread, send(spread, twin()))
    spread = spread_latest(spread, d, [low])
    left, right, own = build_table(source, target, mem_t, node_ticks)
    spread, left = tie(spread, left)
    spread = spread_latest(spread, d, upper)
    latest = spread[:-1].reshape(-1).astype(I32)
    cap = room(nodes, devices)
    msg, keep, ren, gap_own, ren_left, ren_right = gru(
        scale, source, target, event_ticks, own, edge_feats.T, row(event_types), gru_in, gru_hid, vectors)
    packed = pack(cap, source, target, event_ticks, latest, ren_left, ren_right)
    height = packed.shape[1]
    first_round, left, right = tie(packed[0], left, right)
    rows = spread_upper(first_round, d)
    near = gather_near(near_ids, left, right)
    rows, near, vec_late = tie(rows, near, vectors)
    w = main_weights(gru_in, keys_values, tall_stack, squares, vec_late)
    held = gather_level(rows, d, *low)
    mine, theirs = main(scale, near, near_ticks, row(event_ticks), msg, keep, ren, gap_own, row(labels), row(weights),
                        spread[-1:], core.reshape(1), list(w))
    mine, theirs, *held = tie(mine, theirs, *held)
    got = send(theirs, twin())
    items = reduce_level([mine, got], d, *low)
    as_rows = lambda x: x.reshape(-1, height, 128)
    items[0], *held = tie(items[0], *held)
    laid = lay(cap, nodes, [as_rows(x) for x in held])
    joined = tie(*items, *laid)
    items, laid, joined = list(joined[: len(items)]), joined[len(items) : -1], joined[-1]
    swapped = send(joined, twin())
    for level in upper:
        items = reduce_level(items, d, *level)
    where = jnp.stack([core, place(d, *low)])
    *items, swapped, where, weight_sum = tie(*items, swapped, where, spread[-1, 0])
    piece = tree(items, jnp.add)
    for level in upper[::-1]:
        piece = in_order(gather_level(piece, d, *level), d, *level)
    piece, swapped = tie(piece, swapped)
    blocks = gather_level(piece, d, *low)
    new_mem, more = merge(cap, laid, swapped, mem_t)
    *blocks, new_mem = tie(*blocks, new_mem)
    other = [send(x, twin()) for x in blocks]
    grad_norm, loss_sum, news = adam(
        where, [(0, len(blocks))], blocks, other,
        (gru_in, gru_hid, keys_values, tall_stack, squares, vectors) + moments)

    def again(carry):
        r, _, mem_now = carry
        rows = spread_upper(lax.dynamic_index_in_dim(packed, r, 0, False), d)
        held = gather_level(rows, d, *low)
        *laid, joined = lay(cap, nodes, [as_rows(x) for x in held])
        mem_now, more = merge(cap, laid, send(joined, twin()), mem_now)
        return r + 1, more & (r + 1 < packed.shape[0]), mem_now

    if packed.shape[0] > 1:
        new_mem = lax.while_loop(lambda c: c[1], again, (jnp.int32(1), more, new_mem))[2]
    return (grad_norm, loss_sum, weight_sum, new_mem.T, *news)


def solution(mesh):
    split = P(AXES)
    placed = (split, split, P(AXES, None, None), P(AXES, None, None), split, split, split, P(AXES, None), split)
    return jax.shard_map(body, mesh=mesh, in_specs=placed + (P(),) * 20, out_specs=(P(),) * 22, check_vma=False)
```

```python
import math

import jax
import jax.numpy as jnp
from jax import lax
from jax.experimental import pallas as pl
from jax.experimental.pallas import tpu as pltpu
from jax.sharding import PartitionSpec as P

F32 = jnp.float32
BF = jnp.bfloat16
I32 = jnp.int32
NBR = 10
MEM = 172
PAD = 176
HALF = 86
HPAD = 88
STEP = 10
LEARN_RATE = 0.03
VECTOR_RATE = 0.3
BETA_ONE = 0.9
BETA_TWO = 0.999
ADAM_EPS = 1e-08
DECAY = 0.01
CLIP_AT = 0.005
TIME_RATE = 64.0
NORM_EPS = 1e-06
VMEM_CAP = 58 * 2**20


def params(limit=VMEM_CAP):
    return pltpu.CompilerParams(vmem_limit_bytes=limit)


def cost(us):
    return pl.CostEstimate(flops=int(us * 1e9), bytes_accessed=int(us * 3e6), transcendentals=0)


def nn(a, b):
    return lax.dot_general(a, b, (((1,), (0,)), ((), ())), preferred_element_type=F32)


def nt(a, b):
    return lax.dot_general(a, b, (((1,), (1,)), ((), ())), preferred_element_type=F32)


def zeros(rows, cols):
    return jnp.zeros((rows, cols), F32)


def rows_to(x, total):
    return jnp.concatenate([x, zeros(total - x.shape[0], x.shape[1])], axis=0)


def cols_to(x, total):
    return jnp.concatenate([x, zeros(x.shape[0], total - x.shape[1])], axis=1)


def split_rows(x):
    gap = zeros(HPAD - HALF, x.shape[1])
    return jnp.concatenate([x[:HALF], gap, x[HALF:], gap], axis=0)


def eye(n):
    return (lax.broadcasted_iota(I32, (n, n), 0) == lax.broadcasted_iota(I32, (n, n), 1)).astype(BF)


def turned(x):
    return nt(eye(x.shape[1]), x.astype(BF))


def wide_vectors(vec, vb):
    cols = jnp.transpose(cols_to(rows_to(vec[...], 128), 256))
    for i in range(15):
        column = cols[:, i : i + 1]
        if i in (8, 9):
            column = split_rows(column[:MEM])
        wide = jnp.broadcast_to(column[:PAD], (PAD, 128))
        vb[i] = wide * (0.5 / math.pi) if i < 2 else wide


def gate_weights(gin, ghid, vec, wg, wh, vb):
    full = gin[...]
    for gate in range(3):
        rows = full[gate * MEM : (gate + 1) * MEM]
        parts = [cols_to(rows[:, q * MEM : (q + 1) * MEM], PAD) for q in range(4)]
        wg[pl.ds(gate * PAD, PAD), :] = rows_to(jnp.concatenate(parts, axis=1), PAD).astype(BF)
    hid = ghid[...]
    for gate in range(3):
        part = cols_to(rows_to(hid[:, gate * MEM : (gate + 1) * MEM], PAD), 256)
        wh[pl.ds(gate * PAD, PAD), :] = turned(part)[:PAD].astype(BF)
    wide_vectors(vec, vb)


def main_weights_kernel(gin, kv, tall, sq, vec, wgc, kvm, kvct, kvc, t0t, t0, t1t, t1, t2t, t2, s0t, s0, s1t, s1, steady, vb):
    for gate in range(3):
        code = cols_to(rows_to(gin[gate * MEM : (gate + 1) * MEM, 2 * MEM : 3 * MEM], PAD), 256)
        wgc[:, gate * PAD : (gate + 1) * PAD] = turned(code)[:PAD].astype(BF)
    pairs = kv[...]
    both = turned(cols_to(pairs, 384))
    halves = jnp.concatenate([split_rows(both[:MEM]), split_rows(both[MEM : 2 * MEM])], axis=0)
    kvm[...] = cols_to(halves[:, :MEM], 256).astype(BF)
    code_rows = cols_to(halves[:, MEM:], 256)
    kvct[...] = code_rows[:, :PAD].astype(BF)
    kvc[...] = turned(code_rows)[:PAD].astype(BF)
    query = tall[0]
    query_t = cols_to(split_rows(query[:, :MEM]), 256)
    t0t[...] = query_t[:, :PAD].astype(BF)
    t0[...] = turned(query_t)[:PAD].astype(BF)
    for src, fwd, back in ((tall[1], t1t, t1), (tall[2], t2t, t2)):
        wide = rows_to(jnp.concatenate([cols_to(src[:, :MEM], PAD), cols_to(src[:, MEM:], PAD)], axis=1), PAD)
        fwd[...] = wide.astype(BF)
        back[...] = turned(cols_to(wide, 384))[: 2 * PAD].astype(BF)
    first = cols_to(split_rows(sq[:, 0, :]), 256)
    s0[...] = first[:, :PAD].astype(BF)
    s0t[...] = turned(first)[:PAD].astype(BF)
    second = cols_to(rows_to(sq[:, 1, :], PAD), 256)
    s1[...] = second[:, :PAD].astype(BF)
    s1t[...] = turned(second)[:PAD].astype(BF)
    phase_low = jnp.cos(jnp.transpose(cols_to(rows_to(vec[...], 128), 256))[:PAD, 1:2]).astype(BF).astype(F32)
    row_id = lax.broadcasted_iota(I32, (PAD, 128), 0)
    wide_phase = jnp.where(row_id < MEM, jnp.broadcast_to(phase_low, (PAD, 128)), 0.0).astype(BF)
    steady[...] = nn(cols_to(split_rows(query[:, MEM:]), PAD).astype(BF), wide_phase)
    wide_vectors(vec, vb)


def main_weights(gin, kv, tall, sq, vec):
    bf = lambda *s: jax.ShapeDtypeStruct(s, BF)
    outs = [bf(176, 528), bf(352, 256), bf(352, 176), bf(176, 352),
            bf(176, 176), bf(176, 176), bf(176, 352), bf(352, 176), bf(176, 352), bf(352, 176),
            bf(176, 176), bf(176, 176), bf(176, 176), bf(176, 176), jax.ShapeDtypeStruct((PAD, 128), F32),
            jax.ShapeDtypeStruct((15, PAD, 128), F32)]
    return pl.pallas_call(
        main_weights_kernel, out_shape=outs, compiler_params=params(), name="main_weights", cost_estimate=cost(5),
    )(gin.T, kv, jnp.transpose(tall, (0, 2, 1)), jnp.transpose(sq, (1, 0, 2)), vec)


def first_kernel(source, target, ticks, weights, out):
    tiles = source.shape[0]
    heights = out.shape[0] - 1
    nodes, orders = [], []
    for b in range(tiles):
        nodes += [source[b : b + 1, :], target[b : b + 1, :]]
        orders += [2 * ticks[b : b + 1, :], 2 * ticks[b : b + 1, :] + 1]
    count = 2 * tiles
    stack = jnp.concatenate([x.astype(F32) for x in nodes + orders], axis=0)
    cols = jnp.transpose(rows_to(stack, 128))
    lane = lax.broadcasted_iota(I32, (128, 128), 1)
    line = lax.broadcasted_iota(I32, (heights, 128), 0)
    total = zeros(heights, 384)
    for c in range(count):
        node = jnp.broadcast_to(cols[:, c : c + 1], (128, 128)).astype(I32)
        order = jnp.broadcast_to(cols[:, count + c : count + c + 1], (128, 128)).astype(I32)
        beaten = zeros(128, 128)
        for e in range(count):
            beaten = jnp.where((node == nodes[e]) & (orders[e] > order), 1.0, beaten)
        beaten = jnp.max(beaten, axis=1, keepdims=True)
        value = jnp.where(beaten > 0.0, 0, order + 1)
        here = (node & 127) == lane
        pick = lambda v: jnp.where(here, v, 0).astype(F32).astype(BF)
        right = jnp.concatenate([pick(value & 127), pick((value >> 7) & 127), pick(value >> 14)], axis=1)
        left = (jnp.broadcast_to(nodes[c] >> 7, (heights, 128)) == line).astype(BF)
        total = total + nn(left, right)
    out[0:heights, :] = total[:, :128] + 128.0 * total[:, 128:256] + 16384.0 * total[:, 256:] - 1.0
    out[heights : heights + 1, :] = jnp.broadcast_to(jnp.sum(weights[...], keepdims=True), (1, 128))


def first_latest(nodes, source, target, ticks, weights):
    return pl.pallas_call(
        first_kernel, out_shape=jax.ShapeDtypeStruct((nodes // 128 + 1, 128), F32),
        compiler_params=params(), name="latest", cost_estimate=cost(2),
    )(source, target, ticks, weights)


def copy_rows(out, at, tables, ids):
    for h, table in enumerate(tables):
        rows = jnp.concatenate([table[pl.ds(i, 1), :] for i in ids], axis=0)
        out[pl.ds(at, 16), 128 * h : 128 * h + 128] = rows.astype(BF)


def table_kernel(source, target, mem, ticks, far_left, far_right, own, wide, left, right, sems):
    step = pl.program_id(0)
    cols = mem.shape[1]
    steps = far_left.shape[0] // cols

    def copies(at):
        part = pl.ds(pl.multiple_of(at * cols, cols), cols)
        return [pltpu.make_async_copy(near.at[part], far.at[part], sems.at[h, at])
                for h, (near, far) in enumerate(((left, far_left), (right, far_right)))]

    @pl.when(step == 0)
    def _():
        wide[...] = jnp.zeros_like(wide)

    base = pl.multiple_of(step * cols, cols)
    wide[0:MEM, :] = mem[...].astype(BF).astype(F32)
    tick = ticks[...]
    for at, part in ((PAD, tick & 127), (PAD + 1, (tick >> 7) & 127), (PAD + 2, tick >> 14)):
        wide[at : at + 1, :] = part.astype(F32)
    unit = eye(256)
    for c in range(cols // 256):
        rows = nt(unit, wide[:, 256 * c : 256 * c + 256].astype(BF))
        left[pl.ds(base + 256 * c, 256), :] = rows[:, :128]
        right[pl.ds(base + 256 * c, 256), :] = rows[:, 128:]
    for copy in copies(step):
        copy.start()

    @pl.when(step == steps - 1)
    def _():
        def group(b, carry):
            for role, ids in enumerate((source, target)):
                def some(g, carry):
                    for v in range(2):
                        e = g * 32 + v * 16
                        at = pl.multiple_of(b * 256 + role * 128 + e, 16)
                        copy_rows(own, at, (left, right), [ids[b * 128 + e + u] for u in range(16)])
                    return carry

                lax.fori_loop(0, 4, some, 0)
            return carry

        lax.fori_loop(0, own.shape[0] // 256, group, 0)
        for at in range(steps):
            for copy in copies(at):
                copy.wait()


def build_table(source, target, mem_t, ticks):
    nodes = mem_t.shape[1]
    ends = 2 * source.shape[0]
    cols = 4096
    smem = pl.BlockSpec(memory_space=pltpu.SMEM)
    half = jax.ShapeDtypeStruct((nodes, 128), F32)
    fixed = lambda i: (0, 0)
    return pl.pallas_call(
        table_kernel,
        out_shape=[half, half, jax.ShapeDtypeStruct((ends, 256), BF)],
        grid=(nodes // cols,),
        in_specs=[smem, smem, pl.BlockSpec((MEM, cols), lambda i: (0, i)), pl.BlockSpec((1, cols), lambda i: (0, i))],
        out_specs=[pl.BlockSpec(memory_space=pl.ANY), pl.BlockSpec(memory_space=pl.ANY), pl.BlockSpec((ends, 256), fixed)],
        scratch_shapes=[pltpu.VMEM((256, cols), F32), pltpu.VMEM((nodes, 128), F32), pltpu.VMEM((nodes, 128), F32),
                        pltpu.SemaphoreType.DMA((2, nodes // cols))],
        compiler_params=params(), name="table", cost_estimate=cost(9),
    )(source, target, mem_t, ticks.reshape(1, nodes))


def near_kernel(chunk, ids, left, right, near):
    base = pl.program_id(0) * chunk

    def group(g, carry):
        for v in range(4):
            at = pl.multiple_of(g * 64 + v * 16, 16)
            copy_rows(near, at, (left, right), [ids[base + at + u] for u in range(16)])
        return carry

    lax.fori_loop(0, chunk // 64, group, 0)


def gather_near(ids, left, right):
    nears, chunk = ids.shape[0], ids.shape[0]
    whole = lambda a: pl.BlockSpec(a.shape, lambda i: (0, 0))
    return pl.pallas_call(
        lambda *r: near_kernel(chunk, *r),
        out_shape=jax.ShapeDtypeStruct((nears, 256), BF),
        grid=(nears // chunk,),
        in_specs=[pl.BlockSpec(memory_space=pltpu.SMEM), whole(left), whole(right)],
        out_specs=pl.BlockSpec((chunk, 256), lambda i: (i, 0)),
        compiler_params=params(), name="near", cost_estimate=cost(16),
    )(ids, left, right)


ROUND = 12582912.0
SIN = (6.283185005187988, -41.34165573120117, 81.60100555419922, -76.5497817993164, 39.536705017089844)
COS = (0.9999999403953552, -19.739171981811523, 64.9345932006836, -85.2403335571289, 56.24237823486328)


def cos_sin(turns):
    e = turns - ((turns + ROUND) - ROUND)
    w = 0.25 - jnp.abs(e)
    z = w * w
    c = w * (SIN[0] + z * (SIN[1] + z * (SIN[2] + z * (SIN[3] + z * SIN[4]))))
    s = COS[0] + z * (COS[1] + z * (COS[2] + z * (COS[3] + z * COS[4])))
    return c, jnp.where(e > 0.0, -s, s)


def sigmoid(x):
    return 0.5 * jnp.tanh(0.5 * x) + 0.5


BLOCK = 512
TILES = BLOCK // 256


def across(x):
    return jnp.concatenate([x] * (2 * TILES), axis=1)


def chunks(x, width=128):
    return [x[:, at : at + width] for at in range(0, x.shape[1], width)]


def both(x):
    return jnp.concatenate([c for c in chunks(x) for _ in range(2)], axis=1)


def mix(x, y):
    return jnp.concatenate([c for pair in zip(chunks(x), chunks(y)) for c in pair], axis=1)


def sources_of(x):
    return jnp.concatenate(chunks(x)[0::2], axis=1)


def targets_of(x):
    return jnp.concatenate(chunks(x)[1::2], axis=1)


def wide_rows(x, rows):
    return jnp.broadcast_to(x, (rows, x.shape[1]))


SECOND = 48


def round_height(cap):
    return cap + SECOND * (cap // 128) + cap % 128 // 2 + 8


def gru_kernel(scale, own, source, target, ticks, edge, types, gin, ghid, vec,
               msg, keep, ren, gap_out, left, right, wg, wh, vb):
    step = pl.program_id(0)

    @pl.when(step == 0)
    def _():
        gate_weights(gin, ghid, vec, wg, wh, vb)

    own_t = nt(eye(256), own[...])
    seen = own_t[PAD : PAD + 1] + 128.0 * own_t[PAD + 1 : PAD + 2] + 16384.0 * own_t[PAD + 2 : PAD + 3]
    gap = (both(ticks[...].astype(F32)) - seen) * scale
    row_id = lax.broadcasted_iota(I32, (PAD, BLOCK), 0)
    own_x = jnp.where(row_id < MEM, own_t[:PAD], 0.0)
    msg[0:PAD, :] = own_x.astype(BF)
    msg[PAD : 2 * PAD, :] = mix(targets_of(own_x), sources_of(own_x)).astype(BF)
    edges = rows_to(edge[...].astype(F32) * types[...].astype(F32), PAD)
    msg[3 * PAD : 4 * PAD, :] = both(edges).astype(BF)
    gap_out[...] = wide_rows(gap, 8)
    gap16 = wide_rows(gap, 16)
    for st in range(PAD // 16):
        at = 16 * st
        for m in range(TILES):
            q = slice(256 * m, 256 * m + 256)
            rate, phase = vb[0, at : at + 16, :], vb[1, at : at + 16, :]
            x = jnp.concatenate([rate, rate], axis=1) * gap16[:, q] + jnp.concatenate([phase, phase], axis=1)
            c, s = cos_sin(x)
            msg[2 * PAD + at : 2 * PAD + at + 16, q] = c.astype(BF)
            keep[4, at : at + 16, q] = s
    gates = nn(wg[...], msg[...])
    hidden = nn(wh[...], msg[0:PAD, :])
    for st in range(PAD // 8):
        at = 8 * st
        o = own_x[at : at + 8]
        pre = [gates[g * PAD + at : g * PAD + at + 8] + across(vb[2 + g, at : at + 8, :]) for g in range(3)]
        hid = [hidden[g * PAD + at : g * PAD + at + 8] + across(vb[5 + g, at : at + 8, :]) for g in range(3)]
        u = sigmoid(pre[0] + hid[0])
        r = sigmoid(pre[1] + hid[1])
        n = jnp.tanh(pre[2] + r * hid[2])
        keep[0, at : at + 8, :] = u
        keep[1, at : at + 8, :] = r
        keep[2, at : at + 8, :] = n
        keep[3, at : at + 8, :] = hid[2]
        ren[at : at + 8, :] = (1.0 - u) * n + u * o
    numbers = mix(source[...], target[...]).astype(F32)
    low = jnp.concatenate([ren[128:MEM, :], numbers, zeros(255 - MEM, BLOCK)], axis=0)
    for role in range(2 * TILES):
        left[128 * role : 128 * role + 128, :] = jnp.transpose(ren[0:128, 128 * role : 128 * role + 128])
        right[128 * role : 128 * role + 128, :] = jnp.transpose(low[:, 128 * role : 128 * role + 128])


def pack_rows(cap, rounds, nodes, sources, targets, ticks, latest, left, right, out, first, second):
    def chunk(b, count):
        def some(g, count):
            for v in range(16):
                e = b * 128 + g * 16 + v
                i = b * 256 + g * 16 + v
                order = 2 * ticks[e]
                for role, ids in enumerate((sources, targets)):
                    first[pl.ds(count, 1), :] = left[pl.ds(i + 128 * role, 1), :]
                    second[pl.ds(count, 1), :] = right[pl.ds(i + 128 * role, 1), :]
                    count = count + (latest[ids[e]] == order + role).astype(I32)
            return count

        return lax.fori_loop(0, 8, some, count)

    count = lax.fori_loop(0, sources.shape[0] // 128, chunk, jnp.int32(0))
    tiles = cap // 128
    rest = cap - 128 * tiles
    lane = lax.broadcasted_iota(I32, (1, 128), 1)
    for r in range(rounds):
        at = r * cap
        out[r, 0:cap, :] = first[at : at + cap, :]
        here = jnp.clip(count - at, 0, cap)
        lines = []
        for q in range(-(-cap // 128)):
            columns = jnp.transpose(second[at + 128 * q : at + 128 * q + 128, :])
            if q < tiles:
                out[r, cap + SECOND * q : cap + SECOND * q + SECOND, :] = columns[0:SECOND]
            lines.append(jnp.where(lane + 128 * q < here, columns[MEM - 128 : MEM - 127], float(nodes)))
        line, base = cap + SECOND * tiles, at + 128 * tiles
        if rest:
            out[r, line : line + rest // 2, :] = jnp.concatenate(
                [second[base : base + rest // 2, 0:64], second[base + rest // 2 : base + rest, 0:64]], axis=1)
        lines.append(jnp.full((1, 128), here, I32).astype(F32))
        lines += [zeros(1, 128)] * (8 - len(lines))
        out[r, line + rest // 2 :, :] = jnp.concatenate(lines, axis=0)


def pack(cap, sources, targets, ticks, latest, left, right):
    ends, nodes = left.shape[0], latest.shape[0]
    rounds = ends // cap + 1
    spare = rounds * cap + 128
    smem, vm = pl.BlockSpec(memory_space=pltpu.SMEM), pl.BlockSpec(memory_space=pltpu.VMEM)
    return pl.pallas_call(
        lambda *r: pack_rows(cap, rounds, nodes, *r),
        out_shape=jax.ShapeDtypeStruct((rounds, round_height(cap), 128), F32),
        in_specs=[smem] * 4 + [vm, vm], out_specs=vm,
        scratch_shapes=[pltpu.VMEM((spare, 128), F32), pltpu.VMEM((spare, 128), F32)],
        compiler_params=params(), name="pack", cost_estimate=cost(5),
    )(sources, targets, ticks, latest, left, right)


def gru(scale, sources, targets, ticks, own, edge_t, types, gin, ghid, vec):
    ends = own.shape[0]
    blocks = ends // BLOCK
    whole = lambda a: pl.BlockSpec(a.shape, lambda i: (0,) * len(a.shape))
    lanes = lambda: pl.BlockSpec((1, BLOCK // 2), lambda i: (0, i))
    row = lambda x: x.reshape(1, -1)
    gin = gin.T
    half = jax.ShapeDtypeStruct((ends, 128), F32)
    return pl.pallas_call(
        lambda *r: gru_kernel(scale, *r),
        out_shape=[jax.ShapeDtypeStruct((4 * PAD, ends), BF), jax.ShapeDtypeStruct((5, PAD, ends), F32),
                   jax.ShapeDtypeStruct((PAD, ends), F32), jax.ShapeDtypeStruct((8, ends), F32), half, half],
        grid=(blocks,),
        in_specs=[pl.BlockSpec((BLOCK, 256), lambda i: (i, 0)), lanes(), lanes(), lanes(),
                  pl.BlockSpec((MEM, BLOCK // 2), lambda i: (0, i)), lanes(), whole(gin), whole(ghid), whole(vec)],
        out_specs=[pl.BlockSpec((4 * PAD, BLOCK), lambda i: (0, i)), pl.BlockSpec((5, PAD, BLOCK), lambda i: (0, 0, i)),
                   pl.BlockSpec((PAD, BLOCK), lambda i: (0, i)), pl.BlockSpec((8, BLOCK), lambda i: (0, i)),
                   pl.BlockSpec((BLOCK, 128), lambda i: (i, 0)), pl.BlockSpec((BLOCK, 128), lambda i: (i, 0))],
        scratch_shapes=[pltpu.VMEM((528, 704), BF), pltpu.VMEM((528, 176), BF), pltpu.VMEM((15, PAD, 128), F32)],
        compiler_params=params(), name="gru", cost_estimate=cost(8),
    )(own, row(sources), row(targets), row(ticks), edge_t, types, gin, ghid, vec)


UNROLL = 10
ROWS = 2944
VECTORS = 2904
GELU_C = math.sqrt(2.0 / math.pi)


def gelu_parts(x):
    sq = x * x
    t = jnp.tanh(GELU_C * (x + 0.044715 * (sq * x)))
    half = 0.5 * (1.0 + t)
    slope = half + (0.5 * x) * (1.0 - t * t) * (GELU_C + (GELU_C * 3.0 * 0.044715) * sq)
    return x * half, slope


def fold(x):
    total, *others = chunks(x)
    for other in others:
        total = total + other
    return total


def main_kernel(scale, core, near, gaps_t, ticks, msg, keep, ren, gap_own, labels, weights, total,
                wgc, kvm, kvct, kvc, t0t, t0, t1t, t1, t2t, t2, s0t, s0, s1t, s1, steady, vb,
                mine, theirs,
                loss, pair, code, dcode, soft, back, mean, d_query_at, grads, g_in, g_kv, g_one, g_dec, g_qo, g_th, vacc):
    step = pl.program_id(0)
    inv_size = HALF ** -0.5

    @pl.when(step == 0)
    def _():
        for ref in (g_in, g_kv, g_one, g_dec, g_qo, g_th, vacc, loss):
            ref[...] = jnp.zeros_like(ref)

    tick2 = both(ticks[...].astype(F32))
    renewed = ren[...]
    ren_low = renewed.astype(BF)
    queries = nn(t0t[...], ren_low) + across(vb[8] + steady[...])
    def each(one):
        def some(g, carry):
            for v in range(UNROLL):
                one(g * UNROLL + v)
            return carry

        lax.fori_loop(0, NBR // UNROLL, some, 0)

    def look(j):
        gap16 = wide_rows((tick2 - gaps_t[pl.ds(j, 1), :].astype(F32)) * scale, 16)
        for st in range(PAD // 16):
            at = 16 * st
            for m in range(TILES):
                q = slice(256 * m, 256 * m + 256)
                rate, phase = vb[0, at : at + 16, :], vb[1, at : at + 16, :]
                x = jnp.concatenate([rate, rate], axis=1) * gap16[:, q] + jnp.concatenate([phase, phase], axis=1)
                c, s = cos_sin(x)
                code[j, at : at + 16, q] = c.astype(BF)
                dcode[j, at : at + 16, q] = s
        pair[j] = nt(kvm[...], near[j]) + nn(kvct[...], code[j])
        for h in range(2):
            acc = zeros(8, BLOCK)
            for st in range(HPAD // 8):
                at = HPAD * h + 8 * st
                acc = acc + pair[j, at : at + 8, :] * queries[at : at + 8]
            soft[2 * j + h] = wide_rows(jnp.sum(acc, axis=0, keepdims=True) * inv_size, 8)

    each(look)
    for h in range(2):
        top = soft[h]
        for j in range(1, NBR):
            top = jnp.maximum(top, soft[2 * j + h])
        norm = zeros(8, BLOCK)
        for j in range(NBR):
            e = jnp.exp(soft[2 * j + h] - top)
            soft[2 * j + h] = e
            norm = norm + e
        inv = 1.0 / norm
        for j in range(NBR):
            soft[2 * j + h] = soft[2 * j + h] * inv
    att = []
    for st in range(PAD // 8):
        at = 8 * st
        h = 0 if at < HPAD else 1
        acc = across(vb[9, at : at + 8, :])
        for j in range(NBR):
            acc = acc + soft[2 * j + h] * pair[j, PAD + at : PAD + at + 8, :]
        att.append(acc)
    att_low = jnp.concatenate(att, axis=0).astype(BF)
    projected = nn(s0t[...], att_low) + across(vb[10])
    mlp_in = jnp.concatenate([projected.astype(BF), ren_low], axis=0)
    inner = nn(t1t[...], mlp_in) + across(vb[11])
    act, act_slope = gelu_parts(inner)
    act_low = act.astype(BF)
    emb_low = (nn(s1t[...], act_low) + across(vb[12])).astype(BF)
    dec_in = jnp.concatenate([sources_of(emb_low), targets_of(emb_low)], axis=0)
    out_row = jnp.concatenate([vb[14]] * TILES, axis=1)
    dec_pre = nn(t2t[...], dec_in) + jnp.concatenate([vb[13]] * TILES, axis=1)
    dec_act, dec_slope = gelu_parts(dec_pre)
    logit = jnp.sum(dec_act * out_row, axis=0, keepdims=True)
    label = labels[...].astype(F32)
    tail = jnp.exp(-jnp.abs(logit))
    plus = jnp.maximum(logit, 0.0) + jnp.log1p(tail)
    loss[...] += fold(weights[...] * (plus - label * logit))
    d_logit = weights[...] / total[:, 0:1] * (sigmoid(logit) - label)
    d_out = d_logit * dec_act
    d_dec = (d_logit * out_row) * dec_slope
    d_dec_low = d_dec.astype(BF)
    g_dec[...] += nt(d_dec_low, dec_in)
    d_dec_in = nn(t2[...], d_dec_low)
    d_emb = mix(d_dec_in[:PAD], d_dec_in[PAD:])
    d_emb_low = d_emb.astype(BF)
    g_th[:, 0:256] += jnp.concatenate([nt(act_low, d_emb_low), zeros(PAD, 256 - PAD)], axis=1)
    d_inner = nn(s1[...], d_emb_low) * act_slope
    d_inner_low = d_inner.astype(BF)
    g_one[...] += nt(d_inner_low, mlp_in)
    d_mlp = nn(t1[...], d_inner_low)
    d_proj = d_mlp[:PAD]
    d_proj_low = d_proj.astype(BF)
    g_qo[:, 256:512] += jnp.concatenate([nt(att_low, d_proj_low), zeros(PAD, 256 - PAD)], axis=1)
    d_att = nn(s0[...], d_proj_low)
    d_query_at[...] = jnp.zeros_like(d_query_at)
    mean[...] = jnp.zeros_like(mean)

    def weigh(j):
        for h in range(2):
            acc = zeros(8, BLOCK)
            for st in range(HPAD // 8):
                at = HPAD * h + 8 * st
                acc = acc + pair[j, PAD + at : PAD + at + 8, :] * d_att[at : at + 8]
            wide = wide_rows(jnp.sum(acc, axis=0, keepdims=True), 8)
            back[2 * j + h] = wide
            mean[h] += wide * soft[2 * j + h]

    def learn(j):
        share = [soft[2 * j + h] for h in range(2)]
        slope = [(share[h] * inv_size) * (back[2 * j + h] - mean[h]) for h in range(2)]
        for st in range(PAD // 8):
            at = 8 * st
            d_query_at[at : at + 8, :] += slope[at >= HPAD] * pair[j, at : at + 8, :]
        for st in range(2 * PAD // 16):
            parts = []
            for half in range(2):
                at = 16 * st + 8 * half
                if at < PAD:
                    parts.append(slope[at >= HPAD] * queries[at : at + 8])
                else:
                    parts.append(share[at - PAD >= HPAD] * d_att[at - PAD : at - PAD + 8])
            grads[j, 16 * st : 16 * st + 16, :] = jnp.concatenate(parts, axis=0).astype(BF)
        d_code = nn(kvc[...], grads[j])
        gap8 = wide_rows((tick2 - gaps_t[pl.ds(j, 1), :].astype(F32)) * scale, 8)
        for st in range(PAD // 8):
            at = 8 * st
            d_arg = d_code[at : at + 8] * dcode[j, at : at + 8, :]
            vacc[0, at : at + 8, :] += fold(d_arg * gap8)
            vacc[1, at : at + 8, :] += fold(d_arg)
        g_kv[:, 0:256] += nn(grads[j], near[j])
        g_kv[:, 256 : 256 + PAD] += nt(grads[j], code[j])

    each(weigh)
    each(learn)
    d_query = d_query_at[...]
    d_q_low = d_query.astype(BF)
    g_qo[:, 0:256] += jnp.concatenate([nt(d_q_low, ren_low), zeros(PAD, 256 - PAD)], axis=1)
    d_ren = d_mlp[PAD:] + nn(t0[...], d_q_low)
    own_x = msg[0:PAD, :].astype(F32)
    u, r, n, hn = keep[0], keep[1], keep[2], keep[3]
    d_u = d_ren * (own_x - n) * (u * (1.0 - u))
    d_n = d_ren * (1.0 - u) * (1.0 - n * n)
    d_r = d_n * hn * (r * (1.0 - r))
    d_h = d_n * r
    gates = jnp.concatenate([d_u, d_r, d_n], axis=0).astype(BF)
    g_in[...] += nt(gates, msg[...])
    g_th[:, 256:512] += jnp.concatenate([nt(msg[0:PAD, :], d_h.astype(BF)), zeros(PAD, 256 - PAD)], axis=1)
    d_arg = nn(wgc[...], gates) * keep[4]
    vacc[0] += fold(d_arg * gap_own[0:1, :])
    vacc[1] += fold(d_arg)
    for i, item in ((2, d_u), (3, d_r), (4, d_n), (7, d_h), (8, d_query), (9, d_att), (10, d_proj), (11, d_inner),
                    (12, d_emb), (15, d_q_low.astype(F32))):
        vacc[i] += fold(item)
    vacc[13] += fold(d_dec)
    vacc[14] += fold(d_out)

    def finish(ga, gb):
        def panels(out, x):
            rows, lanes = x.shape
            whole = lanes // 128
            for c in range(whole):
                out[rows * c : rows * c + rows, :] = x[:, 128 * c : 128 * c + 128]
            last = x[:, 128 * whole :]
            out[rows * whole : rows * whole + rows // 2, :] = jnp.concatenate([last[: rows // 2], last[rows // 2 :]], axis=1)

        panels(gb, g_in[...])
        lane = lax.broadcasted_iota(I32, (PAD, 128), 1)
        vecs = zeros(PAD, 128)
        for i in range(16):
            column = jnp.sum(vacc[i], axis=1, keepdims=True)
            vecs = jnp.where(lane == i, column, vecs)
        flat = jnp.transpose(jnp.concatenate([vecs, zeros(256 - PAD, 128)], axis=0))
        gb[VECTORS : VECTORS + 16, :] = flat[0:16, 0:128]
        gb[VECTORS + 16 : VECTORS + 32, :] = flat[0:16, 128:256]
        gb[VECTORS + 32 :, :] = zeros(ROWS - VECTORS - 32, 128)
        units = [g_kv[at : at + PAD, c : c + PAD] for at in (0, PAD) for c in (0, 256)]
        units += [g_one[...], g_dec[...]]
        units += [ref[:, c : c + PAD] for ref in (g_qo, g_th) for c in (0, 256)]
        panels(ga, jnp.concatenate(units, axis=1))
        ga[VECTORS:, :] = rows_to(loss[...], ROWS - VECTORS)

    @pl.when((step == pl.num_programs(0) - 1) & (core[0] == 0))
    def _():
        finish(mine, theirs)

    @pl.when((step == pl.num_programs(0) - 1) & (core[0] != 0))
    def _():
        finish(theirs, mine)


def main(scale, near, near_ticks, ticks, msg, keep, ren, gap_own, labels, weights, total, core, w):
    ends = ren.shape[1]
    blocks = ends // BLOCK
    whole = lambda a: pl.BlockSpec(a.shape, lambda i: (0,) * len(a.shape))
    lanes = lambda: pl.BlockSpec((1, BLOCK // 2), lambda i: (0, i))
    return pl.pallas_call(
        lambda *r: main_kernel(scale, *r),
        out_shape=[jax.ShapeDtypeStruct((ROWS, 128), F32), jax.ShapeDtypeStruct((ROWS, 128), F32)],
        grid=(blocks,),
        in_specs=[pl.BlockSpec(memory_space=pltpu.SMEM), pl.BlockSpec((NBR, BLOCK, 256), lambda i: (0, i, 0)), pl.BlockSpec((NBR, BLOCK), lambda i: (0, i)), lanes(),
                  pl.BlockSpec((4 * PAD, BLOCK), lambda i: (0, i)), pl.BlockSpec((5, PAD, BLOCK), lambda i: (0, 0, i)),
                  pl.BlockSpec((PAD, BLOCK), lambda i: (0, i)), pl.BlockSpec((8, BLOCK), lambda i: (0, i)), lanes(), lanes(),
                  pl.BlockSpec((1, 128), lambda i: (0, 0))] + [whole(a) for a in w],
        out_specs=[pl.BlockSpec((ROWS, 128), lambda i: (0, 0)), pl.BlockSpec((ROWS, 128), lambda i: (0, 0))],
        scratch_shapes=[pltpu.VMEM((1, 128), F32), pltpu.VMEM((NBR, 352, BLOCK), F32), pltpu.VMEM((NBR, PAD, BLOCK), BF), pltpu.VMEM((NBR, PAD, BLOCK), F32),
                        pltpu.VMEM((20, 8, BLOCK), F32), pltpu.VMEM((20, 8, BLOCK), F32), pltpu.VMEM((2, 8, BLOCK), F32),
                        pltpu.VMEM((PAD, BLOCK), F32), pltpu.VMEM((NBR, 352, BLOCK), BF),
                        pltpu.VMEM((528, 704), F32), pltpu.VMEM((352, 512), F32), pltpu.VMEM((PAD, 352), F32),
                        pltpu.VMEM((PAD, 352), F32), pltpu.VMEM((PAD, 512), F32), pltpu.VMEM((PAD, 512), F32),
                        pltpu.VMEM((16, PAD, 128), F32)],
        compiler_params=params(), name="main", cost_estimate=cost(35),
    )(core, near.reshape(NBR, ends, 256), near_ticks, ticks, msg, keep, ren, gap_own, labels, weights, total, *w)


def room(nodes, devices):
    return -(-(nodes * 9) // (devices * 8 * 16)) * 16


def turned_exactly(x):
    high = x.astype(BF)
    rest = x - high.astype(F32)
    middle = rest.astype(BF)
    low = (rest - middle.astype(F32)).astype(BF)
    unit = eye(x.shape[1])
    return (nt(unit, high) + nt(unit, middle)) + nt(unit, low)


def fetch_numbers(cap, rows, whole, numbers, sem):
    whole[...] = rows[:, round_height(cap) - 8 :, :].astype(I32)
    copy = pltpu.make_async_copy(whole, numbers, sem)
    copy.start()
    return copy


def lay_rows(cap, rows, numbers, left, right, second):
    tiles = cap // 128
    line, tail = cap + SECOND * tiles, cap % 128 // 2

    def block(q, most):
        for t in range(tiles):
            columns = rows[q, cap + SECOND * t : cap + SECOND * t + SECOND, :]
            second[128 * t : 128 * t + 128, :] = jnp.transpose(rows_to(columns, 128))
        if tail:
            half = rows[q, line : line + tail, :]
            second[128 * tiles : 128 * tiles + tail, :] = half
            second[128 * tiles + tail : cap, :] = jnp.concatenate([half[:, 64:], half[:, :64]], axis=1)
        here = numbers[q, -(-cap // 128), 0]

        def some(g, carry):
            few = numbers.at[q, lax.shift_right_logical(g, 3), pl.ds((g & 7) * 16, 16)]
            for v in range(16):
                i = g * 16 + v
                node = few[v]
                left[pl.ds(node, 1), :] = rows[q, pl.ds(i, 1), :]
                right[pl.ds(node, 1), :] = second[pl.ds(i, 1), :]
            return carry

        lax.fori_loop(0, lax.div(here + 15, 16), some, 0)
        return jnp.maximum(most, here)

    return lax.fori_loop(0, rows.shape[0], block, jnp.int32(0))


def lay_kernel(cap, count, *refs):
    arrays, (left, right, most, joined, second, sems), rest = refs[:count], refs[count : count + 6], refs[count + 6 :]
    wholes, lists = rest[:count], rest[count:]
    copies = [fetch_numbers(cap, arrays[a], wholes[a], lists[a], sems.at[a]) for a in range(count)]
    right[...] = jnp.full_like(right, -1.0)
    for a, rows in enumerate(arrays):
        blocks = rows.shape[0]
        joined[a * blocks : (a + 1) * blocks] = rows[...]
    largest = jnp.int32(0)
    for a, rows in enumerate(arrays):
        copies[a].wait()
        largest = jnp.maximum(largest, lay_rows(cap, rows, lists[a], left, right, second))
    most[0] = largest


def lay(cap, nodes, arrays):
    vm, smem = pl.BlockSpec(memory_space=pltpu.VMEM), pl.BlockSpec(memory_space=pltpu.SMEM)
    table = jax.ShapeDtypeStruct((nodes + 8, 128), F32)
    count = len(arrays)
    blocks, height, _ = arrays[0].shape
    return pl.pallas_call(
        lambda *r: lay_kernel(cap, count, *r),
        out_shape=[table, table, jax.ShapeDtypeStruct((1,), I32), jax.ShapeDtypeStruct((count * blocks, height, 128), F32)],
        in_specs=[vm] * count, out_specs=[vm, vm, smem, vm],
        scratch_shapes=[pltpu.VMEM((cap, 128), F32), pltpu.SemaphoreType.DMA((count,))]
        + [kind((blocks, 8, 128), I32) for kind in (pltpu.VMEM, pltpu.SMEM) for _ in arrays],
        compiler_params=params(), name="lay", cost_estimate=cost(14),
    )(*arrays)


def merge_kernel(cap, far_rows, far_left, far_right, before, mem, out, full, left, right, second, sems, rows, whole, numbers):
    step = pl.program_id(0)

    @pl.when(step == 0)
    def _():
        copies = [pltpu.make_async_copy(far, near, sems.at[i])
                  for i, (far, near) in enumerate(((far_rows, rows), (far_left, left), (far_right, right)))]
        for copy in copies:
            copy.start()
        copies[0].wait()
        copies.append(fetch_numbers(cap, rows, whole, numbers, sems.at[3]))
        for copy in copies[1:]:
            copy.wait()
        most = lay_rows(cap, rows, numbers, left, right, second)
        full[0] = (jnp.maximum(most, before[0]) == cap).astype(I32)

    cols = mem.shape[1]
    base = pl.multiple_of(step * cols, cols)
    for c in range(cols // 256):
        at = base + 256 * c
        s = slice(256 * c, 256 * c + 256)
        top = turned_exactly(left[pl.ds(at, 256), :])
        low = turned_exactly(right[pl.ds(at, 256), :][:, :64])
        fresh = low[MEM - 128 : MEM - 127] >= 0.0
        out[0:128, s] = jnp.where(fresh, top, mem[0:128, s])
        out[128:MEM, s] = jnp.where(fresh, low[: MEM - 128], mem[128:MEM, s])


def merge(cap, laid, rows, mem_t):
    nodes = mem_t.shape[1]
    cols = 2048
    part = pl.BlockSpec((MEM, cols), lambda i: (0, i))
    smem, far = pl.BlockSpec(memory_space=pltpu.SMEM), pl.BlockSpec(memory_space=pl.ANY)
    new, full = pl.pallas_call(
        lambda *r: merge_kernel(cap, *r),
        out_shape=[jax.ShapeDtypeStruct((MEM, nodes), F32), jax.ShapeDtypeStruct((1,), I32)],
        grid=(nodes // cols,),
        in_specs=[far, far, far, smem, part],
        out_specs=[part, smem],
        scratch_shapes=[pltpu.VMEM((nodes + 8, 128), F32), pltpu.VMEM((nodes + 8, 128), F32), pltpu.VMEM((cap, 128), F32),
                        pltpu.SemaphoreType.DMA((4,)), pltpu.VMEM(rows.shape, F32)]
        + [kind((rows.shape[0], 8, 128), I32) for kind in (pltpu.VMEM, pltpu.SMEM)],
        compiler_params=params(), name="merge", cost_estimate=cost(18),
    )(rows, *laid, mem_t)
    return new, full[0] > 0


def move(param, one, two, grad, factor, rate, decay):
    clipped = grad * factor
    one = BETA_ONE * one + (1.0 - BETA_ONE) * clipped
    two = BETA_TWO * two + (1.0 - BETA_TWO) * clipped * clipped
    step = (one * (1.0 / (1.0 - BETA_ONE**STEP))) / (jnp.sqrt(two * (1.0 / (1.0 - BETA_TWO**STEP))) + ADAM_EPS)
    return param - rate * (step + decay * param), one, two


def unsplit(x, axis):
    take = lambda a, b: lax.slice_in_dim(x, a, b, axis=axis)
    return jnp.concatenate([take(0, HALF), take(HPAD, HPAD + HALF)], axis=axis)


def adam_kernel(parts, where, *refs):
    count = sum(n for _, n in parts)
    mine, other = refs[:count], refs[count : 2 * count]
    refs = refs[2 * count :]
    far, out, (norm_out, loss_out) = refs[:18], refs[18:36], refs[36:38]
    a, b, g_gin, g_hid, g_kv, g_tall, g_sq, g_vec = refs[38:46]
    state, sems_in, sems_out = refs[46:64], refs[64], refs[65]
    fetches = [pltpu.make_async_copy(far[i], state[i], sems_in.at[i]) for i in range(18)]
    stores = [pltpu.make_async_copy(state[i], out[i], sems_out.at[i]) for i in range(18)]
    for i in (5, 3, 0, 6, 12, 1, 7, 13, 2, 8, 14, 9, 15, 4, 10, 16, 11, 17):
        fetches[i].start()
    core = where[0]
    at_block = 0
    for p, (first, n) in enumerate(parts):
        height = mine[at_block].shape[0]
        for k in range(n):
            at = pl.multiple_of(first + (where[1 + p] ^ k) * height, 8)
            one, two = mine[at_block], other[at_block]
            at_block += 1

            @pl.when(core == 0)
            def _():
                a[pl.ds(at, height), :] = one[...]
                b[pl.ds(at, height), :] = two[...]

            @pl.when(core != 0)
            def _():
                b[pl.ds(at, height), :] = one[...]
                a[pl.ds(at, height), :] = two[...]

    def panels(ref, rows, lanes):
        whole = lanes // 128
        parts = [ref[c * rows : (c + 1) * rows, :] for c in range(whole)]
        last = ref[whole * rows : whole * rows + rows // 2, :]
        return jnp.concatenate(parts + [jnp.concatenate([last[:, :64], last[:, 64:]], axis=0)], axis=1)

    vec, tall = state[5], state[3]
    wide = panels(b, 528, 704)
    gates = []
    for g in range(3):
        rows = wide[PAD * g : PAD * g + MEM]
        gates.append(jnp.concatenate([rows[:, PAD * q : PAD * q + MEM] for q in range(4)], axis=1))
    g_gin[...] = jnp.concatenate(gates, axis=0)
    vecs = jnp.concatenate([b[VECTORS : VECTORS + 16, :], b[VECTORS + 16 : VECTORS + 32, :]], axis=1)
    units = panels(a, PAD, 12 * PAD)
    unit = lambda i: units[:, PAD * i : PAD * i + MEM]
    kv = jnp.concatenate([jnp.concatenate([unsplit(unit(2 * i), 0), unsplit(unit(2 * i + 1), 0)], axis=1) for i in range(2)], axis=0)
    g_kv[...] = jnp.transpose(rows_to(cols_to(kv, 384), 384))[: 2 * MEM, : 2 * MEM]
    for i in (1, 2):
        g_tall[i] = jnp.concatenate([unit(2 + 2 * i)[:MEM], unit(3 + 2 * i)[:MEM]], axis=1)
    sum_dq = unsplit(jnp.transpose(rows_to(vecs, 128))[:PAD, 15:16], 0)
    fetches[5].wait()
    fetches[3].wait()
    phase = vec[1:2, :]
    phase_low = jnp.cos(phase).astype(BF).astype(F32)
    g_tall[0] = jnp.concatenate([unsplit(unit(8), 0), sum_dq * phase_low], axis=1)
    g_sq[0] = unsplit(unit(9), 0)
    g_sq[1] = unit(10)[:MEM]
    shared = jnp.transpose(rows_to(cols_to(g_gin[0 : 2 * MEM, 0:MEM], 256), 384))[:MEM, : 2 * MEM]
    g_hid[...] = jnp.concatenate([shared, unit(11)[:MEM]], axis=1)
    query_low = tall[0][:, MEM:].astype(BF).astype(F32)
    phase_in = jnp.sum(query_low * sum_dq, axis=0, keepdims=True)
    row = lambda i: vecs[i : i + 1, :MEM]
    g_vec[...] = jnp.concatenate(
        [row(0), row(1) - jnp.sin(phase) * phase_in, row(2), row(3), row(4), row(2), row(3), row(7),
         unsplit(vecs[8:9], 1), unsplit(vecs[9:10], 1)] + [row(i) for i in range(10, 15)], axis=0)
    total = jnp.zeros((1, 1), F32)
    for ref in (g_gin, g_hid, g_kv, g_vec):
        total += jnp.sum(ref[...] * ref[...], keepdims=True)
    for ref in (g_tall, g_sq):
        for i in range(ref.shape[0]):
            total += jnp.sum(ref[i] * ref[i], keepdims=True)
    norm = jnp.sqrt(total)
    factor = jnp.minimum(1.0, CLIP_AT / (norm + NORM_EPS))
    norm_out[...] = norm
    loss_out[...] = jnp.sum(a[VECTORS : VECTORS + 1, :], keepdims=True)
    for i, grad in enumerate((g_gin, g_hid, g_kv, g_tall, g_sq, g_vec)):
        rate, decay = (VECTOR_RATE, 0.0) if i == 5 else (LEARN_RATE, DECAY)
        new = param, one, two = state[i], state[6 + i], state[12 + i]
        for at in (i, 6 + i, 12 + i):
            if at not in (3, 5):
                fetches[at].wait()
        if i == 4:
            for j in range(2):
                made = move(param[:, j, :], one[:, j, :], two[:, j, :], grad[j], factor, rate, decay)
                for ref, value in zip(new, made):
                    ref[:, j, :] = value
        elif len(param.shape) == 3:
            for j in range(param.shape[0]):
                made = move(param[j], one[j], two[j], grad[j], factor, rate, decay)
                for ref, value in zip(new, made):
                    ref[j] = value
        else:
            rows = param.shape[0]
            for at in range(0, rows, 16):
                s = slice(at, min(at + 16, rows))
                made = move(param[s], one[s], two[s], grad[s], factor, rate, decay)
                for ref, value in zip(new, made):
                    ref[s] = value
        for at in (i, 6 + i, 12 + i):
            stores[at].start()
    for store in stores:
        store.wait()


def adam(where, parts, mine, other, state):
    swap = lambda x: jnp.transpose(x, (0, 2, 1))
    def ready(group):
        gin, hid, kv, tall, sq, vec = group
        return [gin.T, hid, kv, swap(tall), jnp.transpose(sq, (1, 0, 2)), vec]
    state = ready(state[0:6]) + ready(state[6:12]) + ready(state[12:18])
    count = len(mine)
    shapes = [x.shape for x in state[:6]]
    shapes[4] = (2, MEM, MEM)
    vm, far = pl.BlockSpec(memory_space=pltpu.VMEM), pl.BlockSpec(memory_space=pl.ANY)
    outs = [jax.ShapeDtypeStruct(x.shape, F32) for x in state] + [jax.ShapeDtypeStruct((1, 1), F32)] * 2
    out = pl.pallas_call(
        lambda *r: adam_kernel(parts, *r),
        out_shape=outs,
        in_specs=[pl.BlockSpec(memory_space=pltpu.SMEM)] + [vm] * (2 * count) + [far] * 18,
        out_specs=[far] * 18 + [vm] * 2,
        scratch_shapes=[pltpu.VMEM((ROWS, 128), F32)] * 2 + [pltpu.VMEM(s, F32) for s in shapes]
        + [pltpu.VMEM(x.shape, F32) for x in state] + [pltpu.SemaphoreType.DMA((18,))] * 2,
        compiler_params=params(), name="adam", cost_estimate=cost(14),
    )(where, *mine, *other, *state)
    back = lambda group: [group[0].T, group[1], group[2], swap(group[3]), jnp.transpose(group[4], (1, 0, 2)), group[5]]
    return out[18].reshape(()), out[19].reshape(()), back(out[0:6]) + back(out[6:12]) + back(out[12:18])


AXES = ("dp", "rep")


def levels(size):
    found, stride = [], 1
    while size > 1:
        n = size if size <= 8 else 4
        found.append((stride, n))
        stride, size = stride * n, size // n
    return found


def peers(stride, k):
    dp, rep = lax.axis_size("dp"), lax.axis_size("rep")
    return [(d * rep + r, (d ^ (k * stride)) * rep + r) for d in range(dp) for r in range(rep)]


def twin():
    dp, rep = lax.axis_size("dp"), lax.axis_size("rep")
    return [(d * rep + r, d * rep + (rep - 1 - r)) for d in range(dp) for r in range(rep)]


def send(x, pairs):
    return lax.ppermute(x, AXES, pairs)


def tree(items, join):
    while len(items) > 1:
        items = [join(items[i], items[i + 1]) for i in range(0, len(items), 2)]
    return items[0]


def place(d, stride, n):
    return lax.rem(lax.div(d, stride), n)


def reduce_level(items, d, stride, n):
    c = place(d, stride, n)
    rows = items[0].shape[0] // n
    piece = lambda k: tree([lax.dynamic_slice_in_dim(x, (c ^ k) * rows, rows, 0) for x in items], jnp.add)
    return [piece(0)] + [send(piece(k), peers(stride, k)) for k in range(1, n)]


def gather_level(x, d, stride, n):
    return [x] + [send(x, peers(stride, k)) for k in range(1, n)]


def in_order(pieces, d, stride, n):
    c = place(d, stride, n)
    lines = []
    for i in range(n):
        line = pieces[i]
        for k in range(n):
            if k != i:
                line = jnp.where((c ^ k) == i, pieces[k], line)
        lines.append(line)
    return jnp.concatenate(lines, axis=0)


def join_latest(p, q):
    nodes = lax.broadcasted_iota(I32, p.shape, 0) < p.shape[0] - 1
    return jnp.where(nodes, jnp.maximum(p, q), p + q)


def spread_latest(x, d, found):
    for level in found:
        x = tree(gather_level(x, d, *level), join_latest)
    return x


def spread_upper(x, d):
    for level in levels(lax.axis_size("dp"))[:0:-1]:
        x = jnp.concatenate(gather_level(x, d, *level), axis=0)
    return x


def tie(*xs):
    return lax.optimization_barrier(xs)


def body(source, target, neighbours, neighbour_ticks, event_ticks, event_types, labels, edge_feats, weights, memory,
         node_ticks, gru_in, gru_hid, keys_values, tall_stack, squares, vectors, *moments):
    events = event_ticks.shape[0]
    nodes = memory.shape[0]
    devices = lax.axis_size("dp") * lax.axis_size("rep")
    d, core = lax.axis_index("dp"), lax.axis_index("rep")
    scale = TIME_RATE / (events * devices)
    tiles = events // 128
    order = lambda x: jnp.transpose(x, (2, 1, 0)).reshape(NBR, 2, tiles, 128).transpose(0, 2, 1, 3).reshape(NBR, 2 * events)
    near_ids = order(neighbours).reshape(-1)
    near_ticks = order(neighbour_ticks)
    row = lambda x: x.reshape(1, events)
    lines = lambda x: x.reshape(tiles, 128)
    mem_t = memory.T
    spread = first_latest(nodes, lines(source), lines(target), lines(event_ticks), lines(weights))
    low, *upper = levels(lax.axis_size("dp"))
    spread = join_latest(spread, send(spread, twin()))
    spread = spread_latest(spread, d, [low])
    left, right, own = build_table(source, target, mem_t, node_ticks)
    spread, left = tie(spread, left)
    spread = spread_latest(spread, d, upper)
    latest = spread[:-1].reshape(-1).astype(I32)
    cap = room(nodes, devices)
    msg, keep, ren, gap_own, ren_left, ren_right = gru(
        scale, source, target, event_ticks, own, edge_feats.T, row(event_types), gru_in, gru_hid, vectors)
    packed = pack(cap, source, target, event_ticks, latest, ren_left, ren_right)
    height = packed.shape[1]
    first_round, left, right = tie(packed[0], left, right)
    rows = spread_upper(first_round, d)
    near = gather_near(near_ids, left, right)
    rows, near, vec_late = tie(rows, near, vectors)
    w = main_weights(gru_in, keys_values, tall_stack, squares, vec_late)
    held = gather_level(rows, d, *low)
    mine, theirs = main(scale, near, near_ticks, row(event_ticks), msg, keep, ren, gap_own, row(labels), row(weights),
                        spread[-1:], core.reshape(1), list(w))
    mine, theirs, *held = tie(mine, theirs, *held)
    got = send(theirs, twin())
    items = reduce_level([mine, got], d, *low)
    as_rows = lambda x: x.reshape(-1, height, 128)
    items[0], *held = tie(items[0], *held)
    laid = lay(cap, nodes, [as_rows(x) for x in held])
    joined = tie(*items, *laid)
    items, laid, joined = list(joined[: len(items)]), joined[len(items) : -1], joined[-1]
    swapped = send(joined, twin())
    for level in upper:
        items = reduce_level(items, d, *level)
    where = jnp.stack([core, place(d, *low)])
    *items, swapped, where, weight_sum = tie(*items, swapped, where, spread[-1, 0])
    piece = tree(items, jnp.add)
    for level in upper[::-1]:
        piece = in_order(gather_level(piece, d, *level), d, *level)
    piece, swapped = tie(piece, swapped)
    blocks = gather_level(piece, d, *low)
    new_mem, more = merge(cap, laid, swapped, mem_t)
    *blocks, new_mem = tie(*blocks, new_mem)
    other = [send(x, twin()) for x in blocks]
    grad_norm, loss_sum, news = adam(
        where, [(0, len(blocks))], blocks, other,
        (gru_in, gru_hid, keys_values, tall_stack, squares, vectors) + moments)

    def again(carry):
        r, _, mem_now = carry
        rows = spread_upper(lax.dynamic_index_in_dim(packed, r, 0, False), d)
        held = gather_level(rows, d, *low)
        *laid, joined = lay(cap, nodes, [as_rows(x) for x in held])
        mem_now, more = merge(cap, laid, send(joined, twin()), mem_now)
        return r + 1, more & (r + 1 < packed.shape[0]), mem_now

    if packed.shape[0] > 1:
        new_mem = lax.while_loop(lambda c: c[1], again, (jnp.int32(1), more, new_mem))[2]
    return (grad_norm, loss_sum, weight_sum, new_mem.T, *news)


def solution(mesh):
    split = P(AXES)
    placed = (split, split, P(AXES, None, None), P(AXES, None, None), split, split, split, P(AXES, None), split)
    return jax.shard_map(body, mesh=mesh, in_specs=placed + (P(),) * 20, out_specs=(P(),) * 22, check_vma=False)
```
